32 devices in a mesh: dp: 8 (over y, x, core), seq: 4 (over z).
Axes of the slice: x: 2, y: 2, z: 4, core: 2. Of those that a mesh axis runs over, the one named last changes fastest.
Arguments:
- tokens: bfloat16 [16, 1024, 1280], P('dp', 'seq'), may hold values from -6 to 6
- first_gain: bfloat16 [1280], P(('dp', 'seq')), may hold values from 0.25 to 1.75
- first_bias: bfloat16 [1280], P(('dp', 'seq')), may hold values from -3 to 3
- in_weight: bfloat16 [1280, 640], P(('dp', 'seq')), may hold values from -0.15625 to 0.15625
- in_bias: bfloat16 [640], P(('dp', 'seq')), may hold values from -2 to 2
- second_gain: bfloat16 [640], P(('dp', 'seq')), may hold values from 0.25 to 1.75
- second_bias: bfloat16 [640], P(('dp', 'seq')), may hold values from -3 to 3
- conv_weight: bfloat16 [640, 5, 640], P(('dp', 'seq')), may hold values from -0.109375 to 0.109375
- conv_bias: bfloat16 [640], P(('dp', 'seq')), may hold values from -2 to 2
- third_gain: bfloat16 [640], P(('dp', 'seq')), may hold values from 0.25 to 1.75
- third_bias: bfloat16 [640], P(('dp', 'seq')), may hold values from -3 to 3
- out_weight: bfloat16 [640, 1280], P(('dp', 'seq')), may hold values from -0.3125 to 0.3125
- out_bias: bfloat16 [1280], P(('dp', 'seq')), may hold values from -2 to 2
- head_weight: bfloat16 [1280, 30], P(('dp', 'seq')), may hold values from -0.25 to 0.25
- head_bias: bfloat16 [30], replicated, may hold values from -3 to 3
- residue_types: int32 [16, 1024], P('dp', 'seq'), may hold values from 0 to 29
- mask_positions: int32 [16, 153], P('dp'), may hold values from 0 to 1023, as said below
- targets: int32 [16, 153], P('dp'), may hold values from 0 to 29
Outputs:
- block_out: bfloat16 [16, 1024, 1280], P('dp', 'seq')
- input_grad: bfloat16 [16, 1024, 1280], P('dp', 'seq')
- first_gain_grad: float32 [1280], P(('dp', 'seq'))
- first_bias_grad: float32 [1280], P(('dp', 'seq'))
- in_weight_grad: float32 [1280, 640], P(('dp', 'seq'))
- in_bias_grad: float32 [640], P(('dp', 'seq'))
- second_gain_grad: float32 [640], P(('dp', 'seq'))
- second_bias_grad: float32 [640], P(('dp', 'seq'))
- conv_weight_grad: float32 [640, 5, 640], P(('dp', 'seq'))
- conv_bias_grad: float32 [640], P(('dp', 'seq'))
- third_gain_grad: float32 [640], P(('dp', 'seq'))
- third_bias_grad: float32 [640], P(('dp', 'seq'))
- out_weight_grad: float32 [640, 1280], P(('dp', 'seq'))
- out_bias_grad: float32 [1280], P(('dp', 'seq'))
- head_weight_grad: float32 [1280, 30], P(('dp', 'seq'))
- head_bias_grad: float32 [30], replicated
- type_counts: int32 [30], replicated
- type_hits: float32 [30], replicated
- mean_loss: float32 [], replicated
The draws below stay inside these ranges and needn't reach their ends.
Inputs may be any that keep to these rules, and one draw needn't show every extreme that they name: `mask_positions`: each row holds 153 different positions of its sequence.
All inputs are finite; a program needn't handle non-finite values.
Results may differ from the reference program's by a relative error of at most 0.0075.
Values may be sent and summed in bfloat16 or wider, within the bound.
No kernel may reach another device: no remote copies, remote signals or barrier semaphores. Data moves between devices by JAX's collectives and lax.ppermute only.
A program may use at most 128 MiB of HBM per device.

```python
import math
import jax
import jax.numpy as jnp
from jax import lax

D = 1280
INNER = 640
V = 30
KERNEL_TAPS = 5
DILATION_RATE = 128
SEQUENCE_LENGTH = 1024
MASKED = 153
SEQS = 16


def draw_mask_positions(key, part):
    row_keys = jax.random.split(key, SEQS)

    def shuffled(row_key):
        return jax.random.permutation(row_key, SEQUENCE_LENGTH)[:MASKED]
    return jax.vmap(shuffled)(row_keys).astype(jnp.int32)


def place_ends(values, stream_key, least, largest):
    index_at = [jax.random.randint(jax.random.fold_in(stream_key, axis), (), 0, length) for axis, length in enumerate(values.shape)]
    longest = values.shape.index(max(values.shape))
    next_to = index_at[:longest] + [(index_at[longest] + 1) % values.shape[longest]] + index_at[longest + 1:]
    return values.at[tuple(index_at)].set(least).at[tuple(next_to)].set(largest)


def shard_levels(stream_key, dims, pieces, low, high):
    gain = 1.0
    for position, parts in pieces:
        draws = jax.random.uniform(jax.random.fold_in(jax.random.fold_in(stream_key, 6), position), (parts,), jnp.float32, low / len(pieces), high / len(pieces))
        gain = gain * jnp.repeat(jnp.exp(draws), dims[position] // parts).reshape((-1,) + (1,) * (len(dims) - 1 - position))
    return gain


def bell_draw(own_key, extent, width, most, pieces=(), kind=jnp.bfloat16):
    gain = shard_levels(own_key, extent, pieces, -0.22, 0.18) if pieces else 1.0
    drawn = jax.random.normal(own_key, extent, jnp.float32) * width * gain
    return jnp.minimum(jnp.maximum(drawn, -most), most).astype(kind)


def setup_inputs(seed: int = 0) -> dict:
    key_of = jax.random.split(jax.random.key(seed), 19)
    tokens = bell_draw(key_of[0], (SEQS, SEQUENCE_LENGTH, D), 1.0, 6.0, ((0, 8), (1, 4)))
    first_gain = jnp.clip(1.0 + 0.15 * jax.random.normal(key_of[1], (D,), jnp.float32), 0.25, 1.75).astype(jnp.bfloat16)
    first_bias = bell_draw(key_of[2], (D,), 0.5, 3.0, ((0, 32),))
    in_weight = bell_draw(key_of[3], (D, INNER), D ** -0.5, 0.15625, ((0, 32),))
    in_bias = bell_draw(key_of[4], (INNER,), 0.3, 2.0, ((0, 32),))
    second_gain = jnp.clip(1.0 + 0.15 * jax.random.normal(key_of[5], (INNER,), jnp.float32), 0.25, 1.75).astype(jnp.bfloat16)
    second_bias = bell_draw(key_of[6], (INNER,), 0.5, 3.0, ((0, 32),))
    conv_weight = bell_draw(key_of[7], (INNER, KERNEL_TAPS, INNER), (KERNEL_TAPS * INNER) ** -0.5, 0.109375, ((0, 32),))
    conv_bias = bell_draw(key_of[8], (INNER,), 0.3, 2.0, ((0, 32),))
    third_gain = jnp.clip(1.0 + 0.15 * jax.random.normal(key_of[9], (INNER,), jnp.float32), 0.25, 1.75).astype(jnp.bfloat16)
    third_bias = bell_draw(key_of[10], (INNER,), 0.5, 3.0, ((0, 32),))
    out_weight = bell_draw(key_of[11], (INNER, D), (INNER // 2) ** -0.5, 0.3125, ((0, 32),))
    out_bias = bell_draw(key_of[12], (D,), 0.3, 2.0, ((0, 32),))
    head_weight = bell_draw(key_of[13], (D, V), (D // 2) ** -0.5, 0.25, ((0, 32),))
    head_bias = bell_draw(key_of[14], (V,), 0.5, 3.0)
    residue_types = place_ends(jax.random.randint(key_of[15], (SEQS, SEQUENCE_LENGTH), 0, V), jax.random.fold_in(key_of[15], 1), 0, V - 1).astype(jnp.int32)
    mask_positions = draw_mask_positions(jax.random.fold_in(key_of[18], 71), 0)
    targets = place_ends(jax.random.randint(key_of[17], (SEQS, MASKED), 0, V), jax.random.fold_in(key_of[17], 1), 0, V - 1).astype(jnp.int32)
    return dict(tokens=tokens, first_gain=first_gain, first_bias=first_bias, in_weight=in_weight, in_bias=in_bias, second_gain=second_gain, second_bias=second_bias, conv_weight=conv_weight, conv_bias=conv_bias, third_gain=third_gain, third_bias=third_bias, out_weight=out_weight, out_bias=out_bias, head_weight=head_weight, head_bias=head_bias, residue_types=residue_types, mask_positions=mask_positions, targets=targets)


NORM_EPSILON = 1e-05
LOSS_SCALE = 16.0

@jax.custom_vjp
def low(v):
    return lax.optimization_barrier(v.astype(jnp.bfloat16)).astype(jnp.float32)

@jax.custom_vjp
def low_back(v):
    return v

def low_keep(v):
    return (low(v), None)

def low_pass(kept, grad):
    return (grad,)

def back_keep(v):
    return (v, None)

def back_low(kept, grad):
    return (low(grad),)
low.defvjp(low_keep, low_pass)
low_back.defvjp(back_keep, back_low)

def normed(inputs, factor, offset):
    average = lax.optimization_barrier(jnp.mean(inputs, axis=-1, keepdims=True))
    centred = inputs - average
    spread = lax.optimization_barrier(jnp.mean(centred * centred, axis=-1, keepdims=True))
    return jax.nn.gelu(centred * lax.rsqrt(spread + NORM_EPSILON) * factor + offset, approximate=False)

def project(former, latter):
    return jnp.einsum('gld,de->gle', former, latter, precision=lax.Precision.HIGHEST)

def conv_stack(series):
    receptive_span = KERNEL_TAPS // 2 * DILATION_RATE
    padded_input = jnp.pad(series, ((0, 0), (receptive_span, receptive_span), (0, 0)))
    return jnp.stack([padded_input[:, kernel_index * DILATION_RATE:kernel_index * DILATION_RATE + SEQUENCE_LENGTH] for kernel_index in range(KERNEL_TAPS)], axis=2)

def block_loss(weight_set, inputs, row_mask, row_target):
    gain_first, bias_first, matrix_in, bias_in, gain_second, bias_second, conv_full, bias_conv, gain_third, bias_third, matrix_out, bias_out, matrix_head, head_shift = weight_set
    first_act = low(normed(inputs, gain_first, bias_first))
    in_proj = low_back(project(first_act, matrix_in) + bias_in)
    conv_in = low_back(low(normed(in_proj, gain_second, bias_second)))
    conv_raw = jnp.einsum('glki,iko->glo', conv_stack(conv_in), conv_full, precision=lax.Precision.HIGHEST) + bias_conv
    conv_out = low_back(low(conv_raw))
    third_act = low(normed(conv_out, gain_third, bias_third))
    branch = low_back(project(third_act, matrix_out) + bias_out)
    block_out = low(inputs + branch)
    logits = low_back(project(block_out, matrix_head) + head_shift)
    highest = lax.optimization_barrier(jnp.max(logits, axis=-1, keepdims=True))
    log_total = highest[..., 0] + jnp.log(lax.optimization_barrier(jnp.sum(jnp.exp(logits - highest), axis=-1)))
    target_hot = (jnp.arange(V, dtype=jnp.int32) == row_target[..., None]).astype(inputs.dtype)
    picked = lax.optimization_barrier(jnp.sum(logits * target_hot, axis=-1))
    cross_entropy = log_total - picked
    objective = LOSS_SCALE * jnp.sum(row_mask * cross_entropy)
    return (objective, (block_out, cross_entropy, jnp.exp(picked - log_total)))

def reference(tokens, first_gain, first_bias, in_weight, in_bias, second_gain, second_bias, conv_weight, conv_bias, third_gain, third_bias, out_weight, out_bias, head_weight, head_bias, residue_types, mask_positions, targets):
    weights = tuple((member.astype(jnp.float32) for member in (first_gain, first_bias, in_weight, in_bias, second_gain, second_bias, conv_weight, conv_bias, third_gain, third_bias, out_weight, out_bias, head_weight, head_bias)))
    group_size = math.gcd(SEQS, max(1, 4096 // SEQUENCE_LENGTH))
    group_count = SEQS // group_size

    def grouped(array):
        return array.reshape((group_count, group_size) + array.shape[1:])
    places = jnp.arange(SEQUENCE_LENGTH, dtype=jnp.int32)
    vocab_ids = jnp.arange(V, dtype=jnp.int32)

    def scan_step(running, batch_item):
        gradients, counts_now, hits_now, loss_now = running
        token_rows, types_now, positions_now, targets_now = batch_item
        matches = positions_now[:, None, :] == places[None, :, None]
        row_mask = lax.optimization_barrier(jnp.sum(matches.astype(jnp.float32), axis=-1))
        row_target = lax.optimization_barrier(jnp.sum(jnp.where(matches, targets_now[:, None, :], 0), axis=-1)).astype(jnp.int32)
        objective, pullback, extras = jax.vjp(lambda weight_set, token_set: block_loss(weight_set, token_set, row_mask, row_target), weights, token_rows.astype(jnp.float32), has_aux=True)
        weight_grads, token_grads = pullback(jnp.ones_like(objective))
        block_out, cross_entropy, chance = extras
        type_hot = (vocab_ids == types_now[..., None]).astype(jnp.float32)
        counts_now = counts_now + lax.optimization_barrier(jnp.sum(row_mask[..., None] * type_hot, axis=(0, 1)))
        hits_now = hits_now + lax.optimization_barrier(jnp.sum((row_mask * chance)[..., None] * type_hot, axis=(0, 1)))
        loss_now = loss_now + jnp.sum(row_mask * cross_entropy)
        gradients = tuple((summed + added for summed, added in zip(gradients, weight_grads)))
        return ((gradients, counts_now, hits_now, loss_now), (block_out.astype(jnp.bfloat16), token_grads.astype(jnp.bfloat16)))
    starting = (tuple((jnp.zeros_like(member) for member in weights)), jnp.zeros((V,), jnp.float32), jnp.zeros((V,), jnp.float32), jnp.zeros((), jnp.float32))
    finished, outputs = lax.scan(scan_step, starting, (grouped(tokens), grouped(residue_types), grouped(mask_positions), grouped(targets)))
    gradients, counts_now, hits_now, loss_now = finished
    block_outs = outputs[0].reshape(SEQS, SEQUENCE_LENGTH, D)
    input_grads = outputs[1].reshape(SEQS, SEQUENCE_LENGTH, D)
    return (block_outs, input_grads, gradients[0], gradients[1], gradients[2], gradients[3], gradients[4], gradients[5], gradients[6], gradients[7], gradients[8], gradients[9], gradients[10], gradients[11], gradients[12], gradients[13], counts_now.astype(jnp.int32), hits_now, loss_now / (SEQS * MASKED))
```

```python
import jax
import jax.numpy as jnp
from jax import lax
from jax.sharding import PartitionSpec as P

KERNEL_TAPS = 5
DILATION_RATE = 128
NORM_EPSILON = 1e-05
LOSS_SCALE = 16.0
REACH = KERNEL_TAPS // 2 * DILATION_RATE
BF = jnp.bfloat16
F32 = jnp.float32


def normed(inputs, factor, offset):
    average = jnp.mean(inputs, axis=-1, keepdims=True)
    centred = inputs - average
    spread = jnp.mean(centred * centred, axis=-1, keepdims=True)
    return jax.nn.gelu(
        centred * lax.rsqrt(spread + NORM_EPSILON) * factor + offset, approximate=False
    )


def matmul(former, latter):
    return jnp.dot(former, latter, preferred_element_type=F32)


def against(former, latter):
    return lax.dot_general(former, latter, (((1,), (1,)), ((), ())), preferred_element_type=F32)


def outer_sum(former, latter):
    return lax.dot_general(former, latter, (((0,), (0,)), ((), ())), preferred_element_type=F32)


def swap(value, bit):
    count = lax.axis_size("dp")
    return lax.ppermute(value, "dp", [(i, i ^ bit) for i in range(count)])


def dp_bits():
    bits = []
    bit = 2
    while bit < lax.axis_size("dp"):
        bits.append(bit)
        bit *= 2
    return bits


def merge(own, other, bit):
    high = (lax.axis_index("dp") & bit) != 0
    return jnp.stack([jnp.where(high, other, own), jnp.where(high, own, other)])


def seq_gather(block):
    size = lax.axis_size("seq")
    me = lax.axis_index("seq")
    parts = [block] + [
        lax.ppermute(block, "seq", [(i, (i + k) % size) for i in range(size)])
        for k in range(1, size)
    ]
    ordered = []
    for place in range(size):
        value = parts[0]
        for k in range(1, size):
            value = jnp.where((me - place) % size == k, parts[k], value)
        ordered.append(value)
    return jnp.stack(ordered)


def gather_all(block):
    tail = block.shape
    size = lax.axis_size("seq")
    over_seq = seq_gather(block)
    bits = dp_bits()
    pieces = []
    for part, order in ((over_seq[: size // 2], bits), (over_seq[size // 2 :], bits[::-1])):
        value = part
        for bit in order:
            value = merge(value, swap(value, bit), bit)
        value = merge(value, swap(value, 1), 1)
        done = [1] + list(order)[::-1]
        wanted = bits[::-1] + [1]
        perm = [done.index(b) for b in wanted]
        rest = list(range(len(done), value.ndim))
        value = jnp.transpose(value, perm + rest)
        pieces.append(value.reshape((lax.axis_size("dp"), size // 2) + tail))
    return jnp.concatenate(pieces, axis=1)


def scatter_all(full):
    dp = lax.axis_size("dp")
    size = lax.axis_size("seq")
    tail = full.shape[2:]
    me = lax.axis_index("dp")
    seat = lax.axis_index("seq")
    bits = dp_bits()
    nbits = len(bits)
    grid = full.reshape((2,) * nbits + (2, size) + tail)
    axis_of = {bit: nbits - 1 - n for n, bit in enumerate(bits)}

    def fold(value, bit, axis):
        mine = ((me & bit) != 0).astype(jnp.int32)
        keep = lax.dynamic_index_in_dim(value, mine, axis, keepdims=True)
        send = lax.dynamic_index_in_dim(value, 1 - mine, axis, keepdims=True).astype(BF)
        return keep + swap(send, bit).astype(F32)

    grid = fold(grid, 1, nbits)
    halves = []
    for part, order in (
        (lax.slice_in_dim(grid, 0, size // 2, axis=nbits + 1), bits[::-1]),
        (lax.slice_in_dim(grid, size // 2, size, axis=nbits + 1), bits),
    ):
        for bit in order:
            part = fold(part, bit, axis_of[bit])
        halves.append(part.reshape((size // 2,) + tail))
    line = jnp.concatenate(halves, axis=0)
    total = lax.dynamic_index_in_dim(line, seat, 0, keepdims=False)
    for k in range(1, size):
        send = lax.dynamic_index_in_dim(line, (seat + k) % size, 0, keepdims=False).astype(BF)
        total = total + lax.ppermute(
            send, "seq", [(i, (i + k) % size) for i in range(size)]
        ).astype(F32)
    return total


def with_halo(series):
    size = lax.axis_size("seq")
    length = series.shape[1]
    hops = -(-REACH // length)
    before = [
        lax.ppermute(series, "seq", [(i, i + h) for i in range(size - h)])
        for h in range(hops, 0, -1)
    ]
    after = [
        lax.ppermute(series, "seq", [(i + h, i) for i in range(size - h)])
        for h in range(1, hops + 1)
    ]
    return jnp.concatenate(before + [series] + after, axis=1), hops * length


VECTORS = ("g1", "b1", "bi", "g2", "b2", "bc", "g3", "b3", "bo")


def shards(
    tokens,
    first_gain,
    first_bias,
    in_weight,
    in_bias,
    second_gain,
    second_bias,
    conv_weight,
    conv_bias,
    third_gain,
    third_bias,
    out_weight,
    out_bias,
    head_weight,
    head_bias,
    residue_types,
    mask_positions,
    targets,
):
    dp = lax.axis_size("dp")
    devices = dp * lax.axis_size("seq")
    seq_count, length, width = tokens.shape
    inner = in_weight.shape[1]
    vocab = head_weight.shape[1]
    rows = seq_count * length
    wide = width // devices
    narrow = inner // devices

    small = jnp.concatenate(
        [
            first_gain,
            first_bias,
            in_bias,
            second_gain,
            second_bias,
            conv_bias,
            third_gain,
            third_bias,
            out_bias,
            head_weight.reshape(-1),
        ]
    )
    small_rows = -(-small.shape[0] // inner)
    small_block = jnp.pad(small, (0, small_rows * inner - small.shape[0])).reshape(
        small_rows, inner
    )
    group_in = gather_all(jnp.concatenate([in_weight, small_block], axis=0))
    matrix_in = group_in[:, :, :wide].reshape(width, inner)
    smalls = group_in[:, :, wide:].reshape(devices, small_rows * inner)
    vectors = {}
    at = 0
    for name, piece in zip(
        VECTORS, (wide, wide, narrow, narrow, narrow, narrow, narrow, narrow, wide)
    ):
        vectors[name] = smalls[:, at : at + piece].reshape(-1).astype(F32)
        at += piece
    matrix_head = smalls[:, at : at + wide * vocab].reshape(width, vocab)

    conv_local = jnp.transpose(conv_weight, (1, 0, 2))
    group_conv = gather_all(conv_local)
    taps = jnp.transpose(group_conv, (2, 0, 1, 3, 4)).reshape(KERNEL_TAPS, inner, inner)
    matrix_out = gather_all(out_weight).reshape(inner, width)

    inputs = tokens.reshape(rows, width).astype(F32)
    first_value, first_pull = jax.vjp(normed, inputs, vectors["g1"], vectors["b1"])
    first_act = first_value.astype(BF)
    in_proj = matmul(first_act, matrix_in) + vectors["bi"]
    second_value, second_pull = jax.vjp(normed, in_proj, vectors["g2"], vectors["b2"])
    conv_in = second_value.astype(BF).reshape(seq_count, length, inner)
    conv_ext, base = with_halo(conv_in)
    starts = [base + (k - KERNEL_TAPS // 2) * DILATION_RATE for k in range(KERNEL_TAPS)]
    shifted = [conv_ext[:, at : at + length].reshape(rows, inner) for at in starts]
    conv_sum = vectors["bc"]
    for k in range(KERNEL_TAPS):
        conv_sum = conv_sum + matmul(shifted[k], taps[k])
    conv_out = conv_sum.astype(BF).astype(F32)
    third_value, third_pull = jax.vjp(normed, conv_out, vectors["g3"], vectors["b3"])
    third_act = third_value.astype(BF)
    block_out = (inputs + matmul(third_act, matrix_out) + vectors["bo"]).astype(BF)
    logits = matmul(block_out, matrix_head) + head_bias.astype(F32)
    highest = jnp.max(logits, axis=1, keepdims=True)
    log_total = highest[:, 0] + jnp.log(jnp.sum(jnp.exp(logits - highest), axis=1))
    places = lax.axis_index("seq") * length + jnp.arange(length, dtype=jnp.int32)
    matches = mask_positions[:, None, :] == places[None, :, None]
    row_mask = jnp.sum(matches.astype(F32), axis=2).reshape(rows)
    row_target = jnp.sum(jnp.where(matches, targets[:, None, :], 0), axis=2).reshape(rows)
    vocab_ids = jnp.arange(vocab, dtype=jnp.int32)
    target_hot = (vocab_ids[None, :] == row_target[:, None]).astype(F32)
    picked = jnp.sum(logits * target_hot, axis=1)
    cross_entropy = log_total - picked
    chance = jnp.exp(picked - log_total)
    type_hot = (vocab_ids[None, :] == residue_types.reshape(rows)[:, None]).astype(F32)
    local_counts = jnp.sum(row_mask[:, None] * type_hot, axis=0)
    local_hits = jnp.sum((row_mask * chance)[:, None] * type_hot, axis=0)
    local_loss = jnp.sum(row_mask * cross_entropy)
    softmax_probs = jnp.exp(logits - log_total[:, None])
    logit_grad = (LOSS_SCALE * row_mask[:, None] * (softmax_probs - target_hot)).astype(BF)
    head_shift_grad = jnp.sum(logit_grad.astype(F32), axis=0)
    head_matrix_grad = outer_sum(block_out, logit_grad)
    out_grad = against(logit_grad, matrix_head)
    out_grad_low = out_grad.astype(BF)
    out_matrix_grad = outer_sum(third_act, out_grad_low)
    out_shift_grad = jnp.sum(out_grad_low.astype(F32), axis=0)
    third_act_grad = against(out_grad_low, matrix_out)
    conv_out_grad, gain_third_grad, bias_third_grad = third_pull(third_act_grad)
    conv_out_low = conv_out_grad.astype(BF)
    conv_shift_grad = jnp.sum(conv_out_low.astype(F32), axis=0)
    grad_ext, _ = with_halo(conv_out_low.reshape(seq_count, length, inner))
    conv_matrix_grad = jnp.stack([outer_sum(shifted[k], conv_out_low) for k in range(KERNEL_TAPS)])
    second_grad = 0.0
    for k in range(KERNEL_TAPS):
        at = starts[KERNEL_TAPS - 1 - k]
        second_grad = second_grad + against(
            grad_ext[:, at : at + length].reshape(rows, inner), taps[k]
        )
    second_grad = second_grad.astype(BF).astype(F32)
    in_proj_grad, gain_second_grad, bias_second_grad = second_pull(second_grad)
    in_proj_low = in_proj_grad.astype(BF)
    in_shift_grad = jnp.sum(in_proj_low.astype(F32), axis=0)
    in_matrix_grad = outer_sum(first_act, in_proj_low)
    first_act_grad = against(in_proj_low, matrix_in)
    branch_grad, gain_first_grad, bias_first_grad = first_pull(first_act_grad)
    input_grad = (out_grad + branch_grad).astype(BF).reshape(seq_count, length, width)

    grid = (dp, devices // dp)
    conv_share = scatter_all(
        jnp.transpose(
            conv_matrix_grad.reshape((KERNEL_TAPS,) + grid + (narrow, inner)), (1, 2, 0, 3, 4)
        )
    )
    out_share = scatter_all(out_matrix_grad.reshape(grid + (narrow, width)))
    small_grads = jnp.concatenate(
        [
            piece.reshape(grid + (-1,))
            for piece in (
                gain_first_grad,
                bias_first_grad,
                in_shift_grad,
                gain_second_grad,
                bias_second_grad,
                conv_shift_grad,
                gain_third_grad,
                bias_third_grad,
                out_shift_grad,
                head_matrix_grad,
            )
        ],
        axis=2,
    )
    small_grads = jnp.pad(
        small_grads, ((0, 0), (0, 0), (0, small_rows * inner - small_grads.shape[2]))
    ).reshape(grid + (small_rows, inner))
    in_share = scatter_all(
        jnp.concatenate([in_matrix_grad.reshape(grid + (wide, inner)), small_grads], axis=2)
    )
    small_share = in_share[wide:].reshape(-1)
    pieces = []
    at = 0
    for piece in (wide, wide, narrow, narrow, narrow, narrow, narrow, narrow, wide):
        pieces.append(small_share[at : at + piece])
        at += piece
    head_share = small_share[at : at + wide * vocab].reshape(wide, vocab)
    summed_shift, summed_counts, summed_hits, summed_loss = lax.psum(
        (head_shift_grad, local_counts, local_hits, local_loss), ("dp", "seq")
    )
    masked_total = seq_count * dp * mask_positions.shape[1]
    return (
        block_out.reshape(seq_count, length, width),
        input_grad,
        pieces[0],
        pieces[1],
        in_share[:wide],
        pieces[2],
        pieces[3],
        pieces[4],
        jnp.transpose(conv_share, (1, 0, 2)),
        pieces[5],
        pieces[6],
        pieces[7],
        out_share,
        pieces[8],
        head_share,
        summed_shift,
        summed_counts.astype(jnp.int32),
        summed_hits,
        summed_loss / masked_total,
    )


def solution(mesh):
    both = P(("dp", "seq"))
    matrix = P(("dp", "seq"), None)
    cube = P(("dp", "seq"), None, None)
    rows = P("dp", "seq", None)
    return jax.shard_map(
        shards,
        mesh=mesh,
        in_specs=(
            rows,
            both,
            both,
            matrix,
            both,
            both,
            both,
            cube,
            both,
            both,
            both,
            matrix,
            both,
            matrix,
            P(),
            P("dp", "seq"),
            P("dp", None),
            P("dp", None),
        ),
        out_specs=(
            rows,
            rows,
            both,
            both,
            matrix,
            both,
            both,
            both,
            cube,
            both,
            both,
            both,
            matrix,
            both,
            matrix,
            P(),
            P(),
            P(),
            P(),
        ),
        check_vma=False,
    )
```

```python
import functools

import jax
import jax.numpy as jnp
from jax import lax
from jax.experimental import pallas as pl
from jax.experimental.pallas import tpu as pltpu
from jax.sharding import PartitionSpec as P

KERNEL_TAPS = 5
CENTRE = KERNEL_TAPS // 2
DILATION_RATE = 128
NORM_EPSILON = 1e-05
LOSS_SCALE = 16.0
REACH = CENTRE * DILATION_RATE
BF = jnp.bfloat16
F32 = jnp.float32
LANES = 128
WIDE_VECTORS = 3
NARROW_VECTORS = 6
MIB = 1024 * 1024
HALF_ROOT = 0.7071067811865476
INV_ROOT_TWO_PI = 0.3989422804014327


def gauss(u):
    z = jnp.abs(u) * HALF_ROOT
    t = pl.reciprocal(1.0 + 0.3275911 * z, approx=False)
    e = jnp.exp(-0.5 * u * u)
    poly = t * (
        0.254829592
        + t * (-0.284496736 + t * (1.421413741 + t * (-1.453152027 + t * 1.061405429)))
    )
    tail = 0.5 * poly * e
    return jnp.where(u < 0, tail, 1.0 - tail), e * INV_ROOT_TWO_PI


def standardize(v):
    average = jnp.mean(v, axis=-1, keepdims=True)
    centred = v - average
    spread = jnp.mean(centred * centred, axis=-1, keepdims=True)
    r = lax.rsqrt(spread + NORM_EPSILON)
    return centred * r, r


def dot(a, b):
    return jnp.dot(a, b, preferred_element_type=F32)


def dot_nt(a, b):
    return lax.dot_general(a, b, (((1,), (1,)), ((), ())), preferred_element_type=F32)


def dot_tn(a, b):
    return lax.dot_general(a, b, (((0,), (0,)), ((), ())), preferred_element_type=F32)


def rows8(x):
    return jnp.sum(x.reshape(x.shape[0] // 8, 8, x.shape[1]), axis=0)


def each_chunk(count, step, body):
    @pl.loop(0, count // step)
    def _(i):
        body(pl.ds(pl.multiple_of(i * step, step), step))


def thirds(x):
    high = x.astype(BF)
    rest = x - high.astype(F32)
    mid = rest.astype(BF)
    low = (rest - mid.astype(F32)).astype(BF)
    return high, mid, low


def vmem(n):
    return [pl.BlockSpec(memory_space=pltpu.VMEM)] * n


def call(kernel, ins, outs, scratch=(), flops=0, limit=24, name=None):
    moved = sum(x.size * x.dtype.itemsize for x in ins)
    moved += sum(o.size * o.dtype.itemsize for o in outs)
    return pl.pallas_call(
        kernel,
        out_shape=list(outs),
        in_specs=vmem(len(ins)),
        out_specs=vmem(len(outs)),
        scratch_shapes=list(scratch),
        compiler_params=pltpu.CompilerParams(vmem_limit_bytes=limit * MIB),
        cost_estimate=pl.CostEstimate(flops=int(flops), bytes_accessed=int(moved), transcendentals=0),
        name=name,
    )(*ins)


def sds(shape, dtype):
    return jax.ShapeDtypeStruct(shape, dtype)


def pack_kernel(vocab, w_in, head_t, *rest):
    vecs = rest[: WIDE_VECTORS + NARROW_VECTORS]
    conv, w_out, group_a, group_b, tile = rest[WIDE_VECTORS + NARROW_VECTORS :]
    wide, inner = w_in.shape
    tile[...] = jnp.zeros_like(tile)
    tile[0:vocab, 0:wide] = head_t[...].astype(F32)
    for j, v in enumerate(vecs):
        n = v.shape[-1]
        tile[vocab + j : vocab + j + 1, 0:n] = v[...].astype(F32).reshape(1, n)
    group_a[:, 0:inner] = w_in[...]
    group_a[:, inner : inner + LANES] = jnp.transpose(tile[...])[0:wide].astype(BF)
    group_b[0:KERNEL_TAPS] = conv[...]
    for h in range(w_out.shape[1] // inner):
        group_b[KERNEL_TAPS + h] = w_out[:, h * inner : (h + 1) * inner]


def place_kernel(axis, n, *refs):
    parts, out = refs[:n], refs[n]
    me = lax.axis_index(axis)
    values = [p[...].astype(F32) for p in parts]
    ordered = []
    for place in range(n):
        value = values[0]
        for k in range(1, n):
            value = jnp.where(lax.rem(me - place + n, n) == k, values[k], value)
        ordered.append(value)
    out[...] = jnp.concatenate(ordered, axis=-2).astype(BF)


def first_kernel(tokens, n1, r1):
    width = tokens.shape[1]

    def body(c):
        n, r = standardize(tokens[c, :].astype(F32))
        n1[c, :] = n
        r1[c, :] = jnp.broadcast_to(r, (r.shape[0], LANES))

    each_chunk(tokens.shape[0], 16, body)


def spread_matrix(width, inner, wide, narrow):
    row = lax.broadcasted_iota(jnp.int32, (width, 1), 0)
    device = row // wide
    r = row - device * wide
    at = jnp.where(r < narrow, device * narrow + r, -1)
    return (lax.broadcasted_iota(jnp.int32, (width, inner), 1) == at).astype(F32).astype(BF)


def second_kernel(chips, vocab, wide, narrow, n1, *refs):
    pieces = refs[: 2 * chips]
    (w_in, extras, wide_v, narrow_v, act, gp1, n2, gp2, r2, conv_in, proj) = refs[2 * chips :]
    width, inner = w_in.shape
    rows = n1.shape[0]
    me = lax.axis_index("dp")
    block = pieces[0].shape[0]
    for c in range(2):
        for m in range(chips):
            at = pl.multiple_of((me ^ (2 * m + c)) * block, block)
            w_in[pl.ds(at, block), :] = pieces[c * chips + m][:, 0:inner]
            extras[pl.ds(at, block), :] = pieces[c * chips + m][:, inner : inner + LANES]
    turned = jnp.transpose(extras[...].astype(F32))
    wide_v[...] = jnp.zeros_like(wide_v)
    wide_v[0:WIDE_VECTORS, :] = turned[vocab : vocab + WIDE_VECTORS]
    first = vocab + WIDE_VECTORS
    narrow_v[0:NARROW_VECTORS, :] = dot(
        turned.astype(BF), spread_matrix(width, inner, wide, narrow)
    )[first : first + NARROW_VECTORS]
    g1, b1 = wide_v[0:1, :], wide_v[1:2, :]
    bias, g2, b2 = narrow_v[0:1, :], narrow_v[1:2, :], narrow_v[2:3, :]

    def body(c):
        u = n1[c, :] * g1 + b1
        cdf, pdf = gauss(u)
        act[c, :] = (u * cdf).astype(BF)
        gp1[c, :] = cdf + u * pdf

    each_chunk(rows, 16, body)
    proj[...] = dot(act[...], w_in[...])

    def later(c):
        n, r = standardize(proj[c, :] + bias)
        u = n * g2 + b2
        cdf, pdf = gauss(u)
        conv_in[c, :] = (u * cdf).astype(BF)
        gp2[c, :] = cdf + u * pdf
        n2[c, :] = n
        r2[c, :] = jnp.broadcast_to(r, (r.shape[0], LANES))

    each_chunk(rows, 32, later)


def middle_kernel(
    chips,
    hops,
    seqs,
    vocab,
    wide_v,
    narrow_v,
    extras,
    head_bias,
    types,
    positions,
    targets,
    tokens,
    *refs,
):
    blocks = refs[: 2 * hops + 1]
    pieces = refs[2 * hops + 1 : 2 * hops + 1 + 2 * chips]
    (
        taps,
        block_out,
        third_act,
        out_low,
        logit_grad,
        head_grad,
        conv_low,
        narrow_sums,
        wide_sums,
        stats,
        ext,
        n3,
        gp3,
        r3,
        work,
    ) = refs[2 * hops + 1 + 2 * chips :]
    inner = taps.shape[1]
    width = tokens.shape[1]
    rows = tokens.shape[0]
    length = rows // seqs
    me = lax.axis_index("dp")
    block = pieces[0].shape[1]
    for c in range(2):
        for m in range(chips):
            at = pl.multiple_of((me ^ (2 * m + c)) * block, block)
            for slab in range(taps.shape[0]):
                taps[slab, pl.ds(at, block), :] = pieces[c * chips + m][slab]
    for b, ref in enumerate(blocks):
        ext[:, b * length : (b + 1) * length, :] = ref[...]
    bias, g3, b3 = narrow_v[3:4, :], narrow_v[4:5, :], narrow_v[5:6, :]
    bias_out = wide_v[2:3, :]
    narrow_sums[...] = jnp.zeros_like(narrow_sums)
    wide_sums[...] = jnp.zeros_like(wide_sums)
    stats[...] = jnp.zeros_like(stats)
    head_grad[...] = jnp.zeros_like(head_grad)
    seat = lax.axis_index("seq")

    @pl.loop(0, seqs)
    def _(s):
        whole = pl.ds(pl.multiple_of(s * length, length), length)
        total = dot(ext[s, pl.ds(hops * length - REACH, length), :], taps[0])
        for k in range(1, KERNEL_TAPS):
            at = hops * length + (k - CENTRE) * DILATION_RATE
            total += dot(ext[s, pl.ds(at, length), :], taps[k])
        work[:, 0:inner] = total

        def ahead(c):
            low = (work[c, 0:inner] + bias).astype(BF).astype(F32)
            n, r = standardize(low)
            u = n * g3 + b3
            cdf, pdf = gauss(u)
            here = pl.ds(pl.multiple_of(s * length + c.start, c.size), c.size)
            third_act[here, :] = (u * cdf).astype(BF)
            gp3[c, :] = cdf + u * pdf
            n3[c, :] = n
            r3[c, :] = jnp.broadcast_to(r, (r.shape[0], LANES))

        each_chunk(length, 32, ahead)
        for h in range(width // inner):
            work[:, h * inner : (h + 1) * inner] = dot(third_act[whole, :], taps[KERNEL_TAPS + h])

        def add(c):
            here = pl.ds(pl.multiple_of(s * length + c.start, c.size), c.size)
            block_out[here, :] = (tokens[here, :].astype(F32) + work[c, :] + bias_out).astype(BF)

        each_chunk(length, 32, add)
        lane = lax.broadcasted_iota(jnp.int32, (length, LANES), 1)
        logits = dot(block_out[whole, :], extras[...]) + head_bias[...]
        logits = jnp.where(lane < vocab, logits, -1e30)
        highest = jnp.max(logits, axis=1, keepdims=True)
        raised = jnp.exp(logits - highest)
        log_total = highest + jnp.log(jnp.sum(raised, axis=1, keepdims=True))
        place = lax.broadcasted_iota(jnp.int32, (length, positions.shape[1]), 0) + seat * length
        matches = positions[pl.ds(s, 1), :] == place
        mask = jnp.sum(jnp.where(matches, 1.0, 0.0), axis=1, keepdims=True)
        goal = jnp.sum(
            jnp.where(matches, targets[pl.ds(s, 1), :].astype(F32), 0.0), axis=1, keepdims=True
        )
        hot = jnp.where(lane == goal.astype(jnp.int32), 1.0, 0.0)
        picked = jnp.sum(logits * hot, axis=1, keepdims=True)
        entropy = log_total - picked
        chance = jnp.exp(picked - log_total)
        grad = (LOSS_SCALE * mask * (jnp.exp(logits - log_total) - hot)).astype(BF)
        logit_grad[whole, :] = grad
        columns = jnp.where(lane == 0, mask, jnp.where(lane == 1, mask * chance, 0.0))
        kinds = lax.broadcasted_iota(jnp.int32, (LANES, length), 0) == types[pl.ds(s, 1), :]
        tallies = jnp.dot(
            jnp.where(kinds, 1.0, 0.0),
            columns,
            preferred_element_type=F32,
            precision=lax.Precision.HIGHEST,
        )
        stats[0:2, :] += jnp.transpose(tallies)[0:2]
        stats[2:3, :] += jnp.sum(grad.astype(F32), axis=0, keepdims=True)
        stats[3:4, :] += jnp.broadcast_to(
            jnp.sum(mask * entropy, axis=0, keepdims=True), (1, LANES)
        )
        head_grad[...] += dot_tn(block_out[whole, :], grad)
        work[...] = dot_nt(grad, extras[...])

        def lower(c):
            here = pl.ds(pl.multiple_of(s * length + c.start, c.size), c.size)
            low = work[c, :].astype(BF)
            out_low[here, :] = low
            wide_sums[...] += rows8(low.astype(F32))

        each_chunk(length, 32, lower)
        back = dot_nt(out_low[whole, 0:inner], taps[KERNEL_TAPS])
        for h in range(1, width // inner):
            back += dot_nt(out_low[whole, h * inner : (h + 1) * inner], taps[KERNEL_TAPS + h])
        work[:, 0:inner] = back

        def behind(c):
            e = work[c, 0:inner] * gp3[c, :]
            n = n3[c, :]
            narrow_sums[0:8, :] += rows8(e * n)
            narrow_sums[8:16, :] += rows8(e)
            eg = e * g3
            mean_e = jnp.mean(eg, axis=1, keepdims=True)
            mean_en = jnp.mean(eg * n, axis=1, keepdims=True)
            low = (r3[c, 0:1] * (eg - mean_e - n * mean_en)).astype(BF)
            here = pl.ds(pl.multiple_of(s * length + c.start, c.size), c.size)
            conv_low[here, :] = low
            narrow_sums[16:24, :] += rows8(low.astype(F32))

        each_chunk(length, 32, behind)


def conv_grad_kernel(chips, hops, seqs, third_act, out_low, conv_low, *refs):
    blocks = refs[: 2 * hops + 1]
    keep, send, turned, total, third_t = refs[2 * hops + 1 :]
    inner = conv_low.shape[1]
    length = conv_low.shape[0] // seqs
    block = keep.shape[2]
    me = lax.axis_index("dp")
    core = me & 1
    slabs = keep.shape[1]
    for s in range(seqs):
        for b, ref in enumerate(blocks):
            turned[s, :, b * length : (b + 1) * length] = jnp.transpose(ref[s])
    third_t[...] = jnp.transpose(third_act[...])

    def share(slab):
        for q in range(chips):
            mine = pl.multiple_of((2 * q + core) * block, block)
            other = pl.multiple_of((2 * q + 1 - core) * block, block)
            keep[q, slab] = total[pl.ds(mine, block), :]
            send[q, slab] = total[pl.ds(other, block), :].astype(BF)

    for k in range(KERNEL_TAPS):
        at = hops * length + (k - CENTRE) * DILATION_RATE
        value = dot(turned[0, :, at : at + length], conv_low[0:length, :])
        for s in range(1, seqs):
            value += dot(
                turned[s, :, at : at + length], conv_low[s * length : (s + 1) * length, :]
            )
        total[...] = value
        share(k)
    for h in range(slabs - KERNEL_TAPS):
        total[...] = dot(third_t[...], out_low[:, h * inner : (h + 1) * inner])
        share(KERNEL_TAPS + h)


def split_b_kernel(chips, keep, got, stats, stats_got, own, own_stats, *sends):
    me = lax.axis_index("dp") // 2
    slabs, block, inner = keep.shape[1:]
    total_stats = stats[...] + stats_got[...]
    own_stats[...] = total_stats
    own[...] = keep[me] + got[me].astype(F32)
    for m in range(1, chips):
        q = me ^ m
        for slab in range(slabs):
            sends[m - 1][slab * block : (slab + 1) * block, :] = (
                keep[q, slab] + got[q, slab].astype(F32)
            ).astype(BF)
        tail = sends[m - 1].at[slabs * block : slabs * block + 16, :]
        tail[...] = jnp.zeros_like(tail)
        for j, term in enumerate(thirds(total_stats)):
            sends[m - 1][slabs * block : slabs * block + 8, j * LANES : (j + 1) * LANES] = term


def sum_terms(ref_value):
    return (
        ref_value[0:8, 0:LANES].astype(F32)
        + ref_value[0:8, LANES : 2 * LANES].astype(F32)
        + ref_value[0:8, 2 * LANES : 3 * LANES].astype(F32)
    )


def line_b_kernel(count, size, part, own, stats, *refs):
    parts = refs[:count]
    keep, keep_stats = refs[count : count + 2]
    sends = refs[count + 2 :]
    slabs, block, inner = own.shape
    me = lax.axis_index("seq")
    sums = stats[...]
    for p in parts:
        sums += sum_terms(p[slabs * block : slabs * block + 16, :])
    keep_stats[...] = sums
    for send in sends:
        send[slabs] = jnp.zeros(send.shape[1:], BF)
        for j, term in enumerate(thirds(sums)):
            send[slabs, 0:8, j * LANES : (j + 1) * LANES] = term
    for slab in range(slabs):
        value = own[slab]
        for p in parts:
            value += p[slab * block : (slab + 1) * block, :].astype(F32)
        cut = [value[z * part : (z + 1) * part] for z in range(size)]
        for k in range(size):
            piece = cut[0]
            for z in range(1, size):
                piece = jnp.where(lax.rem(me + k, size) == z, cut[z], piece)
            if k == 0:
                keep[slab] = piece
            else:
                sends[k - 1][slab, 0:part, :] = piece.astype(BF)


def end_b_kernel(count, keep, stats, *refs):
    parts = refs[:count]
    conv, out, sums, = refs[count:]
    slabs, part, inner = keep.shape
    total = stats[...]
    for p in parts:
        total += sum_terms(p[slabs])
    sums[...] = total
    for slab in range(slabs):
        value = keep[slab]
        for p in parts:
            value += p[slab, 0:part, :].astype(F32)
        if slab < KERNEL_TAPS:
            conv[slab] = value
        else:
            out[:, (slab - KERNEL_TAPS) * inner : (slab - KERNEL_TAPS + 1) * inner] = value


def split_a_kernel(chips, keep, got, own, *sends):
    me = lax.axis_index("dp") // 2
    own[...] = keep[me] + got[me].astype(F32)
    for m in range(1, chips):
        sends[m - 1][...] = (keep[me ^ m] + got[me ^ m].astype(F32)).astype(BF)


def line_a_kernel(count, size, part, own, *refs):
    parts = refs[:count]
    keep = refs[count]
    sends = refs[count + 1 :]
    me = lax.axis_index("seq")
    value = own[...]
    for p in parts:
        value += p[...].astype(F32)
    cut = [value[z * part : (z + 1) * part] for z in range(size)]
    for k in range(size):
        piece = cut[0]
        for z in range(1, size):
            piece = jnp.where(lax.rem(me + k, size) == z, cut[z], piece)
        if k == 0:
            keep[...] = piece
        else:
            sends[k - 1][...] = piece.astype(BF)


def end_a_kernel(count, vocab, keep, *refs):
    parts = refs[:count]
    w_in, head_t = refs[count : count + 2]
    vecs = refs[count + 2 : count + 2 + WIDE_VECTORS + NARROW_VECTORS]
    (tile,) = refs[count + 2 + WIDE_VECTORS + NARROW_VECTORS :]
    wide, inner = w_in.shape
    value = keep[...]
    for p in parts:
        value += p[...].astype(F32)
    w_in[...] = value[:, 0:inner]
    tile[...] = jnp.zeros_like(tile)
    tile[0:wide, :] = value[:, inner : inner + LANES]
    turned = jnp.transpose(tile[...])
    head_t[...] = turned[0:vocab, 0:wide]
    for j, v in enumerate(vecs):
        n = v.shape[-1]
        v[...] = turned[vocab + j : vocab + j + 1, 0:n].reshape(v.shape)


def back_kernel(
    chips,
    hops,
    seqs,
    vocab,
    wide,
    narrow,
    taps,
    n2,
    gp2,
    r2,
    n1,
    gp1,
    act,
    w_in,
    wide_v,
    narrow_v,
    narrow_sums,
    wide_sums,
    head_grad,
    *refs,
):
    blocks = refs[: 2 * hops + 1]
    keep, send, e1, low, ext, work, act_t, sums1, sums2 = refs[2 * hops + 1 :]
    width, inner = w_in.shape
    rows = low.shape[0]
    length = rows // seqs
    g2 = narrow_v[1:2, :]
    for b, ref in enumerate(blocks):
        ext[:, b * length : (b + 1) * length, :] = ref[...]
    sums1[...] = jnp.zeros_like(sums1)
    sums2[...] = jnp.zeros_like(sums2)

    @pl.loop(0, seqs)
    def _(s):
        whole = pl.ds(pl.multiple_of(s * length, length), length)
        total = dot_nt(ext[s, pl.ds(hops * length + REACH, length), :], taps[0])
        for k in range(1, KERNEL_TAPS):
            at = hops * length - (k - CENTRE) * DILATION_RATE
            total += dot_nt(ext[s, pl.ds(at, length), :], taps[k])
        work[:, 0:inner] = total

        def second(c):
            here = pl.ds(pl.multiple_of(s * length + c.start, c.size), c.size)
            e = work[c, 0:inner].astype(BF).astype(F32) * gp2[here, :]
            n = n2[here, :]
            sums2[0:8, :] += rows8(e * n)
            sums2[8:16, :] += rows8(e)
            eg = e * g2
            mean_e = jnp.mean(eg, axis=1, keepdims=True)
            mean_en = jnp.mean(eg * n, axis=1, keepdims=True)
            value = (r2[here, 0:1] * (eg - mean_e - n * mean_en)).astype(BF)
            low[here, :] = value
            sums2[16:24, :] += rows8(value.astype(F32))

        each_chunk(length, 32, second)
        work[...] = dot_nt(low[whole, :], w_in[...])

        def first(c):
            here = pl.ds(pl.multiple_of(s * length + c.start, c.size), c.size)
            e = work[c, :] * gp1[here, :]
            e1[here, :] = e
            sums1[0:8, :] += rows8(e * n1[here, :])
            sums1[8:16, :] += rows8(e)

        each_chunk(length, 16, first)

    def folded(ref, j):
        return jnp.sum(ref[8 * j : 8 * j + 8, :], axis=0, keepdims=True)

    wides = [folded(sums1, 0), folded(sums1, 1), folded(wide_sums, 0)]
    narrows = [folded(sums2, 2), folded(sums2, 0), folded(sums2, 1)]
    narrows += [folded(narrow_sums, 2), folded(narrow_sums, 0), folded(narrow_sums, 1)]
    row = lax.broadcasted_iota(jnp.int32, (16, inner), 0)
    stacked = jnp.zeros((16, inner), F32)
    for j, v in enumerate(narrows):
        stacked = jnp.where(row == j, v, stacked)
    spread = spread_matrix(width, inner, wide, narrow)
    placed = 0.0
    for term in thirds(stacked):
        placed = placed + dot_nt(term, spread)
    row = lax.broadcasted_iota(jnp.int32, (LANES, width), 0)
    grid = jnp.zeros((LANES, width), F32)
    for j, v in enumerate(wides):
        grid = jnp.where(row == vocab + j, v, grid)
    for j in range(NARROW_VECTORS):
        grid = jnp.where(row == vocab + WIDE_VECTORS + j, placed[j : j + 1, :], grid)
    extra = jnp.transpose(grid) + head_grad[...]
    act_t[...] = jnp.transpose(act[...])
    core = lax.axis_index("dp") & 1
    block = keep.shape[1]
    for q in range(chips):
        for c in range(2):
            d = 2 * q + c
            lines = slice(d * block, (d + 1) * block)
            value = dot(act_t[lines, :], low[...])

            @pl.when(core == c)
            def _():
                keep[q, :, 0:inner] = value
                keep[q, :, inner : inner + LANES] = extra[lines]

            @pl.when(core != c)
            def _():
                send[q, :, 0:inner] = value.astype(BF)
                send[q, :, inner : inner + LANES] = extra[lines].astype(BF)


def input_kernel(e1, n1, r1, wide_v, logit_grad, extras, input_grad, work):
    work[...] = dot_nt(logit_grad[...], extras[...])
    g1 = wide_v[0:1, :]

    def body(c):
        n = n1[c, :]
        eg = e1[c, :] * g1
        mean_e = jnp.mean(eg, axis=1, keepdims=True)
        mean_en = jnp.mean(eg * n, axis=1, keepdims=True)
        input_grad[c, :] = (work[c, :] + r1[c, 0:1] * (eg - mean_e - n * mean_en)).astype(BF)

    each_chunk(e1.shape[0], 16, body)


def swap(value, mask):
    count = lax.axis_size("dp")
    return lax.ppermute(value, "dp", [(i, i ^ mask) for i in range(count)])


def shifted(value, k):
    size = lax.axis_size("seq")
    return lax.ppermute(value, "seq", [(i, (i + k) % size) for i in range(size)])


def line_parts(block):
    return [block] + [shifted(block, k) for k in range(1, lax.axis_size("seq"))]


def chip_pieces(block):
    chips = lax.axis_size("dp") // 2
    own = [block] + [swap(block, 2 * m) for m in range(1, chips)]
    return own + [swap(piece, 1) for piece in own]


def halo(series):
    size = lax.axis_size("seq")
    hops = -(-REACH // series.shape[1])
    before = [
        lax.ppermute(series, "seq", [(i, i + h) for i in range(size - h)])
        for h in range(hops, 0, -1)
    ]
    after = [
        lax.ppermute(series, "seq", [(i + h, i) for i in range(size - h)])
        for h in range(1, hops + 1)
    ]
    return before + [series] + after


def shards(
    tokens,
    first_gain,
    first_bias,
    in_weight,
    in_bias,
    second_gain,
    second_bias,
    conv_weight,
    conv_bias,
    third_gain,
    third_bias,
    out_weight,
    out_bias,
    head_weight,
    head_bias,
    residue_types,
    mask_positions,
    targets,
):
    dp = lax.axis_size("dp")
    size = lax.axis_size("seq")
    chips = dp // 2
    seqs, length, width = tokens.shape
    wide, inner = in_weight.shape
    narrow = out_weight.shape[0]
    vocab = head_weight.shape[1]
    rows = seqs * length
    hops = -(-REACH // length)
    slabs = KERNEL_TAPS + width // inner
    flat = tokens.reshape(rows, width)

    block_a, block_b = call(
        functools.partial(pack_kernel, vocab),
        [
            in_weight,
            head_weight.T,
            first_gain,
            first_bias,
            out_bias,
            in_bias,
            second_gain,
            second_bias,
            conv_bias,
            third_gain,
            third_bias,
            jnp.transpose(conv_weight, (1, 0, 2)),
            out_weight,
        ],
        [sds((wide, inner + LANES), BF), sds((slabs, narrow, inner), BF)],
        [pltpu.VMEM((LANES, LANES), F32)],
        name="pack",
    )
    parts_a = line_parts(block_a)
    parts_b = line_parts(block_b)
    n1, r1 = call(
        first_kernel,
        [flat],
        [sds((rows, width), F32), sds((rows, LANES), F32)],
        flops=1e9,
        name="first",
    )
    (line_a,) = call(
        functools.partial(place_kernel, "seq", size),
        parts_a,
        [sds((size * wide, inner + LANES), BF)],
        name="line_a",
    )
    pieces_a = chip_pieces(line_a)
    (line_b,) = call(
        functools.partial(place_kernel, "seq", size),
        parts_b,
        [sds((slabs, size * narrow, inner), BF)],
        name="line_b",
    )
    pieces_b = chip_pieces(line_b)
    w_in, extras, wide_v, narrow_v, act, gp1, n2, gp2, r2, conv_in = call(
        functools.partial(second_kernel, chips, vocab, wide, narrow),
        [n1] + pieces_a,
        [
            sds((width, inner), BF),
            sds((width, LANES), BF),
            sds((8, width), F32),
            sds((8, inner), F32),
            sds((rows, width), BF),
            sds((rows, width), F32),
            sds((rows, inner), F32),
            sds((rows, inner), F32),
            sds((rows, LANES), F32),
            sds((rows, inner), BF),
        ],
        [pltpu.VMEM((rows, inner), F32)],
        flops=10e9,
        limit=40,
        name="second",
    )
    blocks = halo(conv_in.reshape(seqs, length, inner))
    (
        taps,
        block_out,
        third_act,
        out_low,
        logit_grad,
        head_grad,
        conv_low,
        narrow_sums,
        wide_sums,
        stats,
    ) = call(
        functools.partial(middle_kernel, chips, hops, seqs, vocab),
        [
            wide_v,
            narrow_v,
            extras,
            jnp.pad(head_bias.astype(F32), (0, LANES - vocab)).reshape(1, LANES),
            residue_types,
            mask_positions,
            targets,
            flat,
        ]
        + blocks
        + pieces_b,
        [
            sds((slabs, inner, inner), BF),
            sds((rows, width), BF),
            sds((rows, inner), BF),
            sds((rows, width), BF),
            sds((rows, LANES), BF),
            sds((width, LANES), F32),
            sds((rows, inner), BF),
            sds((24, inner), F32),
            sds((8, width), F32),
            sds((8, LANES), F32),
        ],
        [
            pltpu.VMEM((seqs, (2 * hops + 1) * length, inner), BF),
            pltpu.VMEM((length, inner), F32),
            pltpu.VMEM((length, inner), F32),
            pltpu.VMEM((length, LANES), F32),
            pltpu.VMEM((length, width), F32),
        ],
        flops=25e9,
        limit=48,
        name="middle",
    )
    grad_blocks = halo(conv_low.reshape(seqs, length, inner))
    keep_b, send_b = call(
        functools.partial(conv_grad_kernel, chips, hops, seqs),
        [third_act, out_low, conv_low] + blocks,
        [
            sds((chips, slabs, size * narrow, inner), F32),
            sds((chips, slabs, size * narrow, inner), BF),
        ],
        [
            pltpu.VMEM((seqs, inner, (2 * hops + 1) * length), BF),
            pltpu.VMEM((inner, inner), F32),
            pltpu.VMEM((inner, rows), BF),
        ],
        flops=8e9,
        limit=40,
        name="conv_grad",
    )
    got_b = swap(send_b, 1)
    got_stats = swap(stats, 1)
    split = call(
        functools.partial(split_b_kernel, chips),
        [keep_b, got_b, stats, got_stats],
        [sds((slabs, size * narrow, inner), F32), sds((8, LANES), F32)]
        + [sds((slabs * size * narrow + 16, inner), BF)] * (chips - 1),
        limit=32,
        name="split_b",
    )
    from_chips = [swap(piece, 2 * m) for m, piece in zip(range(1, chips), split[2:])]
    line = call(
        functools.partial(line_b_kernel, chips - 1, size, narrow),
        [split[0], split[1]] + from_chips,
        [sds((slabs, narrow, inner), F32), sds((8, LANES), F32)]
        + [sds((slabs + 1, max(narrow, 8), inner), BF)] * (size - 1),
        name="line_grad_b",
    )
    from_line = [shifted(piece, k) for k, piece in zip(range(1, size), line[2:])]
    conv_share, out_share, sums = call(
        functools.partial(end_b_kernel, size - 1),
        [line[0], line[1]] + from_line,
        [sds((KERNEL_TAPS, narrow, inner), F32), sds((narrow, width), F32), sds((8, LANES), F32)],
        name="end_b",
    )

    keep_a, send_a, e1 = call(
        functools.partial(back_kernel, chips, hops, seqs, vocab, wide, narrow),
        [taps, n2, gp2, r2, n1, gp1, act, w_in, wide_v, narrow_v]
        + [narrow_sums, wide_sums, head_grad]
        + grad_blocks,
        [
            sds((chips, size * wide, inner + LANES), F32),
            sds((chips, size * wide, inner + LANES), BF),
            sds((rows, width), F32),
        ],
        [
            pltpu.VMEM((rows, inner), BF),
            pltpu.VMEM((seqs, (2 * hops + 1) * length, inner), BF),
            pltpu.VMEM((length, width), F32),
            pltpu.VMEM((width, rows), BF),
            pltpu.VMEM((16, width), F32),
            pltpu.VMEM((24, inner), F32),
        ],
        flops=20e9,
        limit=56,
        name="back",
    )
    got_a = swap(send_a, 1)
    split = call(
        functools.partial(split_a_kernel, chips),
        [keep_a, got_a],
        [sds((size * wide, inner + LANES), F32)]
        + [sds((size * wide, inner + LANES), BF)] * (chips - 1),
        name="split_a",
    )
    from_chips = [swap(piece, 2 * m) for m, piece in zip(range(1, chips), split[1:])]
    (input_grad,) = call(
        input_kernel,
        [e1, n1, r1, wide_v, logit_grad, extras],
        [sds((rows, width), BF)],
        [pltpu.VMEM((rows, width), F32)],
        flops=5e9,
        name="input",
    )
    line = call(
        functools.partial(line_a_kernel, chips - 1, size, wide),
        [split[0]] + from_chips,
        [sds((wide, inner + LANES), F32)] + [sds((wide, inner + LANES), BF)] * (size - 1),
        name="line_grad_a",
    )
    from_line = [shifted(piece, k) for k, piece in zip(range(1, size), line[1:])]
    ended = call(
        functools.partial(end_a_kernel, size - 1, vocab),
        [line[0]] + from_line,
        [sds((wide, inner), F32), sds((vocab, wide), F32)]
        + [sds((wide,), F32)] * WIDE_VECTORS
        + [sds((narrow,), F32)] * NARROW_VECTORS,
        [pltpu.VMEM((LANES, LANES), F32)],
        name="end_a",
    )
    in_share, head_share, g1, b1, bo, bi, g2, b2, bc, g3, b3 = ended
    masked_total = seqs * dp * mask_positions.shape[1]
    return (
        block_out.reshape(seqs, length, width),
        input_grad.reshape(seqs, length, width),
        g1,
        b1,
        in_share,
        bi,
        g2,
        b2,
        jnp.transpose(conv_share, (1, 0, 2)),
        bc,
        g3,
        b3,
        out_share,
        bo,
        head_share.T,
        sums[2, :vocab],
        sums[0, :vocab].astype(jnp.int32),
        sums[1, :vocab],
        sums[3, 0] / masked_total,
    )


def solution(mesh):
    both = P(("dp", "seq"))
    matrix = P(("dp", "seq"), None)
    cube = P(("dp", "seq"), None, None)
    rows = P("dp", "seq", None)
    return jax.shard_map(
        shards,
        mesh=mesh,
        in_specs=(rows, both, both, matrix, both, both, both, cube, both, both, both, matrix)
        + (both, matrix, P(), P("dp", "seq"), P("dp", None), P("dp", None)),
        out_specs=(rows, rows, both, both, matrix, both, both, both, cube, both, both, both)
        + (matrix, both, matrix, P(), P(), P(), P()),
        check_vma=False,
    )
```

```python
import functools

import jax
import jax.numpy as jnp
from jax import lax
from jax.experimental import pallas as pl
from jax.experimental.pallas import tpu as pltpu
from jax.sharding import PartitionSpec as P

KERNEL_TAPS = 5
CENTRE = KERNEL_TAPS // 2
DILATION_RATE = 128
NORM_EPSILON = 1e-05
LOSS_SCALE = 16.0
REACH = CENTRE * DILATION_RATE
BF = jnp.bfloat16
F32 = jnp.float32
LANES = 128
WIDE_VECTORS = 3
NARROW_VECTORS = 6
MIB = 1024 * 1024
HALF_ROOT = 0.7071067811865476
INV_ROOT_TWO_PI = 0.3989422804014327


def gauss(u):
    z = jnp.abs(u) * HALF_ROOT
    t = pl.reciprocal(1.0 + 0.3275911 * z, approx=False)
    e = jnp.exp(-0.5 * u * u)
    poly = t * (
        0.254829592
        + t * (-0.284496736 + t * (1.421413741 + t * (-1.453152027 + t * 1.061405429)))
    )
    tail = 0.5 * poly * e
    return jnp.where(u < 0, tail, 1.0 - tail), e * INV_ROOT_TWO_PI


def standardize(v):
    average = jnp.mean(v, axis=-1, keepdims=True)
    centred = v - average
    spread = jnp.mean(centred * centred, axis=-1, keepdims=True)
    r = lax.rsqrt(spread + NORM_EPSILON)
    return centred * r, r


def dot(a, b):
    return jnp.dot(a, b, preferred_element_type=F32)


def dot_nt(a, b):
    return lax.dot_general(a, b, (((1,), (1,)), ((), ())), preferred_element_type=F32)


def dot_tn(a, b):
    return lax.dot_general(a, b, (((0,), (0,)), ((), ())), preferred_element_type=F32)


def rows8(x):
    return jnp.sum(x.reshape(x.shape[0] // 8, 8, x.shape[1]), axis=0)


def each_chunk(count, step, body):
    @pl.loop(0, count // step)
    def _(i):
        body(pl.ds(pl.multiple_of(i * step, step), step))


def thirds(x):
    high = x.astype(BF)
    rest = x - high.astype(F32)
    mid = rest.astype(BF)
    low = (rest - mid.astype(F32)).astype(BF)
    return high, mid, low


def by_mask(values, me):
    bit = 1
    while bit < len(values):
        here = (me & bit) != 0
        values = [jnp.where(here, values[m ^ bit], values[m]) for m in range(len(values))]
        bit *= 2
    return values


def vmem(n):
    return [pl.BlockSpec(memory_space=pltpu.VMEM)] * n


def call(kernel, ins, outs, scratch=(), us=1, limit=12, name=None, after=(), free=0):
    count = len(ins)
    skipped = len(after)

    def body(*refs):
        kernel(*refs[:count], *refs[count + skipped :])

    return pl.pallas_call(
        body,
        out_shape=list(outs),
        in_specs=[pl.BlockSpec(memory_space=pltpu.HBM)] * free
        + vmem(count - free)
        + [pl.BlockSpec(memory_space=pl.ANY)] * skipped,
        out_specs=vmem(len(outs)),
        scratch_shapes=list(scratch),
        compiler_params=pltpu.CompilerParams(vmem_limit_bytes=limit * MIB),
        cost_estimate=pl.CostEstimate(flops=int(us * 1e9), bytes_accessed=1000, transcendentals=0),
        name=name,
    )(*ins, *after)


def sds(shape, dtype):
    return jax.ShapeDtypeStruct(shape, dtype)


def fetch(sources, targets, sems):
    copies = [
        pltpu.make_async_copy(source, target, sems.at[j])
        for j, (source, target) in enumerate(zip(sources, targets))
    ]
    for copy in copies:
        copy.start()
    for copy in copies:
        copy.wait()


def pack_a_kernel(vocab, *refs):
    count = 2 + WIDE_VECTORS + NARROW_VECTORS
    group, tile, sems = refs[count : count + 3]
    held = refs[count + 3 :]
    fetch(refs[:count], held, sems)
    w_in, head_t, vecs = held[0], held[1], held[2:]
    wide, inner = w_in.shape
    tile[...] = jnp.zeros_like(tile)
    tile[0:vocab, 0:wide] = head_t[...].astype(F32)
    for j, v in enumerate(vecs):
        n = v.shape[-1]
        tile[vocab + j : vocab + j + 1, 0:n] = v[...].astype(F32).reshape(1, n)
    group[:, 0:inner] = w_in[...]
    group[:, inner : inner + LANES] = jnp.transpose(tile[...])[0:wide].astype(BF)


def pack_b_kernel(conv, w_out, group, sems, conv_held, out_held):
    fetch((conv, w_out), (conv_held, out_held), sems)
    inner = group.shape[2]
    group[0:KERNEL_TAPS] = conv_held[...]
    for h in range(w_out.shape[1] // inner):
        group[KERNEL_TAPS + h] = out_held[:, h * inner : (h + 1) * inner]


def place_kernel(axis, n, *refs):
    parts, out = refs[:n], refs[n]
    me = lax.axis_index(axis)
    values = [p[...].astype(F32) for p in parts]
    ordered = []
    for place in range(n):
        value = values[0]
        for k in range(1, n):
            value = jnp.where(lax.rem(me - place + n, n) == k, values[k], value)
        ordered.append(value)
    out[...] = jnp.concatenate(ordered, axis=-2).astype(BF)


def first_kernel(tokens, n1, r1):
    width = tokens.shape[1]

    def body(c):
        n, r = standardize(tokens[c, :].astype(F32))
        n1[c, :] = n
        r1[c, :] = jnp.broadcast_to(r, (r.shape[0], LANES))

    each_chunk(tokens.shape[0], 16, body)


def spread_matrix(width, inner, wide, narrow):
    row = lax.broadcasted_iota(jnp.int32, (width, 1), 0)
    device = row // wide
    r = row - device * wide
    at = jnp.where(r < narrow, device * narrow + r, -1)
    return (lax.broadcasted_iota(jnp.int32, (width, inner), 1) == at).astype(F32).astype(BF)


def second_kernel(chips, vocab, wide, narrow, n1, *refs):
    pieces = refs[: 2 * chips]
    (w_in, extras, wide_v, narrow_v, act, gp1, n2, gp2, r2, conv_in, proj) = refs[2 * chips :]
    width, inner = w_in.shape
    rows = n1.shape[0]
    me = lax.axis_index("dp")
    block = pieces[0].shape[0]
    for c in range(2):
        for m in range(chips):
            at = pl.multiple_of((me ^ (2 * m + c)) * block, block)
            w_in[pl.ds(at, block), :] = pieces[c * chips + m][:, 0:inner]
            extras[pl.ds(at, block), :] = pieces[c * chips + m][:, inner : inner + LANES]
    turned = jnp.transpose(extras[...].astype(F32))
    wide_v[...] = jnp.zeros_like(wide_v)
    wide_v[0:WIDE_VECTORS, :] = turned[vocab : vocab + WIDE_VECTORS]
    first = vocab + WIDE_VECTORS
    narrow_v[0:NARROW_VECTORS, :] = dot(
        turned.astype(BF), spread_matrix(width, inner, wide, narrow)
    )[first : first + NARROW_VECTORS]
    g1, b1 = wide_v[0:1, :], wide_v[1:2, :]
    bias, g2, b2 = narrow_v[0:1, :], narrow_v[1:2, :], narrow_v[2:3, :]

    def body(c):
        u = n1[c, :] * g1 + b1
        cdf, pdf = gauss(u)
        act[c, :] = (u * cdf).astype(BF)
        gp1[c, :] = cdf + u * pdf

    each_chunk(rows, 16, body)
    proj[...] = dot(act[...], w_in[...])

    def later(c):
        n, r = standardize(proj[c, :] + bias)
        u = n * g2 + b2
        cdf, pdf = gauss(u)
        conv_in[c, :] = (u * cdf).astype(BF)
        gp2[c, :] = cdf + u * pdf
        n2[c, :] = n
        r2[c, :] = jnp.broadcast_to(r, (r.shape[0], LANES))

    each_chunk(rows, 32, later)


def middle_kernel(
    chips,
    hops,
    seqs,
    vocab,
    wide_v,
    narrow_v,
    extras,
    head_bias,
    types,
    positions,
    targets,
    tokens,
    *refs,
):
    blocks = refs[: 2 * hops + 1]
    pieces = refs[2 * hops + 1 : 2 * hops + 1 + 2 * chips]
    (
        taps,
        block_out,
        third_act,
        out_low,
        logit_grad,
        head_grad,
        conv_low,
        narrow_sums,
        wide_sums,
        stats,
        ext,
        n3,
        gp3,
        r3,
        work,
    ) = refs[2 * hops + 1 + 2 * chips :]
    inner = taps.shape[1]
    width = tokens.shape[1]
    rows = tokens.shape[0]
    length = rows // seqs
    me = lax.axis_index("dp")
    block = pieces[0].shape[1]
    for c in range(2):
        for m in range(chips):
            at = pl.multiple_of((me ^ (2 * m + c)) * block, block)
            for slab in range(taps.shape[0]):
                taps[slab, pl.ds(at, block), :] = pieces[c * chips + m][slab]
    for b, ref in enumerate(blocks):
        ext[:, b * length : (b + 1) * length, :] = ref[...]
    bias, g3, b3 = narrow_v[3:4, :], narrow_v[4:5, :], narrow_v[5:6, :]
    bias_out = wide_v[2:3, :]
    narrow_sums[...] = jnp.zeros_like(narrow_sums)
    wide_sums[...] = jnp.zeros_like(wide_sums)
    stats[...] = jnp.zeros_like(stats)
    head_grad[...] = jnp.zeros_like(head_grad)
    seat = lax.axis_index("seq")

    @pl.loop(0, seqs)
    def _(s):
        whole = pl.ds(pl.multiple_of(s * length, length), length)
        total = dot(ext[s, pl.ds(hops * length - REACH, length), :], taps[0])
        for k in range(1, KERNEL_TAPS):
            at = hops * length + (k - CENTRE) * DILATION_RATE
            total += dot(ext[s, pl.ds(at, length), :], taps[k])
        work[:, 0:inner] = total

        def ahead(c):
            low = (work[c, 0:inner] + bias).astype(BF).astype(F32)
            n, r = standardize(low)
            u = n * g3 + b3
            cdf, pdf = gauss(u)
            here = pl.ds(pl.multiple_of(s * length + c.start, c.size), c.size)
            third_act[here, :] = (u * cdf).astype(BF)
            gp3[c, :] = cdf + u * pdf
            n3[c, :] = n
            r3[c, :] = jnp.broadcast_to(r, (r.shape[0], LANES))

        each_chunk(length, 32, ahead)
        for h in range(width // inner):
            work[:, h * inner : (h + 1) * inner] = dot(third_act[whole, :], taps[KERNEL_TAPS + h])

        def add(c):
            here = pl.ds(pl.multiple_of(s * length + c.start, c.size), c.size)
            block_out[here, :] = (tokens[here, :].astype(F32) + work[c, :] + bias_out).astype(BF)

        each_chunk(length, 32, add)
        lane = lax.broadcasted_iota(jnp.int32, (length, LANES), 1)
        logits = dot(block_out[whole, :], extras[...]) + head_bias[...]
        logits = jnp.where(lane < vocab, logits, -1e30)
        highest = jnp.max(logits, axis=1, keepdims=True)
        raised = jnp.exp(logits - highest)
        log_total = highest + jnp.log(jnp.sum(raised, axis=1, keepdims=True))
        place = lax.broadcasted_iota(jnp.int32, (length, positions.shape[1]), 0) + seat * length
        matches = positions[pl.ds(s, 1), :] == place
        mask = jnp.sum(jnp.where(matches, 1.0, 0.0), axis=1, keepdims=True)
        goal = jnp.sum(
            jnp.where(matches, targets[pl.ds(s, 1), :].astype(F32), 0.0), axis=1, keepdims=True
        )
        hot = jnp.where(lane == goal.astype(jnp.int32), 1.0, 0.0)
        picked = jnp.sum(logits * hot, axis=1, keepdims=True)
        entropy = log_total - picked
        chance = jnp.exp(picked - log_total)
        grad = (LOSS_SCALE * mask * (jnp.exp(logits - log_total) - hot)).astype(BF)
        logit_grad[whole, :] = grad
        columns = jnp.where(lane == 0, mask, jnp.where(lane == 1, mask * chance, 0.0))
        kinds = lax.broadcasted_iota(jnp.int32, (LANES, length), 0) == types[pl.ds(s, 1), :]
        tallies = jnp.dot(
            jnp.where(kinds, 1.0, 0.0),
            columns,
            preferred_element_type=F32,
            precision=lax.Precision.HIGHEST,
        )
        stats[0:2, :] += jnp.transpose(tallies)[0:2]
        stats[2:3, :] += jnp.sum(grad.astype(F32), axis=0, keepdims=True)
        stats[3:4, :] += jnp.broadcast_to(
            jnp.sum(mask * entropy, axis=0, keepdims=True), (1, LANES)
        )
        head_grad[...] += dot_tn(block_out[whole, :], grad)
        work[...] = dot_nt(grad, extras[...])

        def lower(c):
            here = pl.ds(pl.multiple_of(s * length + c.start, c.size), c.size)
            low = work[c, :].astype(BF)
            out_low[here, :] = low
            wide_sums[...] += rows8(low.astype(F32))

        each_chunk(length, 32, lower)
        back = dot_nt(out_low[whole, 0:inner], taps[KERNEL_TAPS])
        for h in range(1, width // inner):
            back += dot_nt(out_low[whole, h * inner : (h + 1) * inner], taps[KERNEL_TAPS + h])
        work[:, 0:inner] = back

        def behind(c):
            e = work[c, 0:inner] * gp3[c, :]
            n = n3[c, :]
            narrow_sums[0:8, :] += rows8(e * n)
            narrow_sums[8:16, :] += rows8(e)
            eg = e * g3
            mean_e = jnp.mean(eg, axis=1, keepdims=True)
            mean_en = jnp.mean(eg * n, axis=1, keepdims=True)
            low = (r3[c, 0:1] * (eg - mean_e - n * mean_en)).astype(BF)
            here = pl.ds(pl.multiple_of(s * length + c.start, c.size), c.size)
            conv_low[here, :] = low
            narrow_sums[16:24, :] += rows8(low.astype(F32))

        each_chunk(length, 32, behind)


def conv_grad_kernel(
    chips,
    hops,
    seqs,
    third_own,
    third_other,
    low_own,
    low_other,
    out_low,
    logit_other,
    extras,
    stats,
    stats_other,
    *refs,
):
    count = 2 * hops + 1
    blocks = (refs[:count], refs[count : 2 * count])
    own, own_stats = refs[2 * count : 2 * count + 2]
    sends = refs[2 * count + 2 : 2 * count + 1 + chips]
    turned, turn, third_t, out_other = refs[2 * count + 1 + chips :]
    slabs, block, inner = own.shape
    length = low_own.shape[0] // seqs
    me = lax.axis_index("dp") // 2
    core = lax.axis_index("dp") & 1
    total_stats = stats[...] + stats_other[...]
    own_stats[...] = total_stats
    for send in sends:
        send[slabs * block : slabs * block + 16, :] = jnp.zeros((16, inner), BF)
        for j, term in enumerate(thirds(total_stats)):
            send[slabs * block : slabs * block + 8, j * LANES : (j + 1) * LANES] = term

    def chosen(ref, q):
        even = ref[2 * q * block : (2 * q + 1) * block, :]
        odd = ref[(2 * q + 1) * block : (2 * q + 2) * block, :]
        return jnp.where(core == 1, odd, even)

    for side in range(2):
        for s in range(seqs):
            for b, ref in enumerate(blocks[side]):
                turn[...] = jnp.transpose(ref[s])
                for q in range(chips):
                    turned[
                        side * seqs + s,
                        q * block : (q + 1) * block,
                        b * length : (b + 1) * length,
                    ] = chosen(turn, q)
        for s in range(seqs):
            columns = slice(s * length, (s + 1) * length)
            turn[...] = jnp.transpose((third_own, third_other)[side][columns, :])
            for q in range(chips):
                third_t[side, q * block : (q + 1) * block, columns] = chosen(turn, q)
    out_other[...] = dot_nt(logit_other[...], extras[...]).astype(BF)

    def share(slab, value):
        parts = by_mask([value[q * block : (q + 1) * block] for q in range(chips)], me)
        own[slab] = parts[0]
        for m in range(1, chips):
            sends[m - 1][slab * block : (slab + 1) * block, :] = parts[m].astype(BF)

    for k in range(KERNEL_TAPS):
        at = hops * length + (k - CENTRE) * DILATION_RATE
        value = 0.0
        for side, low in enumerate((low_own, low_other)):
            for s in range(seqs):
                value = value + dot(
                    turned[side * seqs + s, :, at : at + length],
                    low[s * length : (s + 1) * length, :],
                )
        share(k, value)
    for h in range(slabs - KERNEL_TAPS):
        columns = slice(h * inner, (h + 1) * inner)
        share(
            KERNEL_TAPS + h,
            dot(third_t[0], out_low[:, columns]) + dot(third_t[1], out_other[:, columns]),
        )


def sum_terms(ref_value):
    return (
        ref_value[0:8, 0:LANES].astype(F32)
        + ref_value[0:8, LANES : 2 * LANES].astype(F32)
        + ref_value[0:8, 2 * LANES : 3 * LANES].astype(F32)
    )


def line_b_kernel(count, size, part, own, stats, *refs):
    parts = refs[:count]
    keep, keep_stats = refs[count : count + 2]
    sends = refs[count + 2 :]
    slabs, block, inner = own.shape
    me = lax.axis_index("seq")
    sums = stats[...]
    for p in parts:
        sums += sum_terms(p[slabs * block : slabs * block + 16, :])
    keep_stats[...] = sums
    for send in sends:
        send[slabs] = jnp.zeros(send.shape[1:], BF)
        for j, term in enumerate(thirds(sums)):
            send[slabs, 0:8, j * LANES : (j + 1) * LANES] = term
    for slab in range(slabs):
        value = own[slab]
        for p in parts:
            value += p[slab * block : (slab + 1) * block, :].astype(F32)
        cut = [value[z * part : (z + 1) * part] for z in range(size)]
        for k in range(size):
            piece = cut[0]
            for z in range(1, size):
                piece = jnp.where(lax.rem(me + k, size) == z, cut[z], piece)
            if k == 0:
                keep[slab] = piece
            else:
                sends[k - 1][slab, 0:part, :] = piece.astype(BF)


def end_b_kernel(count, keep, stats, *refs):
    parts = refs[:count]
    conv, out, sums, = refs[count:]
    slabs, part, inner = keep.shape
    total = stats[...]
    for p in parts:
        total += sum_terms(p[slabs])
    sums[...] = total
    for slab in range(slabs):
        value = keep[slab]
        for p in parts:
            value += p[slab, 0:part, :].astype(F32)
        if slab < KERNEL_TAPS:
            conv[slab] = value
        else:
            out[:, (slab - KERNEL_TAPS) * inner : (slab - KERNEL_TAPS + 1) * inner] = value


def split_a_kernel(chips, keep, got, own, token, *sends):
    token[...] = jnp.zeros_like(token)
    me = lax.axis_index("dp") // 2
    own[...] = keep[me] + got[me].astype(F32)
    for m in range(1, chips):
        sends[m - 1][...] = (keep[me ^ m] + got[me ^ m].astype(F32)).astype(BF)


def line_a_kernel(count, size, part, own, *refs):
    parts = refs[:count]
    keep = refs[count]
    sends = refs[count + 1 :]
    me = lax.axis_index("seq")
    value = own[...]
    for p in parts:
        value += p[...].astype(F32)
    cut = [value[z * part : (z + 1) * part] for z in range(size)]
    for k in range(size):
        piece = cut[0]
        for z in range(1, size):
            piece = jnp.where(lax.rem(me + k, size) == z, cut[z], piece)
        if k == 0:
            keep[...] = piece
        else:
            sends[k - 1][...] = piece.astype(BF)


def end_a_kernel(count, vocab, keep, *refs):
    parts = refs[:count]
    w_in, head_t = refs[count : count + 2]
    vecs = refs[count + 2 : count + 2 + WIDE_VECTORS + NARROW_VECTORS]
    (tile,) = refs[count + 2 + WIDE_VECTORS + NARROW_VECTORS :]
    wide, inner = w_in.shape
    value = keep[...]
    for p in parts:
        value += p[...].astype(F32)
    w_in[...] = value[:, 0:inner]
    tile[...] = jnp.zeros_like(tile)
    tile[0:wide, :] = value[:, inner : inner + LANES]
    turned = jnp.transpose(tile[...])
    head_t[...] = turned[0:vocab, 0:wide]
    for j, v in enumerate(vecs):
        n = v.shape[-1]
        v[...] = turned[vocab + j : vocab + j + 1, 0:n].reshape(v.shape)


def back_kernel(
    chips,
    hops,
    seqs,
    vocab,
    wide,
    narrow,
    taps,
    n2,
    gp2,
    r2,
    n1,
    gp1,
    act,
    w_in,
    wide_v,
    narrow_v,
    narrow_sums,
    wide_sums,
    head_grad,
    *refs,
):
    blocks = refs[: 2 * hops + 1]
    keep, send, e1, low, ext, work, act_t, sums1, sums2 = refs[2 * hops + 1 :]
    width, inner = w_in.shape
    rows = low.shape[0]
    length = rows // seqs
    g2 = narrow_v[1:2, :]
    for b, ref in enumerate(blocks):
        ext[:, b * length : (b + 1) * length, :] = ref[...]
    sums1[...] = jnp.zeros_like(sums1)
    sums2[...] = jnp.zeros_like(sums2)

    @pl.loop(0, seqs)
    def _(s):
        whole = pl.ds(pl.multiple_of(s * length, length), length)
        total = dot_nt(ext[s, pl.ds(hops * length + REACH, length), :], taps[0])
        for k in range(1, KERNEL_TAPS):
            at = hops * length - (k - CENTRE) * DILATION_RATE
            total += dot_nt(ext[s, pl.ds(at, length), :], taps[k])
        work[:, 0:inner] = total

        def second(c):
            here = pl.ds(pl.multiple_of(s * length + c.start, c.size), c.size)
            e = work[c, 0:inner].astype(BF).astype(F32) * gp2[here, :]
            n = n2[here, :]
            sums2[0:8, :] += rows8(e * n)
            sums2[8:16, :] += rows8(e)
            eg = e * g2
            mean_e = jnp.mean(eg, axis=1, keepdims=True)
            mean_en = jnp.mean(eg * n, axis=1, keepdims=True)
            value = (r2[here, 0:1] * (eg - mean_e - n * mean_en)).astype(BF)
            low[here, :] = value
            sums2[16:24, :] += rows8(value.astype(F32))

        each_chunk(length, 32, second)
        work[...] = dot_nt(low[whole, :], w_in[...])

        def first(c):
            here = pl.ds(pl.multiple_of(s * length + c.start, c.size), c.size)
            e = work[c, :] * gp1[here, :]
            e1[here, :] = e
            sums1[0:8, :] += rows8(e * n1[here, :])
            sums1[8:16, :] += rows8(e)

        each_chunk(length, 16, first)

    def folded(ref, j):
        return jnp.sum(ref[8 * j : 8 * j + 8, :], axis=0, keepdims=True)

    wides = [folded(sums1, 0), folded(sums1, 1), folded(wide_sums, 0)]
    narrows = [folded(sums2, 2), folded(sums2, 0), folded(sums2, 1)]
    narrows += [folded(narrow_sums, 2), folded(narrow_sums, 0), folded(narrow_sums, 1)]
    row = lax.broadcasted_iota(jnp.int32, (16, inner), 0)
    stacked = jnp.zeros((16, inner), F32)
    for j, v in enumerate(narrows):
        stacked = jnp.where(row == j, v, stacked)
    spread = spread_matrix(width, inner, wide, narrow)
    placed = 0.0
    for term in thirds(stacked):
        placed = placed + dot_nt(term, spread)
    row = lax.broadcasted_iota(jnp.int32, (LANES, width), 0)
    grid = jnp.zeros((LANES, width), F32)
    for j, v in enumerate(wides):
        grid = jnp.where(row == vocab + j, v, grid)
    for j in range(NARROW_VECTORS):
        grid = jnp.where(row == vocab + WIDE_VECTORS + j, placed[j : j + 1, :], grid)
    extra = jnp.transpose(grid) + head_grad[...]
    act_t[...] = jnp.transpose(act[...])
    core = lax.axis_index("dp") & 1
    block = keep.shape[1]
    for q in range(chips):
        for c in range(2):
            d = 2 * q + c
            lines = slice(d * block, (d + 1) * block)
            value = dot(act_t[lines, :], low[...])

            @pl.when(core == c)
            def _():
                keep[q, :, 0:inner] = value
                keep[q, :, inner : inner + LANES] = extra[lines]

            @pl.when(core != c)
            def _():
                send[q, :, 0:inner] = value.astype(BF)
                send[q, :, inner : inner + LANES] = extra[lines].astype(BF)


def input_kernel(e1, n1, r1, wide_v, logit_grad, extras, input_grad, token, work):
    token[...] = jnp.zeros_like(token)
    work[...] = dot_nt(logit_grad[...], extras[...])
    g1 = wide_v[0:1, :]

    def body(c):
        n = n1[c, :]
        eg = e1[c, :] * g1
        mean_e = jnp.mean(eg, axis=1, keepdims=True)
        mean_en = jnp.mean(eg * n, axis=1, keepdims=True)
        input_grad[c, :] = (work[c, :] + r1[c, 0:1] * (eg - mean_e - n * mean_en)).astype(BF)

    each_chunk(e1.shape[0], 16, body)


def swap(value, mask):
    count = lax.axis_size("dp")
    return lax.ppermute(value, "dp", [(i, i ^ mask) for i in range(count)])


def shifted(value, k):
    size = lax.axis_size("seq")
    return lax.ppermute(value, "seq", [(i, (i + k) % size) for i in range(size)])


def line_parts(block):
    return [block] + [shifted(block, k) for k in range(1, lax.axis_size("seq"))]


def chip_pieces(block):
    chips = lax.axis_size("dp") // 2
    own = [block] + [swap(block, 2 * m) for m in range(1, chips)]
    return own + [swap(piece, 1) for piece in own]


def halo(series):
    size = lax.axis_size("seq")
    hops = -(-REACH // series.shape[1])
    before = [
        lax.ppermute(series, "seq", [(i, i + h) for i in range(size - h)])
        for h in range(hops, 0, -1)
    ]
    after = [
        lax.ppermute(series, "seq", [(i + h, i) for i in range(size - h)])
        for h in range(1, hops + 1)
    ]
    return before + [series] + after


def shards(
    tokens,
    first_gain,
    first_bias,
    in_weight,
    in_bias,
    second_gain,
    second_bias,
    conv_weight,
    conv_bias,
    third_gain,
    third_bias,
    out_weight,
    out_bias,
    head_weight,
    head_bias,
    residue_types,
    mask_positions,
    targets,
):
    dp = lax.axis_size("dp")
    size = lax.axis_size("seq")
    chips = dp // 2
    seqs, length, width = tokens.shape
    wide, inner = in_weight.shape
    narrow = out_weight.shape[0]
    vocab = head_weight.shape[1]
    rows = seqs * length
    hops = -(-REACH // length)
    slabs = KERNEL_TAPS + width // inner
    flat = tokens.reshape(rows, width)

    ins = [
        in_weight,
        head_weight.T,
        first_gain,
        first_bias,
        out_bias,
        in_bias,
        second_gain,
        second_bias,
        conv_bias,
        third_gain,
        third_bias,
    ]
    (block_a,) = call(
        functools.partial(pack_a_kernel, vocab),
        ins,
        [sds((wide, inner + LANES), BF)],
        [pltpu.VMEM((LANES, LANES), F32), pltpu.SemaphoreType.DMA((len(ins),))]
        + [pltpu.VMEM(x.shape, BF) for x in ins],
        limit=56,
        name="pack_a",
        free=len(ins),
    )
    parts_a = line_parts(block_a)
    (line_a,) = call(
        functools.partial(place_kernel, "seq", size),
        parts_a,
        [sds((size * wide, inner + LANES), BF)],
        name="line_a",
    )
    ins = [jnp.transpose(conv_weight, (1, 0, 2)), out_weight]
    (block_b,) = call(
        pack_b_kernel,
        ins,
        [sds((slabs, narrow, inner), BF)],
        [pltpu.SemaphoreType.DMA((2,))] + [pltpu.VMEM(x.shape, BF) for x in ins],
        limit=8,
        name="pack_b",
        free=2,
        after=[block_a],
    )
    own_a = [line_a] + [swap(line_a, 2 * m) for m in range(1, chips)]
    parts_b = line_parts(block_b)
    n1, r1 = call(
        first_kernel,
        [flat],
        [sds((rows, width), F32), sds((rows, LANES), F32)],
        us=6,
        limit=8,
        name="first",
        after=[block_b],
    )
    *own_a, _ = lax.optimization_barrier((*own_a, r1))
    pieces_a = list(own_a) + [swap(piece, 1) for piece in own_a]
    (line_b,) = call(
        functools.partial(place_kernel, "seq", size),
        parts_b,
        [sds((slabs, size * narrow, inner), BF)],
        name="line_b",
        after=[r1],
    )
    own_b = [line_b] + [swap(line_b, 2 * m) for m in range(1, chips)]
    w_in, extras, wide_v, narrow_v, act, gp1, n2, gp2, r2, conv_in = call(
        functools.partial(second_kernel, chips, vocab, wide, narrow),
        [n1] + pieces_a,
        [
            sds((width, inner), BF),
            sds((width, LANES), BF),
            sds((8, width), F32),
            sds((8, inner), F32),
            sds((rows, width), BF),
            sds((rows, width), F32),
            sds((rows, inner), F32),
            sds((rows, inner), F32),
            sds((rows, LANES), F32),
            sds((rows, inner), BF),
        ],
        [pltpu.VMEM((rows, inner), F32)],
        us=9,
        limit=16,
        name="second",
        after=[line_b],
    )
    blocks = halo(conv_in.reshape(seqs, length, inner))
    other_line = swap(line_b, 1)
    *chip_b, _, _ = lax.optimization_barrier((*own_b[1:], blocks[0], blocks[-1]))
    pieces_b = [line_b] + list(chip_b) + [other_line] + [swap(piece, 1) for piece in chip_b]
    other_blocks = [swap(piece, 1) for piece in blocks]
    (
        taps,
        block_out,
        third_act,
        out_low,
        logit_grad,
        head_grad,
        conv_low,
        narrow_sums,
        wide_sums,
        stats,
    ) = call(
        functools.partial(middle_kernel, chips, hops, seqs, vocab),
        [
            wide_v,
            narrow_v,
            extras,
            jnp.pad(head_bias.astype(F32), (0, LANES - vocab)).reshape(1, LANES),
            residue_types,
            mask_positions,
            targets,
            flat,
        ]
        + blocks
        + pieces_b,
        [
            sds((slabs, inner, inner), BF),
            sds((rows, width), BF),
            sds((rows, inner), BF),
            sds((rows, width), BF),
            sds((rows, LANES), BF),
            sds((width, LANES), F32),
            sds((rows, inner), BF),
            sds((24, inner), F32),
            sds((8, width), F32),
            sds((8, LANES), F32),
        ],
        [
            pltpu.VMEM((seqs, (2 * hops + 1) * length, inner), BF),
            pltpu.VMEM((length, inner), F32),
            pltpu.VMEM((length, inner), F32),
            pltpu.VMEM((length, LANES), F32),
            pltpu.VMEM((length, width), F32),
        ],
        us=17,
        limit=16,
        name="middle",
    )
    grad_blocks = halo(conv_low.reshape(seqs, length, inner))
    low_other = swap(conv_low, 1)
    third_other = swap(third_act, 1)
    logit_other = swap(logit_grad, 1)
    stats_other = swap(stats, 1)
    split_b = call(
        functools.partial(conv_grad_kernel, chips, hops, seqs),
        [third_act, third_other, conv_low, low_other, out_low, logit_other, extras]
        + [stats, stats_other]
        + blocks
        + other_blocks,
        [sds((slabs, size * narrow, inner), F32), sds((8, LANES), F32)]
        + [sds((slabs * size * narrow + 16, inner), BF)] * (chips - 1),
        [
            pltpu.VMEM((2 * seqs, inner // 2, (2 * hops + 1) * length), BF),
            pltpu.VMEM((inner, length), BF),
            pltpu.VMEM((2, inner // 2, rows), BF),
            pltpu.VMEM((rows, width), BF),
        ],
        us=7,
        limit=16,
        name="conv_grad",
    )
    from_chips_b = [swap(piece, 2 * m) for m, piece in zip(range(1, chips), split_b[2:])]
    keep_a, send_a, e1 = call(
        functools.partial(back_kernel, chips, hops, seqs, vocab, wide, narrow),
        [taps, n2, gp2, r2, n1, gp1, act, w_in, wide_v, narrow_v]
        + [narrow_sums, wide_sums, head_grad]
        + grad_blocks,
        [
            sds((chips, size * wide, inner + LANES), F32),
            sds((chips, size * wide, inner + LANES), BF),
            sds((rows, width), F32),
        ],
        [
            pltpu.VMEM((rows, inner), BF),
            pltpu.VMEM((seqs, (2 * hops + 1) * length, inner), BF),
            pltpu.VMEM((length, width), F32),
            pltpu.VMEM((width, rows), BF),
            pltpu.VMEM((16, width), F32),
            pltpu.VMEM((24, inner), F32),
        ],
        us=12,
        limit=20,
        name="back",
        after=[split_b[1]],
    )
    line_b2 = call(
        functools.partial(line_b_kernel, chips - 1, size, narrow),
        [split_b[0], split_b[1]] + from_chips_b,
        [sds((slabs, narrow, inner), F32), sds((8, LANES), F32)]
        + [sds((slabs + 1, max(narrow, 8), inner), BF)] * (size - 1),
        name="line_grad_b",
    )
    send_a, _ = lax.optimization_barrier((send_a, line_b2[1]))
    got_a = swap(send_a, 1)
    split = call(
        functools.partial(split_a_kernel, chips),
        [keep_a, got_a],
        [sds((size * wide, inner + LANES), F32), sds((8, LANES), F32)]
        + [sds((size * wide, inner + LANES), BF)] * (chips - 1),
        name="split_a",
        after=[line_b2[1]],
    )
    from_chips = [swap(piece, 2 * m) for m, piece in zip(range(1, chips), split[2:])]
    from_line_b = [shifted(piece, k) for k, piece in zip(range(1, size), line_b2[2:])]

    input_grad, input_token = call(
        input_kernel,
        [e1, n1, r1, wide_v, logit_grad, extras],
        [sds((rows, width), BF), sds((8, LANES), F32)],
        [pltpu.VMEM((rows, width), F32)],
        us=5,
        name="input",
        after=[split[1]],
    )
    line = call(
        functools.partial(line_a_kernel, chips - 1, size, wide),
        [split[0]] + from_chips,
        [sds((wide, inner + LANES), F32)] + [sds((wide, inner + LANES), BF)] * (size - 1),
        name="line_grad_a",
        after=[input_token],
    )
    conv_share, out_share, sums = call(
        functools.partial(end_b_kernel, size - 1),
        [line_b2[0], line_b2[1]] + from_line_b,
        [sds((KERNEL_TAPS, narrow, inner), F32), sds((narrow, width), F32), sds((8, LANES), F32)],
        name="end_b",
        after=[line[0]],
    )
    from_line = [shifted(piece, k) for k, piece in zip(range(1, size), line[1:])]
    ended = call(
        functools.partial(end_a_kernel, size - 1, vocab),
        [line[0]] + from_line,
        [sds((wide, inner), F32), sds((vocab, wide), F32)]
        + [sds((wide,), F32)] * WIDE_VECTORS
        + [sds((narrow,), F32)] * NARROW_VECTORS,
        [pltpu.VMEM((LANES, LANES), F32)],
        name="end_a",
    )
    in_share, head_share, g1, b1, bo, bi, g2, b2, bc, g3, b3 = ended
    masked_total = seqs * dp * mask_positions.shape[1]
    return (
        block_out.reshape(seqs, length, width),
        input_grad.reshape(seqs, length, width),
        g1,
        b1,
        in_share,
        bi,
        g2,
        b2,
        jnp.transpose(conv_share, (1, 0, 2)),
        bc,
        g3,
        b3,
        out_share,
        bo,
        head_share.T,
        sums[2, :vocab],
        sums[0, :vocab].astype(jnp.int32),
        sums[1, :vocab],
        sums[3, 0] / masked_total,
    )


def solution(mesh):
    both = P(("dp", "seq"))
    matrix = P(("dp", "seq"), None)
    cube = P(("dp", "seq"), None, None)
    rows = P("dp", "seq", None)
    return jax.shard_map(
        shards,
        mesh=mesh,
        in_specs=(rows, both, both, matrix, both, both, both, cube, both, both, both, matrix)
        + (both, matrix, P(), P("dp", "seq"), P("dp", None), P("dp", None)),
        out_specs=(rows, rows, both, both, matrix, both, both, both, cube, both, both, both)
        + (matrix, both, matrix, P(), P(), P(), P()),
        check_vma=False,
    )
```

```python
import functools

import jax
import jax.numpy as jnp
from jax import lax
from jax.experimental import pallas as pl
from jax.experimental.pallas import tpu as pltpu
from jax.sharding import PartitionSpec as P

KERNEL_TAPS = 5
CENTRE = KERNEL_TAPS // 2
DILATION_RATE = 128
NORM_EPSILON = 1e-05
LOSS_SCALE = 16.0
REACH = CENTRE * DILATION_RATE
BF = jnp.bfloat16
F32 = jnp.float32
LANES = 128
US_S = 0.1
WIDE_VECTORS = 3
NARROW_VECTORS = 6
MIB = 1024 * 1024
HALF_ROOT = 0.7071067811865476
INV_ROOT_TWO_PI = 0.3989422804014327


def gauss(u):
    z = jnp.abs(u) * HALF_ROOT
    t = pl.reciprocal(1.0 + 0.3275911 * z, approx=False)
    e = jnp.exp(-0.5 * u * u)
    poly = t * (
        0.254829592
        + t * (-0.284496736 + t * (1.421413741 + t * (-1.453152027 + t * 1.061405429)))
    )
    tail = 0.5 * poly * e
    return jnp.where(u < 0, tail, 1.0 - tail), e * INV_ROOT_TWO_PI


def standardize(v):
    average = jnp.mean(v, axis=-1, keepdims=True)
    centred = v - average
    spread = jnp.mean(centred * centred, axis=-1, keepdims=True)
    r = lax.rsqrt(spread + NORM_EPSILON)
    return centred * r, r


def dot(a, b):
    return jnp.dot(a, b, preferred_element_type=F32)


def dot_nt(a, b):
    return lax.dot_general(a, b, (((1,), (1,)), ((), ())), preferred_element_type=F32)


def dot_tn(a, b):
    return lax.dot_general(a, b, (((0,), (0,)), ((), ())), preferred_element_type=F32)


def rows8(x):
    return jnp.sum(x.reshape(x.shape[0] // 8, 8, x.shape[1]), axis=0)


def each_chunk(count, step, body):
    @pl.loop(0, count // step, unroll=8 if count // step >= 8 else 4)
    def _(i):
        body(pl.ds(pl.multiple_of(i * step, step), step))


def thirds(x):
    high = x.astype(BF)
    rest = x - high.astype(F32)
    mid = rest.astype(BF)
    low = (rest - mid.astype(F32)).astype(BF)
    return high, mid, low


def by_mask(values, me):
    bit = 1
    while bit < len(values):
        here = (me & bit) != 0
        values = [jnp.where(here, values[m ^ bit], values[m]) for m in range(len(values))]
        bit *= 2
    return values


def by_shift(values, me):
    bit = 1
    n = len(values)
    while bit < n:
        here = (me & bit) != 0
        values = [jnp.where(here, values[(k + bit) % n], values[k]) for k in range(n)]
        bit *= 2
    return values


def of_core(values):
    core = lax.axis_index("dp") & 1
    return [
        jnp.where(core == 1, odd, even) for even, odd in zip(values[0::2], values[1::2])
    ]


def beside(value, count):
    r = value.shape[0] // count
    return jnp.concatenate([value[g * r : (g + 1) * r] for g in range(count)], axis=1)


def below(value):
    count = value.shape[1] // LANES
    return jnp.concatenate([value[:, g * LANES : (g + 1) * LANES] for g in range(count)], axis=0)


def stats_rows(total, inner):
    terms = [term.astype(F32) for term in thirds(total)]
    rest = inner - 3 * LANES
    return jnp.concatenate(terms + ([jnp.zeros((8, rest), F32)] if rest else []), axis=1)


def padded(value, rows):
    gap = rows - value.shape[0]
    if gap == 0:
        return value
    return jnp.concatenate([value, jnp.zeros((gap, value.shape[1]), F32)], axis=0)


def vmem(n):
    return [pl.BlockSpec(memory_space=pltpu.VMEM)] * n


def call(kernel, ins, outs, scratch=(), us=1, limit=12, name=None, after=(), free=0):
    count = len(ins)
    skipped = len(after)

    def body(*refs):
        kernel(*refs[:count], *refs[count + skipped :])

    return pl.pallas_call(
        body,
        out_shape=list(outs),
        in_specs=[pl.BlockSpec(memory_space=pltpu.HBM)] * free
        + vmem(count - free)
        + [pl.BlockSpec(memory_space=pl.ANY)] * skipped,
        out_specs=vmem(len(outs)),
        scratch_shapes=list(scratch),
        compiler_params=pltpu.CompilerParams(vmem_limit_bytes=limit * MIB),
        cost_estimate=pl.CostEstimate(flops=int(us * 1e9), bytes_accessed=1000, transcendentals=0),
        name=name,
    )(*ins, *after)


def sds(shape, dtype):
    return jax.ShapeDtypeStruct(shape, dtype)


def fetch(sources, targets, sems):
    copies = [
        pltpu.make_async_copy(source, target, sems.at[j])
        for j, (source, target) in enumerate(zip(sources, targets))
    ]
    for copy in copies:
        copy.start()
    for copy in copies:
        copy.wait()


def pack_a_kernel(vocab, *refs):
    count = 2 + WIDE_VECTORS + NARROW_VECTORS
    group, tile, sems = refs[count : count + 3]
    held = refs[count + 3 :]
    fetch(refs[:count], held, sems)
    w_in, head_t, vecs = held[0], held[1], held[2:]
    wide, inner = w_in.shape
    tile[...] = jnp.zeros_like(tile)
    tile[0:vocab, 0:wide] = head_t[...].astype(F32)
    for j, v in enumerate(vecs):
        n = v.shape[-1]
        tile[vocab + j : vocab + j + 1, 0:n] = v[...].astype(F32).reshape(1, n)
    group[:, 0:inner] = w_in[...]
    group[:, inner : inner + LANES] = jnp.transpose(tile[...])[0:wide].astype(BF)


def pack_b_kernel(conv, w_out, group, sems, conv_held, out_held):
    fetch((conv, w_out), (conv_held, out_held), sems)
    inner = group.shape[1]
    rows = [conv_held[k].astype(F32) for k in range(KERNEL_TAPS)]
    for h in range(w_out.shape[1] // inner):
        rows.append(out_held[:, h * inner : (h + 1) * inner].astype(F32))
    group[...] = jnp.concatenate(rows, axis=0).astype(BF)


def line_a_kernel(n, *refs):
    parts, out = refs[:n], refs[n]
    ordered = by_shift([parts[-k % n][...].astype(F32) for k in range(n)], -lax.axis_index("seq") % n)
    out[...] = jnp.concatenate(ordered, axis=0).astype(BF)


def line_b_kernel(n, *refs):
    parts, out = refs[:n], refs[n]
    slabs = out.shape[0]
    values = [parts[-k % n][...].astype(F32) for k in range(n)]
    ordered = by_shift(values, -lax.axis_index("seq") % n)
    part = values[0].shape[0] // slabs
    for slab in range(slabs):
        out[slab] = jnp.concatenate(
            [value[slab * part : (slab + 1) * part] for value in ordered], axis=0
        ).astype(BF)


def first_kernel(wide, narrow, tokens, n1, r1, spread):
    spread[...] = spread_matrix(tokens.shape[1], spread.shape[1], wide, narrow)

    def body(c):
        n, r = standardize(tokens[c, :].astype(F32))
        n1[c, :] = n
        r1[c, :] = jnp.broadcast_to(r, (r.shape[0], LANES))

    each_chunk(tokens.shape[0], 16, body)


def spread_matrix(width, inner, wide, narrow):
    row = lax.broadcasted_iota(jnp.int32, (width, 1), 0)
    device = row // wide
    r = row - device * wide
    at = jnp.where(r < narrow, device * narrow + r, -1)
    return (lax.broadcasted_iota(jnp.int32, (width, inner), 1) == at).astype(F32).astype(BF)


def second_kernel(chips, vocab, n1, spread, *refs):
    pieces = refs[: 2 * chips]
    (w_in, extras, wide_v, narrow_v, act, gp1, n2, gp2, r2, conv_in, proj) = refs[2 * chips :]
    width, inner = w_in.shape
    rows = n1.shape[0]
    me = lax.axis_index("dp")
    block = pieces[0].shape[0]
    for c in range(2):
        for m in range(chips):
            at = pl.multiple_of((me ^ (2 * m + c)) * block, block)
            w_in[pl.ds(at, block), :] = pieces[c * chips + m][:, 0:inner]
            extras[pl.ds(at, block), :] = pieces[c * chips + m][:, inner : inner + LANES]
    turned = jnp.transpose(extras[...].astype(F32))
    wide_v[...] = jnp.zeros_like(wide_v)
    wide_v[0:WIDE_VECTORS, :] = turned[vocab : vocab + WIDE_VECTORS]
    first = vocab + WIDE_VECTORS
    narrow_v[0:NARROW_VECTORS, :] = dot(
        turned.astype(BF), spread[...]
    )[first : first + NARROW_VECTORS]
    g1, b1 = wide_v[0:1, :], wide_v[1:2, :]
    bias, g2, b2 = narrow_v[0:1, :], narrow_v[1:2, :], narrow_v[2:3, :]

    def body(c):
        u = n1[c, :] * g1 + b1
        cdf, pdf = gauss(u)
        act[c, :] = (u * cdf).astype(BF)
        gp1[c, :] = cdf + u * pdf

    each_chunk(rows, 16, body)
    proj[...] = dot(act[...], w_in[...])

    def later(c):
        n, r = standardize(proj[c, :] + bias)
        u = n * g2 + b2
        cdf, pdf = gauss(u)
        conv_in[c, :] = (u * cdf).astype(BF)
        gp2[c, :] = cdf + u * pdf
        n2[c, :] = n
        r2[c, :] = jnp.broadcast_to(r, (r.shape[0], LANES))

    each_chunk(rows, 32, later)


def middle_kernel(
    chips,
    hops,
    seqs,
    vocab,
    wide_v,
    narrow_v,
    extras,
    head_bias,
    types,
    positions,
    targets,
    tokens,
    *refs,
):
    blocks = refs[: 2 * hops + 1]
    pieces = refs[2 * hops + 1 : 2 * hops + 1 + 2 * chips]
    (
        taps,
        block_out,
        third_act,
        logit_grad,
        head_grad,
        conv_low,
        narrow_sums,
        stats,
        ext,
        n3,
        gp3,
        r3,
        work,
        product,
    ) = refs[2 * hops + 1 + 2 * chips :]
    inner = taps.shape[1]
    width = tokens.shape[1]
    rows = tokens.shape[0]
    length = rows // seqs
    me = lax.axis_index("dp")
    block = pieces[0].shape[1]
    for c in range(2):
        for m in range(chips):
            at = pl.multiple_of((me ^ (2 * m + c)) * block, block)
            for slab in range(taps.shape[0]):
                taps[slab, pl.ds(at, block), :] = pieces[c * chips + m][slab]
    for b, ref in enumerate(blocks):
        ext[:, b * length : (b + 1) * length, :] = ref[...]
    bias, g3, b3 = narrow_v[3:4, :], narrow_v[4:5, :], narrow_v[5:6, :]
    bias_out = wide_v[2:3, :]
    narrow_sums[...] = jnp.zeros_like(narrow_sums)
    value = dot(taps[KERNEL_TAPS], extras[0:inner, :])
    for h in range(1, width // inner):
        value += dot(taps[KERNEL_TAPS + h], extras[h * inner : (h + 1) * inner, :])
    product[:, 0:LANES] = value.astype(BF)
    product[:, LANES : 2 * LANES] = (value - value.astype(BF).astype(F32)).astype(BF)
    stats[...] = jnp.zeros_like(stats)
    head_grad[...] = jnp.zeros_like(head_grad)
    seat = lax.axis_index("seq")

    @pl.loop(0, seqs)
    def _(s):
        whole = pl.ds(pl.multiple_of(s * length, length), length)
        total = dot(ext[s, pl.ds(hops * length - REACH, length), :], taps[0])
        for k in range(1, KERNEL_TAPS):
            at = hops * length + (k - CENTRE) * DILATION_RATE
            total += dot(ext[s, pl.ds(at, length), :], taps[k])
        work[:, 0:inner] = total

        def ahead(c):
            low = (work[c, 0:inner] + bias).astype(BF).astype(F32)
            n, r = standardize(low)
            u = n * g3 + b3
            cdf, pdf = gauss(u)
            here = pl.ds(pl.multiple_of(s * length + c.start, c.size), c.size)
            third_act[here, :] = (u * cdf).astype(BF)
            gp3[c, :] = cdf + u * pdf
            n3[c, :] = n
            r3[c, :] = jnp.broadcast_to(r, (r.shape[0], LANES))

        each_chunk(length, 32, ahead)
        for h in range(width // inner):
            work[:, h * inner : (h + 1) * inner] = dot(third_act[whole, :], taps[KERNEL_TAPS + h])

        def add(c):
            here = pl.ds(pl.multiple_of(s * length + c.start, c.size), c.size)
            block_out[here, :] = (tokens[here, :].astype(F32) + work[c, :] + bias_out).astype(BF)

        each_chunk(length, 32, add)
        lane = lax.broadcasted_iota(jnp.int32, (length, LANES), 1)
        logits = dot(block_out[whole, :], extras[...]) + head_bias[...]
        logits = jnp.where(lane < vocab, logits, -1e30)
        highest = jnp.max(logits, axis=1, keepdims=True)
        raised = jnp.exp(logits - highest)
        log_total = highest + jnp.log(jnp.sum(raised, axis=1, keepdims=True))
        place = lax.broadcasted_iota(jnp.int32, (length, positions.shape[1]), 0) + seat * length
        matches = positions[pl.ds(s, 1), :] == place
        mask = jnp.sum(jnp.where(matches, 1.0, 0.0), axis=1, keepdims=True)
        goal = jnp.sum(
            jnp.where(matches, targets[pl.ds(s, 1), :].astype(F32), 0.0), axis=1, keepdims=True
        )
        hot = jnp.where(lane == goal.astype(jnp.int32), 1.0, 0.0)
        picked = jnp.sum(logits * hot, axis=1, keepdims=True)
        entropy = log_total - picked
        chance = jnp.exp(picked - log_total)
        grad = (LOSS_SCALE * mask * (jnp.exp(logits - log_total) - hot)).astype(BF)
        logit_grad[whole, :] = grad
        columns = jnp.where(lane == 0, mask, jnp.where(lane == 1, mask * chance, 0.0))
        kinds = lax.broadcasted_iota(jnp.int32, (LANES, length), 0) == types[pl.ds(s, 1), :]
        tallies = jnp.dot(
            jnp.where(kinds, 1.0, 0.0),
            columns,
            preferred_element_type=F32,
            precision=lax.Precision.HIGHEST,
        )
        stats[0:2, :] += jnp.transpose(tallies)[0:2]
        stats[2:3, :] += jnp.sum(grad.astype(F32), axis=0, keepdims=True)
        stats[3:4, :] += jnp.broadcast_to(
            jnp.sum(mask * entropy, axis=0, keepdims=True), (1, LANES)
        )
        head_grad[...] += dot_tn(block_out[whole, :], grad)
        work[:, 0:inner] = dot_nt(jnp.concatenate([grad, grad], axis=1), product[...])

        def behind(c):
            e = work[c, 0:inner] * gp3[c, :]
            n = n3[c, :]
            narrow_sums[0:8, :] += rows8(e * n)
            narrow_sums[8:16, :] += rows8(e)
            eg = e * g3
            mean_e = jnp.mean(eg, axis=1, keepdims=True)
            mean_en = jnp.mean(eg * n, axis=1, keepdims=True)
            low = (r3[c, 0:1] * (eg - mean_e - n * mean_en)).astype(BF)
            here = pl.ds(pl.multiple_of(s * length + c.start, c.size), c.size)
            conv_low[here, :] = low
            narrow_sums[16:24, :] += rows8(low.astype(F32))

        each_chunk(length, 32, behind)


def conv_grad_kernel(
    chips,
    hops,
    seqs,
    third_own,
    third_other,
    low_own,
    low_other,
    logit_own,
    logit_other,
    stats,
    stats_other,
    *refs,
):
    count = 2 * hops + 1
    blocks = (refs[:count], refs[count : 2 * count])
    own, own_stats, own_out = refs[2 * count : 2 * count + 3]
    sends = refs[2 * count + 3 : 2 * count + 2 + chips]
    turned, turn, third_t = refs[2 * count + 2 + chips :]
    slabs, block, inner = own.shape
    length = low_own.shape[0] // seqs
    me = lax.axis_index("dp") // 2
    core = lax.axis_index("dp") & 1
    total_stats = stats[...] + stats_other[...]
    own_stats[...] = total_stats
    tail = jnp.concatenate([stats_rows(total_stats, inner), jnp.zeros((8, inner), F32)], axis=0)
    for send in sends:
        send[send.shape[0] - 16 :, :] = tail.astype(BF)

    def chosen(ref, q):
        even = ref[2 * q * block : (2 * q + 1) * block, :]
        odd = ref[(2 * q + 1) * block : (2 * q + 2) * block, :]
        return jnp.where(core == 1, odd, even)

    for side in range(2):
        for s in range(seqs):
            for b, ref in enumerate(blocks[side]):
                turn[...] = jnp.transpose(ref[s])
                for q in range(chips):
                    turned[
                        side * seqs + s,
                        q * block : (q + 1) * block,
                        b * length : (b + 1) * length,
                    ] = chosen(turn, q)
        for s in range(seqs):
            columns = slice(s * length, (s + 1) * length)
            turn[...] = jnp.transpose((third_own, third_other)[side][columns, :])
            for q in range(chips):
                third_t[side, q * block : (q + 1) * block, columns] = chosen(turn, q)

    def share(slab, value):
        parts = by_mask([value[q * block : (q + 1) * block] for q in range(chips)], me)
        own[slab] = parts[0]
        for m in range(1, chips):
            sends[m - 1][slab * block : (slab + 1) * block, :] = parts[m].astype(BF)

    for k in range(KERNEL_TAPS):
        at = hops * length + (k - CENTRE) * DILATION_RATE
        value = 0.0
        for side, low in enumerate((low_own, low_other)):
            for s in range(seqs):
                value = value + dot(
                    turned[side * seqs + s, :, at : at + length],
                    low[s * length : (s + 1) * length, :],
                )
        share(k, value)
    value = dot(third_t[0], logit_own[...]) + dot(third_t[1], logit_other[...])
    parts = by_mask([value[q * block : (q + 1) * block] for q in range(chips)], me)
    own_out[...] = parts[0]
    for m in range(1, chips):
        lines = beside(parts[m], inner // LANES)
        sends[m - 1][slabs * block : slabs * block + lines.shape[0], :] = lines.astype(BF)


def sum_terms(ref_value):
    return (
        ref_value[0:8, 0:LANES].astype(F32)
        + ref_value[0:8, LANES : 2 * LANES].astype(F32)
        + ref_value[0:8, 2 * LANES : 3 * LANES].astype(F32)
    )


def line_grad_b_kernel(count, size, part, own, stats, own_out, *refs):
    parts = refs[:count]
    keep, keep_stats, keep_out = refs[count : count + 3]
    sends = refs[count + 3 :]
    slabs, block, inner = own.shape
    me = lax.axis_index("seq")
    rows = parts[0].shape[0]
    sums = stats[...]
    out = own_out[...]
    for p in parts:
        sums += sum_terms(p[rows - 16 :, :])
        out += below(p[slabs * block : rows - 16, :].astype(F32))
    keep_stats[...] = sums
    pieces = [[] for _ in range(size)]
    for slab in range(slabs):
        value = own[slab]
        for p in parts:
            value += p[slab * block : (slab + 1) * block, :].astype(F32)
        cut = by_shift([value[z * part : (z + 1) * part] for z in range(size)], me)
        keep[slab] = cut[0]
        for k in range(1, size):
            pieces[k].append(cut[k])
    cut = by_shift([out[z * part : (z + 1) * part] for z in range(size)], me)
    tail_rows = keep_out.shape[0]
    keep_out[...] = padded(cut[0], tail_rows)
    terms = padded(stats_rows(sums, 3 * LANES), tail_rows)
    gap = sends[0].shape[0] - slabs * part - tail_rows
    for k in range(1, size):
        rest = inner - 4 * LANES
        tail = [terms, padded(cut[k], tail_rows), jnp.zeros((tail_rows, rest), F32)]
        lines = pieces[k] + ([jnp.zeros((gap, inner), F32)] if gap else [])
        lines.append(jnp.concatenate(tail, axis=1))
        sends[k - 1][...] = jnp.concatenate(lines, axis=0).astype(BF)


def end_b_kernel(count, keep, stats, keep_out, extras, *refs):
    parts = refs[:count]
    conv, out, sums = refs[count:]
    slabs, part, inner = keep.shape
    tail_rows = keep_out.shape[0]
    values = [p[...].astype(F32) for p in parts]
    total = stats[...]
    product = keep_out[...]
    for value in values:
        tail = value[value.shape[0] - tail_rows :]
        total += sum_terms(tail)
        product += tail[:, 3 * LANES : 4 * LANES]
    sums[...] = total
    value = 0.0
    for term in thirds(product):
        value = value + dot_nt(term, extras[...])
    out[...] = value[0:part]
    for slab in range(slabs):
        value = keep[slab]
        for v in values:
            value += v[slab * part : (slab + 1) * part]
        conv[slab] = value


def split_a_kernel(chips, keep, got_low, got_high, own, token, *sends):
    token[...] = jnp.zeros_like(token)
    half = chips // 2
    sums = [
        keep[q] + (got_low, got_high)[q // half][q % half].astype(F32) for q in range(chips)
    ]
    sums = by_mask(sums, lax.axis_index("dp") // 2)
    own[...] = sums[0]
    for m in range(1, chips):
        sends[m - 1][...] = sums[m].astype(BF)


def line_grad_a_kernel(count, size, part, own, *refs):
    parts = refs[:count]
    keep = refs[count]
    sends = refs[count + 1 :]
    me = lax.axis_index("seq")
    value = own[...]
    for p in parts:
        value += p[...].astype(F32)
    cut = [value[z * part : (z + 1) * part] for z in range(size)]
    for k in range(size):
        piece = cut[0]
        for z in range(1, size):
            piece = jnp.where(lax.rem(me + k, size) == z, cut[z], piece)
        if k == 0:
            keep[...] = piece
        else:
            sends[k - 1][...] = piece.astype(BF)


def end_a_kernel(count, vocab, keep, *refs):
    parts = refs[:count]
    w_in, head_t = refs[count : count + 2]
    vecs = refs[count + 2 : count + 2 + WIDE_VECTORS + NARROW_VECTORS]
    (tile,) = refs[count + 2 + WIDE_VECTORS + NARROW_VECTORS :]
    wide, inner = w_in.shape
    value = keep[...]
    for p in parts:
        value += p[...].astype(F32)
    w_in[...] = value[:, 0:inner]
    tile[...] = jnp.zeros_like(tile)
    tile[0:wide, :] = value[:, inner : inner + LANES]
    turned = jnp.transpose(tile[...])
    head_t[...] = turned[0:vocab, 0:wide]
    for j, v in enumerate(vecs):
        n = v.shape[-1]
        v[...] = turned[vocab + j : vocab + j + 1, 0:n].reshape(v.shape)


def back_kernel(
    chips,
    hops,
    seqs,
    vocab,
    wide,
    narrow,
    taps,
    n2,
    gp2,
    r2,
    n1,
    gp1,
    act,
    w_in,
    wide_v,
    narrow_v,
    narrow_sums,
    stats,
    extras,
    head_grad,
    *refs,
):
    blocks = refs[: 2 * hops + 1]
    keep, send_low, send_high, e1, low, ext, work, act_t, sums1, sums2 = refs[2 * hops + 1 :]
    half = chips // 2
    width, inner = w_in.shape
    rows = low.shape[0]
    length = rows // seqs
    g2 = narrow_v[1:2, :]
    for b, ref in enumerate(blocks):
        ext[:, b * length : (b + 1) * length, :] = ref[...]
    sums1[...] = jnp.zeros_like(sums1)
    sums2[...] = jnp.zeros_like(sums2)

    @pl.loop(0, seqs)
    def _(s):
        whole = pl.ds(pl.multiple_of(s * length, length), length)
        total = dot_nt(ext[s, pl.ds(hops * length + REACH, length), :], taps[0])
        for k in range(1, KERNEL_TAPS):
            at = hops * length - (k - CENTRE) * DILATION_RATE
            total += dot_nt(ext[s, pl.ds(at, length), :], taps[k])
        work[:, 0:inner] = total

        def second(c):
            here = pl.ds(pl.multiple_of(s * length + c.start, c.size), c.size)
            e = work[c, 0:inner].astype(BF).astype(F32) * gp2[here, :]
            n = n2[here, :]
            sums2[0:8, :] += rows8(e * n)
            sums2[8:16, :] += rows8(e)
            eg = e * g2
            mean_e = jnp.mean(eg, axis=1, keepdims=True)
            mean_en = jnp.mean(eg * n, axis=1, keepdims=True)
            value = (r2[here, 0:1] * (eg - mean_e - n * mean_en)).astype(BF)
            low[here, :] = value
            sums2[16:24, :] += rows8(value.astype(F32))

        each_chunk(length, 32, second)
        work[...] = dot_nt(low[whole, :], w_in[...])

        def first(c):
            here = pl.ds(pl.multiple_of(s * length + c.start, c.size), c.size)
            e = work[c, :] * gp1[here, :]
            e1[here, :] = e
            sums1[0:8, :] += rows8(e * n1[here, :])
            sums1[8:16, :] += rows8(e)

        each_chunk(length, 16, first)

    def folded(ref, j):
        return jnp.sum(ref[8 * j : 8 * j + 8, :], axis=0, keepdims=True)

    bias = 0.0
    for term in thirds(stats[...]):
        bias = bias + dot_nt(term, extras[...])
    wides = [folded(sums1, 0), folded(sums1, 1), bias[2:3, :]]
    narrows = [folded(sums2, 2), folded(sums2, 0), folded(sums2, 1)]
    narrows += [folded(narrow_sums, 2), folded(narrow_sums, 0), folded(narrow_sums, 1)]
    row = lax.broadcasted_iota(jnp.int32, (16, inner), 0)
    stacked = jnp.zeros((16, inner), F32)
    for j, v in enumerate(narrows):
        stacked = jnp.where(row == j, v, stacked)
    spread = spread_matrix(width, inner, wide, narrow)
    placed = 0.0
    for term in thirds(stacked):
        placed = placed + dot_nt(term, spread)
    row = lax.broadcasted_iota(jnp.int32, (LANES, width), 0)
    grid = jnp.zeros((LANES, width), F32)
    for j, v in enumerate(wides):
        grid = jnp.where(row == vocab + j, v, grid)
    for j in range(NARROW_VECTORS):
        grid = jnp.where(row == vocab + WIDE_VECTORS + j, placed[j : j + 1, :], grid)
    extra = jnp.transpose(grid) + head_grad[...]
    act_t[...] = jnp.transpose(act[...])
    core = lax.axis_index("dp") & 1
    block = keep.shape[1]
    for q in range(chips):
        for c in range(2):
            d = 2 * q + c
            lines = slice(d * block, (d + 1) * block)
            value = dot(act_t[lines, :], low[...])

            @pl.when(core == c)
            def _():
                keep[q, :, 0:inner] = value
                keep[q, :, inner : inner + LANES] = extra[lines]

            @pl.when(core != c)
            def _():
                send = (send_low, send_high)[q // half]
                send[q % half, :, 0:inner] = value.astype(BF)
                send[q % half, :, inner : inner + LANES] = extra[lines].astype(BF)


def input_kernel(e1, n1, r1, wide_v, logit_grad, extras, input_grad, token, work):
    token[...] = jnp.zeros_like(token)
    work[...] = dot_nt(logit_grad[...], extras[...])
    g1 = wide_v[0:1, :]

    def body(c):
        n = n1[c, :]
        eg = e1[c, :] * g1
        mean_e = jnp.mean(eg, axis=1, keepdims=True)
        mean_en = jnp.mean(eg * n, axis=1, keepdims=True)
        input_grad[c, :] = (work[c, :] + r1[c, 0:1] * (eg - mean_e - n * mean_en)).astype(BF)

    each_chunk(e1.shape[0], 16, body)


def swap(value, mask):
    count = lax.axis_size("dp")
    return lax.ppermute(value, "dp", [(i, i ^ mask) for i in range(count)])


def shifted(value, k):
    size = lax.axis_size("seq")
    return lax.ppermute(value, "seq", [(i, (i + k) % size) for i in range(size)])


def line_parts(block):
    return [block] + [shifted(block, k) for k in range(1, lax.axis_size("seq"))]


def chip_pieces(block):
    chips = lax.axis_size("dp") // 2
    own = [block] + [swap(block, 2 * m) for m in range(1, chips)]
    return own + [swap(piece, 1) for piece in own]


def halo(series):
    size = lax.axis_size("seq")
    hops = -(-REACH // series.shape[1])
    before = [
        lax.ppermute(series, "seq", [(i, i + h) for i in range(size - h)])
        for h in range(hops, 0, -1)
    ]
    after = [
        lax.ppermute(series, "seq", [(i + h, i) for i in range(size - h)])
        for h in range(1, hops + 1)
    ]
    return before + [series] + after


def shards(
    tokens,
    first_gain,
    first_bias,
    in_weight,
    in_bias,
    second_gain,
    second_bias,
    conv_weight,
    conv_bias,
    third_gain,
    third_bias,
    out_weight,
    out_bias,
    head_weight,
    head_bias,
    residue_types,
    mask_positions,
    targets,
):
    dp = lax.axis_size("dp")
    size = lax.axis_size("seq")
    chips = dp // 2
    seqs, length, width = tokens.shape
    wide, inner = in_weight.shape
    narrow = out_weight.shape[0]
    vocab = head_weight.shape[1]
    rows = seqs * length
    hops = -(-REACH // length)
    slabs = KERNEL_TAPS + width // inner
    flat = tokens.reshape(rows, width)

    ins = [
        in_weight,
        head_weight.T,
        first_gain,
        first_bias,
        out_bias,
        in_bias,
        second_gain,
        second_bias,
        conv_bias,
        third_gain,
        third_bias,
    ]
    (block_a,) = call(
        functools.partial(pack_a_kernel, vocab),
        ins,
        [sds((wide, inner + LANES), BF)],
        [pltpu.VMEM((LANES, LANES), F32), pltpu.SemaphoreType.DMA((len(ins),))]
        + [pltpu.VMEM(x.shape, BF) for x in ins],
        limit=56,
        name="pack_a",
        free=len(ins),
    )
    parts_a = line_parts(block_a)
    (line_a,) = call(
        functools.partial(line_a_kernel, size),
        parts_a,
        [sds((size * wide, inner + LANES), BF)],
        name="line_a",
    )
    ins = [jnp.transpose(conv_weight, (1, 0, 2)), out_weight]
    (block_b,) = call(
        pack_b_kernel,
        ins,
        [sds((slabs * narrow, inner), BF)],
        [pltpu.SemaphoreType.DMA((2,))] + [pltpu.VMEM(x.shape, BF) for x in ins],
        limit=8,
        name="pack_b",
        free=2,
        after=[block_a],
    )
    own_a = [line_a] + [swap(line_a, 2 * m) for m in range(1, chips)]
    parts_b = line_parts(block_b)
    n1, r1, spread = call(
        functools.partial(first_kernel, wide, narrow),
        [flat],
        [sds((rows, width), F32), sds((rows, LANES), F32), sds((width, inner), BF)],
        us=6,
        limit=8,
        name="first",
        after=[block_b],
    )
    *own_a, _ = lax.optimization_barrier((*own_a, r1))
    pieces_a = list(own_a) + [swap(piece, 1) for piece in own_a]
    (line_b,) = call(
        functools.partial(line_b_kernel, size),
        parts_b,
        [sds((slabs, size * narrow, inner), BF)],
        name="line_b",
        after=[r1],
    )
    own_b = [line_b] + [swap(line_b, 2 * m) for m in range(1, chips)]
    w_in, extras, wide_v, narrow_v, act, gp1, n2, gp2, r2, conv_in = call(
        functools.partial(second_kernel, chips, vocab),
        [n1, spread] + pieces_a,
        [
            sds((width, inner), BF),
            sds((width, LANES), BF),
            sds((8, width), F32),
            sds((8, inner), F32),
            sds((rows, width), BF),
            sds((rows, width), F32),
            sds((rows, inner), F32),
            sds((rows, inner), F32),
            sds((rows, LANES), F32),
            sds((rows, inner), BF),
        ],
        [pltpu.VMEM((rows, inner), F32)],
        us=9,
        limit=16,
        name="second",
        after=[line_b],
    )
    blocks = halo(conv_in.reshape(seqs, length, inner))
    other_line = swap(line_b, 1)
    *chip_b, _, _ = lax.optimization_barrier((*own_b[1:], blocks[0], blocks[-1]))
    pieces_b = [line_b] + list(chip_b) + [other_line] + [swap(piece, 1) for piece in chip_b]
    other_blocks = [swap(piece, 1) for piece in blocks]
    (
        taps,
        block_out,
        third_act,
        logit_grad,
        head_grad,
        conv_low,
        narrow_sums,
        stats,
    ) = call(
        functools.partial(middle_kernel, chips, hops, seqs, vocab),
        [
            wide_v,
            narrow_v,
            extras,
            jnp.pad(head_bias.astype(F32), (0, LANES - vocab)).reshape(1, LANES),
            residue_types,
            mask_positions,
            targets,
            flat,
        ]
        + blocks
        + pieces_b,
        [
            sds((slabs, inner, inner), BF),
            sds((rows, width), BF),
            sds((rows, inner), BF),
            sds((rows, LANES), BF),
            sds((width, LANES), F32),
            sds((rows, inner), BF),
            sds((24, inner), F32),
            sds((8, LANES), F32),
        ],
        [
            pltpu.VMEM((seqs, (2 * hops + 1) * length, inner), BF),
            pltpu.VMEM((length, inner), F32),
            pltpu.VMEM((length, inner), F32),
            pltpu.VMEM((length, LANES), F32),
            pltpu.VMEM((length, width), F32),
            pltpu.VMEM((inner, 2 * LANES), BF),
        ],
        us=17,
        limit=16,
        name="middle",
    )
    grad_blocks = halo(conv_low.reshape(seqs, length, inner))
    low_other = swap(conv_low, 1)
    third_other = swap(third_act, 1)
    logit_other = swap(logit_grad, 1)
    stats_other = swap(stats, 1)
    message = KERNEL_TAPS * size * narrow + size * narrow // (inner // LANES) + 16
    split_b = call(
        functools.partial(conv_grad_kernel, chips, hops, seqs),
        [third_act, third_other, conv_low, low_other, logit_grad, logit_other]
        + [stats, stats_other]
        + blocks
        + other_blocks,
        [
            sds((KERNEL_TAPS, size * narrow, inner), F32),
            sds((8, LANES), F32),
            sds((size * narrow, LANES), F32),
        ]
        + [sds((message, inner), BF)] * (chips - 1),
        [
            pltpu.VMEM((2 * seqs, inner // 2, (2 * hops + 1) * length), BF),
            pltpu.VMEM((inner, length), BF),
            pltpu.VMEM((2, inner // 2, rows), BF),
        ],
        us=7,
        limit=16,
        name="conv_grad",
    )
    from_chips_b = [swap(piece, 2 * m) for m, piece in zip(range(1, chips), split_b[3:])]
    keep_a, send_low, send_high, e1 = call(
        functools.partial(back_kernel, chips, hops, seqs, vocab, wide, narrow),
        [taps, n2, gp2, r2, n1, gp1, act, w_in, wide_v, narrow_v]
        + [narrow_sums, stats, extras, head_grad]
        + grad_blocks,
        [
            sds((chips, size * wide, inner + LANES), F32),
            sds((chips // 2, size * wide, inner + LANES), BF),
            sds((chips // 2, size * wide, inner + LANES), BF),
            sds((rows, width), F32),
        ],
        [
            pltpu.VMEM((rows, inner), BF),
            pltpu.VMEM((seqs, (2 * hops + 1) * length, inner), BF),
            pltpu.VMEM((length, width), F32),
            pltpu.VMEM((width, rows), BF),
            pltpu.VMEM((16, width), F32),
            pltpu.VMEM((24, inner), F32),
        ],
        us=US_S,
        limit=20,
        name="back",
        after=[split_b[1]],
    )
    got_low, got_high = swap(send_low, 1), swap(send_high, 1)
    split = call(
        functools.partial(split_a_kernel, chips),
        [keep_a, got_low, got_high],
        [sds((size * wide, inner + LANES), F32), sds((8, LANES), F32)]
        + [sds((size * wide, inner + LANES), BF)] * (chips - 1),
        us=US_S,
        name="split_a",
    )
    tail = -(-max(narrow, 8) // 8) * 8
    line_b2 = call(
        functools.partial(line_grad_b_kernel, chips - 1, size, narrow),
        list(split_b[:3]) + from_chips_b,
        [sds((KERNEL_TAPS, narrow, inner), F32), sds((8, LANES), F32), sds((tail, LANES), F32)]
        + [sds((-(-KERNEL_TAPS * narrow // 8) * 8 + tail, inner), BF)] * (size - 1),
        name="line_grad_b",
        after=[split[1]],
    )
    *a_sends, _ = lax.optimization_barrier((*split[2:], line_b2[1]))
    from_chips = [swap(piece, 2 * m) for m, piece in zip(range(1, chips), a_sends)]

    input_grad, input_token = call(
        input_kernel,
        [e1, n1, r1, wide_v, logit_grad, extras],
        [sds((rows, width), BF), sds((8, LANES), F32)],
        [pltpu.VMEM((rows, width), F32)],
        us=3,
        name="input",
        after=[line_b2[1]],
    )
    from_line_b = [shifted(piece, k) for k, piece in zip(range(1, size), line_b2[3:])]
    line = call(
        functools.partial(line_grad_a_kernel, chips - 1, size, wide),
        [split[0]] + from_chips,
        [sds((wide, inner + LANES), F32)] + [sds((wide, inner + LANES), BF)] * (size - 1),
        name="line_grad_a",
        after=[input_token],
    )
    conv_share, out_share, sums = call(
        functools.partial(end_b_kernel, size - 1),
        [line_b2[0], line_b2[1], line_b2[2], extras] + from_line_b,
        [sds((KERNEL_TAPS, narrow, inner), F32), sds((narrow, width), F32), sds((8, LANES), F32)],
        name="end_b",
        after=[line[0]],
    )
    from_line = [shifted(piece, k) for k, piece in zip(range(1, size), line[1:])]
    ended = call(
        functools.partial(end_a_kernel, size - 1, vocab),
        [line[0]] + from_line,
        [sds((wide, inner), F32), sds((vocab, wide), F32)]
        + [sds((wide,), F32)] * WIDE_VECTORS
        + [sds((narrow,), F32)] * NARROW_VECTORS,
        [pltpu.VMEM((LANES, LANES), F32)],
        name="end_a",
    )
    in_share, head_share, g1, b1, bo, bi, g2, b2, bc, g3, b3 = ended
    masked_total = seqs * dp * mask_positions.shape[1]
    return (
        block_out.reshape(seqs, length, width),
        input_grad.reshape(seqs, length, width),
        g1,
        b1,
        in_share,
        bi,
        g2,
        b2,
        jnp.transpose(conv_share, (1, 0, 2)),
        bc,
        g3,
        b3,
        out_share,
        bo,
        head_share.T,
        sums[2, :vocab],
        sums[0, :vocab].astype(jnp.int32),
        sums[1, :vocab],
        sums[3, 0] / masked_total,
    )


def solution(mesh):
    both = P(("dp", "seq"))
    matrix = P(("dp", "seq"), None)
    cube = P(("dp", "seq"), None, None)
    rows = P("dp", "seq", None)
    return jax.shard_map(
        shards,
        mesh=mesh,
        in_specs=(rows, both, both, matrix, both, both, both, cube, both, both, both, matrix)
        + (both, matrix, P(), P("dp", "seq"), P("dp", None), P("dp", None)),
        out_specs=(rows, rows, both, both, matrix, both, both, both, cube, both, both, both)
        + (matrix, both, matrix, P(), P(), P(), P()),
        check_vma=False,
    )
```

```python
import functools

import jax
import jax.numpy as jnp
from jax import lax
from jax.experimental import pallas as pl
from jax.experimental.pallas import tpu as pltpu
from jax.sharding import PartitionSpec as P

KERNEL_TAPS = 5
CENTRE = KERNEL_TAPS // 2
DILATION_RATE = 128
NORM_EPSILON = 1e-05
LOSS_SCALE = 16.0
REACH = CENTRE * DILATION_RATE
BF = jnp.bfloat16
F32 = jnp.float32
LANES = 128
US_S = 0.1
WIDE_VECTORS = 3
NARROW_VECTORS = 6
MIB = 1024 * 1024
HALF_ROOT = 0.7071067811865476
INV_ROOT_TWO_PI = 0.3989422804014327


def gauss(u):
    z = jnp.abs(u) * HALF_ROOT
    t = pl.reciprocal(1.0 + 0.3275911 * z, approx=False)
    e = jnp.exp(-0.5 * u * u)
    poly = t * (
        0.254829592
        + t * (-0.284496736 + t * (1.421413741 + t * (-1.453152027 + t * 1.061405429)))
    )
    tail = 0.5 * poly * e
    return jnp.where(u < 0, tail, 1.0 - tail), e * INV_ROOT_TWO_PI


def standardize(v):
    average = jnp.mean(v, axis=-1, keepdims=True)
    centred = v - average
    spread = jnp.mean(centred * centred, axis=-1, keepdims=True)
    r = lax.rsqrt(spread + NORM_EPSILON)
    return centred * r, r


def dot(a, b):
    return jnp.dot(a, b, preferred_element_type=F32)


def dot_nt(a, b):
    return lax.dot_general(a, b, (((1,), (1,)), ((), ())), preferred_element_type=F32)


def dot_tn(a, b):
    return lax.dot_general(a, b, (((0,), (0,)), ((), ())), preferred_element_type=F32)


def rows8(x):
    return jnp.sum(x.reshape(x.shape[0] // 8, 8, x.shape[1]), axis=0)


def each_chunk(count, step, body):
    @pl.loop(0, count // step, unroll=8 if count // step >= 8 else 4)
    def _(i):
        body(pl.ds(pl.multiple_of(i * step, step), step))


def thirds(x):
    high = x.astype(BF)
    rest = x - high.astype(F32)
    mid = rest.astype(BF)
    low = (rest - mid.astype(F32)).astype(BF)
    return high, mid, low


def by_mask(values, me):
    bit = 1
    while bit < len(values):
        here = (me & bit) != 0
        values = [jnp.where(here, values[m ^ bit], values[m]) for m in range(len(values))]
        bit *= 2
    return values


def by_shift(values, me):
    bit = 1
    n = len(values)
    while bit < n:
        here = (me & bit) != 0
        values = [jnp.where(here, values[(k + bit) % n], values[k]) for k in range(n)]
        bit *= 2
    return values


def of_core(values):
    core = lax.axis_index("dp") & 1
    return [
        jnp.where(core == 1, odd, even) for even, odd in zip(values[0::2], values[1::2])
    ]


def beside(value, count):
    r = value.shape[0] // count
    return jnp.concatenate([value[g * r : (g + 1) * r] for g in range(count)], axis=1)


def below(value):
    count = value.shape[1] // LANES
    return jnp.concatenate([value[:, g * LANES : (g + 1) * LANES] for g in range(count)], axis=0)


def stats_rows(total, inner):
    terms = [term.astype(F32) for term in thirds(total)]
    rest = inner - 3 * LANES
    return jnp.concatenate(terms + ([jnp.zeros((8, rest), F32)] if rest else []), axis=1)


def padded(value, rows):
    gap = rows - value.shape[0]
    if gap == 0:
        return value
    return jnp.concatenate([value, jnp.zeros((gap, value.shape[1]), F32)], axis=0)


def vmem(n):
    return [pl.BlockSpec(memory_space=pltpu.VMEM)] * n


def call(kernel, ins, outs, scratch=(), us=1, limit=12, name=None, after=(), free=0):
    count = len(ins)
    skipped = len(after)

    def body(*refs):
        kernel(*refs[:count], *refs[count + skipped :])

    return pl.pallas_call(
        body,
        out_shape=list(outs),
        in_specs=[pl.BlockSpec(memory_space=pltpu.HBM)] * free
        + vmem(count - free)
        + [pl.BlockSpec(memory_space=pl.ANY)] * skipped,
        out_specs=vmem(len(outs)),
        scratch_shapes=list(scratch),
        compiler_params=pltpu.CompilerParams(vmem_limit_bytes=limit * MIB),
        cost_estimate=pl.CostEstimate(flops=int(us * 1e9), bytes_accessed=1000, transcendentals=0),
        name=name,
    )(*ins, *after)


def sds(shape, dtype):
    return jax.ShapeDtypeStruct(shape, dtype)


def fetch(sources, targets, sems):
    copies = [
        pltpu.make_async_copy(source, target, sems.at[j])
        for j, (source, target) in enumerate(zip(sources, targets))
    ]
    for copy in copies:
        copy.start()
    for copy in copies:
        copy.wait()


def pack_a_kernel(vocab, *refs):
    count = 2 + WIDE_VECTORS + NARROW_VECTORS
    group, tile, sems = refs[count : count + 3]
    held = refs[count + 3 :]
    fetch(refs[:count], held, sems)
    w_in, head_t, vecs = held[0], held[1], held[2:]
    wide, inner = w_in.shape
    tile[...] = jnp.zeros_like(tile)
    tile[0:vocab, 0:wide] = head_t[...].astype(F32)
    for j, v in enumerate(vecs):
        n = v.shape[-1]
        tile[vocab + j : vocab + j + 1, 0:n] = v[...].astype(F32).reshape(1, n)
    group[:, 0:inner] = w_in[...]
    group[:, inner : inner + LANES] = jnp.transpose(tile[...])[0:wide].astype(BF)


def pack_b_kernel(conv, w_out, group, sems, conv_held, out_held):
    fetch((conv, w_out), (conv_held, out_held), sems)
    inner = group.shape[1]
    rows = [conv_held[k].astype(F32) for k in range(KERNEL_TAPS)]
    for h in range(w_out.shape[1] // inner):
        rows.append(out_held[:, h * inner : (h + 1) * inner].astype(F32))
    group[...] = jnp.concatenate(rows, axis=0).astype(BF)


def line_a_kernel(n, *refs):
    parts, out = refs[:n], refs[n]
    ordered = by_shift([parts[-k % n][...].astype(F32) for k in range(n)], -lax.axis_index("seq") % n)
    out[...] = jnp.concatenate(ordered, axis=0).astype(BF)


def line_b_kernel(n, *refs):
    parts, out = refs[:n], refs[n]
    slabs = out.shape[0]
    values = [parts[-k % n][...].astype(F32) for k in range(n)]
    ordered = by_shift(values, -lax.axis_index("seq") % n)
    part = values[0].shape[0] // slabs
    for slab in range(slabs):
        out[slab] = jnp.concatenate(
            [value[slab * part : (slab + 1) * part] for value in ordered], axis=0
        ).astype(BF)


def first_kernel(wide, narrow, tokens, n1, r1, spread):
    spread[...] = spread_matrix(tokens.shape[1], spread.shape[1], wide, narrow)

    def body(c):
        n, r = standardize(tokens[c, :].astype(F32))
        n1[c, :] = n
        r1[c, :] = jnp.broadcast_to(r, (r.shape[0], LANES))

    each_chunk(tokens.shape[0], 16, body)


def spread_matrix(width, inner, wide, narrow):
    row = lax.broadcasted_iota(jnp.int32, (width, 1), 0)
    device = row // wide
    r = row - device * wide
    at = jnp.where(r < narrow, device * narrow + r, -1)
    return (lax.broadcasted_iota(jnp.int32, (width, inner), 1) == at).astype(F32).astype(BF)


def second_kernel(chips, vocab, n1, spread, *refs):
    pieces = refs[: 2 * chips]
    (w_in, extras, wide_v, narrow_v, act, gp1, n2, gp2, r2, conv_in, proj) = refs[2 * chips :]
    width, inner = w_in.shape
    rows = n1.shape[0]
    me = lax.axis_index("dp")
    block = pieces[0].shape[0]
    for c in range(2):
        for m in range(chips):
            at = pl.multiple_of((me ^ (2 * m + c)) * block, block)
            w_in[pl.ds(at, block), :] = pieces[c * chips + m][:, 0:inner]
            extras[pl.ds(at, block), :] = pieces[c * chips + m][:, inner : inner + LANES]
    turned = jnp.transpose(extras[...].astype(F32))
    wide_v[...] = jnp.zeros_like(wide_v)
    wide_v[0:WIDE_VECTORS, :] = turned[vocab : vocab + WIDE_VECTORS]
    first = vocab + WIDE_VECTORS
    narrow_v[0:NARROW_VECTORS, :] = dot(
        turned.astype(BF), spread[...]
    )[first : first + NARROW_VECTORS]
    g1, b1 = wide_v[0:1, :], wide_v[1:2, :]
    bias, g2, b2 = narrow_v[0:1, :], narrow_v[1:2, :], narrow_v[2:3, :]

    def body(c):
        u = n1[c, :] * g1 + b1
        cdf, pdf = gauss(u)
        act[c, :] = (u * cdf).astype(BF)
        gp1[c, :] = cdf + u * pdf

    each_chunk(rows, 16, body)
    proj[...] = dot(act[...], w_in[...])

    def later(c):
        n, r = standardize(proj[c, :] + bias)
        u = n * g2 + b2
        cdf, pdf = gauss(u)
        conv_in[c, :] = (u * cdf).astype(BF)
        gp2[c, :] = cdf + u * pdf
        n2[c, :] = n
        r2[c, :] = jnp.broadcast_to(r, (r.shape[0], LANES))

    each_chunk(rows, 32, later)


def middle_kernel(
    layout,
    hops,
    seqs,
    vocab,
    wide_v,
    narrow_v,
    extras,
    head_bias,
    types,
    positions,
    targets,
    tokens,
    *refs,
):
    blocks = refs[: 2 * hops + 1]
    pieces = refs[2 * hops + 1 : 2 * hops + 1 + len(layout)]
    (
        taps,
        block_out,
        bundle,
        head_grad,
        conv_low,
        narrow_sums,
        stats,
        ext,
        n3,
        gp3,
        r3,
        work,
        product,
    ) = refs[2 * hops + 1 + len(layout) :]
    inner = taps.shape[1]
    width = tokens.shape[1]
    rows = tokens.shape[0]
    length = rows // seqs
    me = lax.axis_index("dp")
    block = pieces[0].shape[1]
    for (mask, first), piece in zip(layout, pieces):
        at = pl.multiple_of((me ^ mask) * block, block)
        for slab in range(piece.shape[0]):
            taps[first + slab, pl.ds(at, block), :] = piece[slab]
    for b, ref in enumerate(blocks):
        ext[:, b * length : (b + 1) * length, :] = ref[...]
    bias, g3, b3 = narrow_v[3:4, :], narrow_v[4:5, :], narrow_v[5:6, :]
    bias_out = wide_v[2:3, :]
    narrow_sums[...] = jnp.zeros_like(narrow_sums)
    value = dot(taps[KERNEL_TAPS], extras[0:inner, :])
    for h in range(1, width // inner):
        value += dot(taps[KERNEL_TAPS + h], extras[h * inner : (h + 1) * inner, :])
    product[:, 0:LANES] = value.astype(BF)
    product[:, LANES : 2 * LANES] = (value - value.astype(BF).astype(F32)).astype(BF)
    stats[...] = jnp.zeros_like(stats)
    head_grad[...] = jnp.zeros_like(head_grad)
    seat = lax.axis_index("seq")

    @pl.loop(0, seqs)
    def _(s):
        whole = pl.ds(pl.multiple_of(s * length, length), length)
        total = dot(ext[s, pl.ds(hops * length - REACH, length), :], taps[0])
        for k in range(1, KERNEL_TAPS):
            at = hops * length + (k - CENTRE) * DILATION_RATE
            total += dot(ext[s, pl.ds(at, length), :], taps[k])
        work[:, 0:inner] = total

        def ahead(c):
            low = (work[c, 0:inner] + bias).astype(BF).astype(F32)
            n, r = standardize(low)
            u = n * g3 + b3
            cdf, pdf = gauss(u)
            here = pl.ds(pl.multiple_of(s * length + c.start, c.size), c.size)
            bundle[here, inner : 2 * inner] = (u * cdf).astype(BF)
            gp3[c, :] = cdf + u * pdf
            n3[c, :] = n
            r3[c, :] = jnp.broadcast_to(r, (r.shape[0], LANES))

        each_chunk(length, 32, ahead)
        for h in range(width // inner):
            work[:, h * inner : (h + 1) * inner] = dot(
                bundle[whole, inner : 2 * inner], taps[KERNEL_TAPS + h]
            )

        def add(c):
            here = pl.ds(pl.multiple_of(s * length + c.start, c.size), c.size)
            block_out[here, :] = (tokens[here, :].astype(F32) + work[c, :] + bias_out).astype(BF)

        each_chunk(length, 32, add)
        lane = lax.broadcasted_iota(jnp.int32, (length, LANES), 1)
        logits = dot(block_out[whole, :], extras[...]) + head_bias[...]
        logits = jnp.where(lane < vocab, logits, -1e30)
        highest = jnp.max(logits, axis=1, keepdims=True)
        raised = jnp.exp(logits - highest)
        log_total = highest + jnp.log(jnp.sum(raised, axis=1, keepdims=True))
        place = lax.broadcasted_iota(jnp.int32, (length, positions.shape[1]), 0) + seat * length
        matches = positions[pl.ds(s, 1), :] == place
        mask = jnp.sum(jnp.where(matches, 1.0, 0.0), axis=1, keepdims=True)
        goal = jnp.sum(
            jnp.where(matches, targets[pl.ds(s, 1), :].astype(F32), 0.0), axis=1, keepdims=True
        )
        hot = jnp.where(lane == goal.astype(jnp.int32), 1.0, 0.0)
        picked = jnp.sum(logits * hot, axis=1, keepdims=True)
        entropy = log_total - picked
        chance = jnp.exp(picked - log_total)
        grad = (LOSS_SCALE * mask * (jnp.exp(logits - log_total) - hot)).astype(BF)
        bundle[whole, 2 * inner :] = grad
        columns = jnp.where(lane == 0, mask, jnp.where(lane == 1, mask * chance, 0.0))
        kinds = lax.broadcasted_iota(jnp.int32, (LANES, length), 0) == types[pl.ds(s, 1), :]
        tallies = jnp.dot(
            jnp.where(kinds, 1.0, 0.0),
            columns,
            preferred_element_type=F32,
            precision=lax.Precision.HIGHEST,
        )
        stats[0:2, :] += jnp.transpose(tallies)[0:2]
        stats[2:3, :] += jnp.sum(grad.astype(F32), axis=0, keepdims=True)
        stats[3:4, :] += jnp.broadcast_to(
            jnp.sum(mask * entropy, axis=0, keepdims=True), (1, LANES)
        )
        head_grad[...] += dot_tn(block_out[whole, :], grad)
        work[:, 0:inner] = dot_nt(jnp.concatenate([grad, grad], axis=1), product[...])

        def behind(c):
            e = work[c, 0:inner] * gp3[c, :]
            n = n3[c, :]
            narrow_sums[0:8, :] += rows8(e * n)
            narrow_sums[8:16, :] += rows8(e)
            eg = e * g3
            mean_e = jnp.mean(eg, axis=1, keepdims=True)
            mean_en = jnp.mean(eg * n, axis=1, keepdims=True)
            low = (r3[c, 0:1] * (eg - mean_e - n * mean_en)).astype(BF)
            here = pl.ds(pl.multiple_of(s * length + c.start, c.size), c.size)
            conv_low[here, :] = low
            bundle[here, 0:inner] = low
            narrow_sums[16:24, :] += rows8(low.astype(F32))

        each_chunk(length, 32, behind)

    bundle[rows:, :] = jnp.zeros((16, bundle.shape[1]), BF)
    for j, term in enumerate(thirds(stats[...])):
        bundle[rows : rows + 8, j * LANES : (j + 1) * LANES] = term


def conv_grad_kernel(
    chips,
    hops,
    seqs,
    bundle_own,
    bundle_other,
    stats,
    *refs,
):
    count = 2 * hops + 1
    blocks = (refs[:count], refs[count : 2 * count])
    own, own_stats, own_out = refs[2 * count : 2 * count + 3]
    sends = refs[2 * count + 3 : 2 * count + 2 + chips]
    turned, turn, third_t = refs[2 * count + 2 + chips :]
    slabs, block, inner = own.shape
    rows = bundle_own.shape[0] - 16
    length = rows // seqs
    me = lax.axis_index("dp") // 2
    core = lax.axis_index("dp") & 1
    total_stats = stats[...] + sum_terms(bundle_other[rows:, :])
    own_stats[...] = total_stats
    tail = jnp.concatenate([stats_rows(total_stats, inner), jnp.zeros((8, inner), F32)], axis=0)
    for send in sends:
        send[send.shape[0] - 16 :, :] = tail.astype(BF)

    def chosen(ref, q):
        even = ref[2 * q * block : (2 * q + 1) * block, :]
        odd = ref[(2 * q + 1) * block : (2 * q + 2) * block, :]
        return jnp.where(core == 1, odd, even)

    for side in range(2):
        for s in range(seqs):
            for b, ref in enumerate(blocks[side]):
                turn[...] = jnp.transpose(ref[s])
                for q in range(chips):
                    turned[
                        side * seqs + s,
                        q * block : (q + 1) * block,
                        b * length : (b + 1) * length,
                    ] = chosen(turn, q)
        for s in range(seqs):
            columns = slice(s * length, (s + 1) * length)
            source = (bundle_own, bundle_other)[side]
            turn[...] = jnp.transpose(source[columns, inner : 2 * inner])
            for q in range(chips):
                third_t[side, q * block : (q + 1) * block, columns] = chosen(turn, q)

    def share(slab, value):
        parts = by_mask([value[q * block : (q + 1) * block] for q in range(chips)], me)
        own[slab] = parts[0]
        for m in range(1, chips):
            sends[m - 1][slab * block : (slab + 1) * block, :] = parts[m].astype(BF)

    for k in range(KERNEL_TAPS):
        at = hops * length + (k - CENTRE) * DILATION_RATE
        value = 0.0
        for side, low in enumerate((bundle_own, bundle_other)):
            for s in range(seqs):
                value = value + dot(
                    turned[side * seqs + s, :, at : at + length],
                    low[s * length : (s + 1) * length, 0:inner],
                )
        share(k, value)
    value = dot(third_t[0], bundle_own[0:rows, 2 * inner :])
    value += dot(third_t[1], bundle_other[0:rows, 2 * inner :])
    parts = by_mask([value[q * block : (q + 1) * block] for q in range(chips)], me)
    own_out[...] = parts[0]
    for m in range(1, chips):
        lines = beside(parts[m], inner // LANES)
        sends[m - 1][slabs * block : slabs * block + lines.shape[0], :] = lines.astype(BF)


def sum_terms(ref_value):
    return (
        ref_value[0:8, 0:LANES].astype(F32)
        + ref_value[0:8, LANES : 2 * LANES].astype(F32)
        + ref_value[0:8, 2 * LANES : 3 * LANES].astype(F32)
    )


def line_grad_b_kernel(count, size, part, own, stats, own_out, *refs):
    parts = refs[:count]
    keep, keep_stats, keep_out = refs[count : count + 3]
    sends = refs[count + 3 :]
    slabs, block, inner = own.shape
    me = lax.axis_index("seq")
    rows = parts[0].shape[0]
    sums = stats[...]
    out = own_out[...]
    for p in parts:
        sums += sum_terms(p[rows - 16 :, :])
        out += below(p[slabs * block : rows - 16, :].astype(F32))
    keep_stats[...] = sums
    pieces = [[] for _ in range(size)]
    for slab in range(slabs):
        value = own[slab]
        for p in parts:
            value += p[slab * block : (slab + 1) * block, :].astype(F32)
        cut = by_shift([value[z * part : (z + 1) * part] for z in range(size)], me)
        keep[slab] = cut[0]
        for k in range(1, size):
            pieces[k].append(cut[k])
    cut = by_shift([out[z * part : (z + 1) * part] for z in range(size)], me)
    tail_rows = keep_out.shape[0]
    keep_out[...] = padded(cut[0], tail_rows)
    terms = padded(stats_rows(sums, 3 * LANES), tail_rows)
    gap = sends[0].shape[0] - slabs * part - tail_rows
    for k in range(1, size):
        rest = inner - 4 * LANES
        tail = [terms, padded(cut[k], tail_rows), jnp.zeros((tail_rows, rest), F32)]
        lines = pieces[k] + ([jnp.zeros((gap, inner), F32)] if gap else [])
        lines.append(jnp.concatenate(tail, axis=1))
        sends[k - 1][...] = jnp.concatenate(lines, axis=0).astype(BF)


def end_b_kernel(count, keep, stats, keep_out, extras, *refs):
    parts = refs[:count]
    conv, out, sums = refs[count:]
    slabs, part, inner = keep.shape
    tail_rows = keep_out.shape[0]
    values = [p[...].astype(F32) for p in parts]
    total = stats[...]
    product = keep_out[...]
    for value in values:
        tail = value[value.shape[0] - tail_rows :]
        total += sum_terms(tail)
        product += tail[:, 3 * LANES : 4 * LANES]
    sums[...] = total
    value = 0.0
    for term in thirds(product):
        value = value + dot_nt(term, extras[...])
    out[...] = value[0:part]
    for slab in range(slabs):
        value = keep[slab]
        for v in values:
            value += v[slab * part : (slab + 1) * part]
        conv[slab] = value


def split_a_kernel(chips, keep, got_low, got_high, own, token, *sends):
    token[...] = jnp.zeros_like(token)
    half = chips // 2
    sums = [
        keep[q] + (got_low, got_high)[q // half][q % half].astype(F32) for q in range(chips)
    ]
    sums = by_mask(sums, lax.axis_index("dp") // 2)
    own[...] = sums[0]
    for m in range(1, chips):
        sends[m - 1][...] = sums[m].astype(BF)


def line_grad_a_kernel(count, size, part, own, *refs):
    parts = refs[:count]
    keep = refs[count]
    sends = refs[count + 1 :]
    me = lax.axis_index("seq")
    value = own[...]
    for p in parts:
        value += p[...].astype(F32)
    cut = [value[z * part : (z + 1) * part] for z in range(size)]
    for k in range(size):
        piece = cut[0]
        for z in range(1, size):
            piece = jnp.where(lax.rem(me + k, size) == z, cut[z], piece)
        if k == 0:
            keep[...] = piece
        else:
            sends[k - 1][...] = piece.astype(BF)


def end_a_kernel(count, vocab, keep, *refs):
    parts = refs[:count]
    w_in, head_t = refs[count : count + 2]
    vecs = refs[count + 2 : count + 2 + WIDE_VECTORS + NARROW_VECTORS]
    (tile,) = refs[count + 2 + WIDE_VECTORS + NARROW_VECTORS :]
    wide, inner = w_in.shape
    value = keep[...]
    for p in parts:
        value += p[...].astype(F32)
    w_in[...] = value[:, 0:inner]
    tile[...] = jnp.zeros_like(tile)
    tile[0:wide, :] = value[:, inner : inner + LANES]
    turned = jnp.transpose(tile[...])
    head_t[...] = turned[0:vocab, 0:wide]
    for j, v in enumerate(vecs):
        n = v.shape[-1]
        v[...] = turned[vocab + j : vocab + j + 1, 0:n].reshape(v.shape)


def back_kernel(
    chips,
    hops,
    seqs,
    vocab,
    wide,
    narrow,
    taps,
    n2,
    gp2,
    r2,
    n1,
    gp1,
    act,
    w_in,
    wide_v,
    narrow_v,
    narrow_sums,
    stats,
    extras,
    head_grad,
    *refs,
):
    blocks = refs[: 2 * hops + 1]
    keep, send_low, send_high, e1, low, ext, work, act_t, sums1, sums2 = refs[2 * hops + 1 :]
    half = chips // 2
    width, inner = w_in.shape
    rows = low.shape[0]
    length = rows // seqs
    g2 = narrow_v[1:2, :]
    for b, ref in enumerate(blocks):
        ext[:, b * length : (b + 1) * length, :] = ref[...]
    sums1[...] = jnp.zeros_like(sums1)
    sums2[...] = jnp.zeros_like(sums2)

    @pl.loop(0, seqs)
    def _(s):
        whole = pl.ds(pl.multiple_of(s * length, length), length)
        total = dot_nt(ext[s, pl.ds(hops * length + REACH, length), :], taps[0])
        for k in range(1, KERNEL_TAPS):
            at = hops * length - (k - CENTRE) * DILATION_RATE
            total += dot_nt(ext[s, pl.ds(at, length), :], taps[k])
        work[:, 0:inner] = total

        def second(c):
            here = pl.ds(pl.multiple_of(s * length + c.start, c.size), c.size)
            e = work[c, 0:inner].astype(BF).astype(F32) * gp2[here, :]
            n = n2[here, :]
            sums2[0:8, :] += rows8(e * n)
            sums2[8:16, :] += rows8(e)
            eg = e * g2
            mean_e = jnp.mean(eg, axis=1, keepdims=True)
            mean_en = jnp.mean(eg * n, axis=1, keepdims=True)
            value = (r2[here, 0:1] * (eg - mean_e - n * mean_en)).astype(BF)
            low[here, :] = value
            sums2[16:24, :] += rows8(value.astype(F32))

        each_chunk(length, 32, second)
        work[...] = dot_nt(low[whole, :], w_in[...])

        def first(c):
            here = pl.ds(pl.multiple_of(s * length + c.start, c.size), c.size)
            e = work[c, :] * gp1[here, :]
            e1[here, :] = e
            sums1[0:8, :] += rows8(e * n1[here, :])
            sums1[8:16, :] += rows8(e)

        each_chunk(length, 16, first)

    def folded(ref, j):
        return jnp.sum(ref[8 * j : 8 * j + 8, :], axis=0, keepdims=True)

    bias = 0.0
    for term in thirds(stats[...]):
        bias = bias + dot_nt(term, extras[...])
    wides = [folded(sums1, 0), folded(sums1, 1), bias[2:3, :]]
    narrows = [folded(sums2, 2), folded(sums2, 0), folded(sums2, 1)]
    narrows += [folded(narrow_sums, 2), folded(narrow_sums, 0), folded(narrow_sums, 1)]
    row = lax.broadcasted_iota(jnp.int32, (16, inner), 0)
    stacked = jnp.zeros((16, inner), F32)
    for j, v in enumerate(narrows):
        stacked = jnp.where(row == j, v, stacked)
    spread = spread_matrix(width, inner, wide, narrow)
    placed = 0.0
    for term in thirds(stacked):
        placed = placed + dot_nt(term, spread)
    row = lax.broadcasted_iota(jnp.int32, (LANES, width), 0)
    grid = jnp.zeros((LANES, width), F32)
    for j, v in enumerate(wides):
        grid = jnp.where(row == vocab + j, v, grid)
    for j in range(NARROW_VECTORS):
        grid = jnp.where(row == vocab + WIDE_VECTORS + j, placed[j : j + 1, :], grid)
    extra = jnp.transpose(grid) + head_grad[...]
    act_t[...] = jnp.transpose(act[...])
    core = lax.axis_index("dp") & 1
    block = keep.shape[1]
    for q in range(chips):
        for c in range(2):
            d = 2 * q + c
            lines = slice(d * block, (d + 1) * block)
            value = dot(act_t[lines, :], low[...])

            @pl.when(core == c)
            def _():
                keep[q, :, 0:inner] = value
                keep[q, :, inner : inner + LANES] = extra[lines]

            @pl.when(core != c)
            def _():
                send = (send_low, send_high)[q // half]
                send[q % half, :, 0:inner] = value.astype(BF)
                send[q % half, :, inner : inner + LANES] = extra[lines].astype(BF)


def input_kernel(e1, n1, r1, wide_v, bundle, extras, input_grad, token, work):
    token[...] = jnp.zeros_like(token)
    logit_grad = bundle[0 : e1.shape[0], bundle.shape[1] - LANES :]
    work[...] = dot_nt(logit_grad, extras[...])
    g1 = wide_v[0:1, :]

    def body(c):
        n = n1[c, :]
        eg = e1[c, :] * g1
        mean_e = jnp.mean(eg, axis=1, keepdims=True)
        mean_en = jnp.mean(eg * n, axis=1, keepdims=True)
        input_grad[c, :] = (work[c, :] + r1[c, 0:1] * (eg - mean_e - n * mean_en)).astype(BF)

    each_chunk(e1.shape[0], 16, body)


def swap(value, mask):
    count = lax.axis_size("dp")
    return lax.ppermute(value, "dp", [(i, i ^ mask) for i in range(count)])


def shifted(value, k):
    size = lax.axis_size("seq")
    return lax.ppermute(value, "seq", [(i, (i + k) % size) for i in range(size)])


def line_parts(block):
    return [block] + [shifted(block, k) for k in range(1, lax.axis_size("seq"))]


def chip_pieces(block):
    chips = lax.axis_size("dp") // 2
    own = [block] + [swap(block, 2 * m) for m in range(1, chips)]
    return own + [swap(piece, 1) for piece in own]


def halo(series):
    size = lax.axis_size("seq")
    hops = -(-REACH // series.shape[1])
    before = [
        lax.ppermute(series, "seq", [(i, i + h) for i in range(size - h)])
        for h in range(hops, 0, -1)
    ]
    after = [
        lax.ppermute(series, "seq", [(i + h, i) for i in range(size - h)])
        for h in range(1, hops + 1)
    ]
    return before + [series] + after


def shards(
    tokens,
    first_gain,
    first_bias,
    in_weight,
    in_bias,
    second_gain,
    second_bias,
    conv_weight,
    conv_bias,
    third_gain,
    third_bias,
    out_weight,
    out_bias,
    head_weight,
    head_bias,
    residue_types,
    mask_positions,
    targets,
):
    dp = lax.axis_size("dp")
    size = lax.axis_size("seq")
    chips = dp // 2
    seqs, length, width = tokens.shape
    wide, inner = in_weight.shape
    narrow = out_weight.shape[0]
    vocab = head_weight.shape[1]
    rows = seqs * length
    hops = -(-REACH // length)
    slabs = KERNEL_TAPS + width // inner
    flat = tokens.reshape(rows, width)

    ins = [
        in_weight,
        head_weight.T,
        first_gain,
        first_bias,
        out_bias,
        in_bias,
        second_gain,
        second_bias,
        conv_bias,
        third_gain,
        third_bias,
    ]
    (block_a,) = call(
        functools.partial(pack_a_kernel, vocab),
        ins,
        [sds((wide, inner + LANES), BF)],
        [pltpu.VMEM((LANES, LANES), F32), pltpu.SemaphoreType.DMA((len(ins),))]
        + [pltpu.VMEM(x.shape, BF) for x in ins],
        limit=56,
        name="pack_a",
        free=len(ins),
    )
    parts_a = line_parts(block_a)
    (line_a,) = call(
        functools.partial(line_a_kernel, size),
        parts_a,
        [sds((size * wide, inner + LANES), BF)],
        name="line_a",
    )
    ins = [jnp.transpose(conv_weight, (1, 0, 2)), out_weight]
    (block_b,) = call(
        pack_b_kernel,
        ins,
        [sds((slabs * narrow, inner), BF)],
        [pltpu.SemaphoreType.DMA((2,))] + [pltpu.VMEM(x.shape, BF) for x in ins],
        limit=8,
        name="pack_b",
        free=2,
        after=[block_a],
    )
    own_a = [line_a] + [swap(line_a, 2 * m) for m in range(1, chips)]
    parts_b = line_parts(block_b)
    n1, r1, spread = call(
        functools.partial(first_kernel, wide, narrow),
        [flat],
        [sds((rows, width), F32), sds((rows, LANES), F32), sds((width, inner), BF)],
        us=6,
        limit=8,
        name="first",
        after=[block_b],
    )
    *own_a, _ = lax.optimization_barrier((*own_a, r1))
    pieces_a = list(own_a) + [swap(piece, 1) for piece in own_a]
    (line_b,) = call(
        functools.partial(line_b_kernel, size),
        parts_b,
        [sds((slabs, size * narrow, inner), BF)],
        name="line_b",
        after=[r1],
    )
    if chips == 4:
        half = slabs // 2
        by_x, by_y = swap(line_b, 2), swap(line_b, 4)
        own_b = [line_b, by_x, by_y, swap(by_x[:half], 4), swap(by_y[half:], 2)]
        layout = [(0, 0), (2, 0), (4, 0), (6, 0), (6, half)]
    else:
        own_b = [line_b] + [swap(line_b, 2 * m) for m in range(1, chips)]
        layout = [(2 * m, 0) for m in range(chips)]
    layout = layout + [(mask + 1, first) for mask, first in layout]
    w_in, extras, wide_v, narrow_v, act, gp1, n2, gp2, r2, conv_in = call(
        functools.partial(second_kernel, chips, vocab),
        [n1, spread] + pieces_a,
        [
            sds((width, inner), BF),
            sds((width, LANES), BF),
            sds((8, width), F32),
            sds((8, inner), F32),
            sds((rows, width), BF),
            sds((rows, width), F32),
            sds((rows, inner), F32),
            sds((rows, inner), F32),
            sds((rows, LANES), F32),
            sds((rows, inner), BF),
        ],
        [pltpu.VMEM((rows, inner), F32)],
        us=9,
        limit=16,
        name="second",
        after=[line_b],
    )
    blocks = halo(conv_in.reshape(seqs, length, inner))
    other_line = swap(line_b, 1)
    early = 3 if chips == 4 else 1
    near = [swap(piece, 1) for piece in own_b[1:early]]
    *late, _, _ = lax.optimization_barrier((*own_b[early:], blocks[0], blocks[-1]))
    pieces_b = own_b[:early] + list(late) + [other_line] + near + [swap(piece, 1) for piece in late]
    other_blocks = [swap(piece, 1) for piece in blocks]
    (
        taps,
        block_out,
        bundle,
        head_grad,
        conv_low,
        narrow_sums,
        stats,
    ) = call(
        functools.partial(middle_kernel, layout, hops, seqs, vocab),
        [
            wide_v,
            narrow_v,
            extras,
            jnp.pad(head_bias.astype(F32), (0, LANES - vocab)).reshape(1, LANES),
            residue_types,
            mask_positions,
            targets,
            flat,
        ]
        + blocks
        + pieces_b,
        [
            sds((slabs, inner, inner), BF),
            sds((rows, width), BF),
            sds((rows + 16, 2 * inner + LANES), BF),
            sds((width, LANES), F32),
            sds((rows, inner), BF),
            sds((24, inner), F32),
            sds((8, LANES), F32),
        ],
        [
            pltpu.VMEM((seqs, (2 * hops + 1) * length, inner), BF),
            pltpu.VMEM((length, inner), F32),
            pltpu.VMEM((length, inner), F32),
            pltpu.VMEM((length, LANES), F32),
            pltpu.VMEM((length, width), F32),
            pltpu.VMEM((inner, 2 * LANES), BF),
        ],
        us=17,
        limit=16,
        name="middle",
    )
    grad_blocks = halo(conv_low.reshape(seqs, length, inner))
    other_bundle = swap(bundle, 1)
    message = KERNEL_TAPS * size * narrow + size * narrow // (inner // LANES) + 16
    split_b = call(
        functools.partial(conv_grad_kernel, chips, hops, seqs),
        [bundle, other_bundle, stats]
        + blocks
        + other_blocks,
        [
            sds((KERNEL_TAPS, size * narrow, inner), F32),
            sds((8, LANES), F32),
            sds((size * narrow, LANES), F32),
        ]
        + [sds((message, inner), BF)] * (chips - 1),
        [
            pltpu.VMEM((2 * seqs, inner // 2, (2 * hops + 1) * length), BF),
            pltpu.VMEM((inner, length), BF),
            pltpu.VMEM((2, inner // 2, rows), BF),
        ],
        us=7,
        limit=16,
        name="conv_grad",
    )
    from_chips_b = [swap(piece, 2 * m) for m, piece in zip(range(1, chips), split_b[3:])]
    keep_a, send_low, send_high, e1 = call(
        functools.partial(back_kernel, chips, hops, seqs, vocab, wide, narrow),
        [taps, n2, gp2, r2, n1, gp1, act, w_in, wide_v, narrow_v]
        + [narrow_sums, stats, extras, head_grad]
        + grad_blocks,
        [
            sds((chips, size * wide, inner + LANES), F32),
            sds((chips // 2, size * wide, inner + LANES), BF),
            sds((chips // 2, size * wide, inner + LANES), BF),
            sds((rows, width), F32),
        ],
        [
            pltpu.VMEM((rows, inner), BF),
            pltpu.VMEM((seqs, (2 * hops + 1) * length, inner), BF),
            pltpu.VMEM((length, width), F32),
            pltpu.VMEM((width, rows), BF),
            pltpu.VMEM((16, width), F32),
            pltpu.VMEM((24, inner), F32),
        ],
        us=US_S,
        limit=20,
        name="back",
        after=[split_b[1]],
    )
    got_low, got_high = swap(send_low, 1), swap(send_high, 1)
    split = call(
        functools.partial(split_a_kernel, chips),
        [keep_a, got_low, got_high],
        [sds((size * wide, inner + LANES), F32), sds((8, LANES), F32)]
        + [sds((size * wide, inner + LANES), BF)] * (chips - 1),
        us=US_S,
        name="split_a",
    )
    tail = -(-max(narrow, 8) // 8) * 8
    line_b2 = call(
        functools.partial(line_grad_b_kernel, chips - 1, size, narrow),
        list(split_b[:3]) + from_chips_b,
        [sds((KERNEL_TAPS, narrow, inner), F32), sds((8, LANES), F32), sds((tail, LANES), F32)]
        + [sds((-(-KERNEL_TAPS * narrow // 8) * 8 + tail, inner), BF)] * (size - 1),
        name="line_grad_b",
        after=[split[1]],
    )
    *a_sends, _ = lax.optimization_barrier((*split[2:], line_b2[1]))
    from_chips = [swap(piece, 2 * m) for m, piece in zip(range(1, chips), a_sends)]

    input_grad, input_token = call(
        input_kernel,
        [e1, n1, r1, wide_v, bundle, extras],
        [sds((rows, width), BF), sds((8, LANES), F32)],
        [pltpu.VMEM((rows, width), F32)],
        us=3,
        name="input",
        after=[line_b2[1]],
    )
    from_line_b = [shifted(piece, k) for k, piece in zip(range(1, size), line_b2[3:])]
    line = call(
        functools.partial(line_grad_a_kernel, chips - 1, size, wide),
        [split[0]] + from_chips,
        [sds((wide, inner + LANES), F32)] + [sds((wide, inner + LANES), BF)] * (size - 1),
        name="line_grad_a",
        after=[input_token],
    )
    conv_share, out_share, sums = call(
        functools.partial(end_b_kernel, size - 1),
        [line_b2[0], line_b2[1], line_b2[2], extras] + from_line_b,
        [sds((KERNEL_TAPS, narrow, inner), F32), sds((narrow, width), F32), sds((8, LANES), F32)],
        name="end_b",
        after=[line[0]],
    )
    from_line = [shifted(piece, k) for k, piece in zip(range(1, size), line[1:])]
    ended = call(
        functools.partial(end_a_kernel, size - 1, vocab),
        [line[0]] + from_line,
        [sds((wide, inner), F32), sds((vocab, wide), F32)]
        + [sds((wide,), F32)] * WIDE_VECTORS
        + [sds((narrow,), F32)] * NARROW_VECTORS,
        [pltpu.VMEM((LANES, LANES), F32)],
        name="end_a",
    )
    in_share, head_share, g1, b1, bo, bi, g2, b2, bc, g3, b3 = ended
    masked_total = seqs * dp * mask_positions.shape[1]
    return (
        block_out.reshape(seqs, length, width),
        input_grad.reshape(seqs, length, width),
        g1,
        b1,
        in_share,
        bi,
        g2,
        b2,
        jnp.transpose(conv_share, (1, 0, 2)),
        bc,
        g3,
        b3,
        out_share,
        bo,
        head_share.T,
        sums[2, :vocab],
        sums[0, :vocab].astype(jnp.int32),
        sums[1, :vocab],
        sums[3, 0] / masked_total,
    )


def solution(mesh):
    both = P(("dp", "seq"))
    matrix = P(("dp", "seq"), None)
    cube = P(("dp", "seq"), None, None)
    rows = P("dp", "seq", None)
    return jax.shard_map(
        shards,
        mesh=mesh,
        in_specs=(rows, both, both, matrix, both, both, both, cube, both, both, both, matrix)
        + (both, matrix, P(), P("dp", "seq"), P("dp", None), P("dp", None)),
        out_specs=(rows, rows, both, both, matrix, both, both, both, cube, both, both, both)
        + (matrix, both, matrix, P(), P(), P(), P()),
        check_vma=False,
    )
```

```python
import functools

import jax
import jax.numpy as jnp
from jax import lax
from jax.experimental import pallas as pl
from jax.experimental.pallas import tpu as pltpu
from jax.sharding import PartitionSpec as P

KERNEL_TAPS = 5
CENTRE = KERNEL_TAPS // 2
DILATION_RATE = 128
NORM_EPSILON = 1e-05
LOSS_SCALE = 16.0
REACH = CENTRE * DILATION_RATE
BF = jnp.bfloat16
F32 = jnp.float32
LANES = 128
US_S = 0.1
WIDE_VECTORS = 3
NARROW_VECTORS = 6
MIB = 1024 * 1024
HALF_ROOT = 0.7071067811865476
INV_ROOT_TWO_PI = 0.3989422804014327


def gauss(u):
    t = pl.reciprocal(1.0 + (0.3275911 * HALF_ROOT) * jnp.abs(u), approx=False)
    e = jnp.exp2(u * u * -0.7213475204444817)
    poly = t * (
        0.127414796
        + t * (-0.142248368 + t * (0.7107068705 + t * (-0.7265760135 + t * 0.5307027145)))
    )
    tail = poly * e
    return jnp.where(u < 0, tail, 1.0 - tail), e * INV_ROOT_TWO_PI


def standardize(v):
    average = jnp.mean(v, axis=-1, keepdims=True)
    centred = v - average
    spread = jnp.mean(centred * centred, axis=-1, keepdims=True)
    r = lax.rsqrt(spread + NORM_EPSILON)
    return centred * r, r


def dot(a, b):
    return jnp.dot(a, b, preferred_element_type=F32)


def dot_nt(a, b):
    return lax.dot_general(a, b, (((1,), (1,)), ((), ())), preferred_element_type=F32)


def dot_tn(a, b):
    return lax.dot_general(a, b, (((0,), (0,)), ((), ())), preferred_element_type=F32)


def rows8(x):
    return jnp.sum(x.reshape(x.shape[0] // 8, 8, x.shape[1]), axis=0)


def each_chunk(count, step, body):
    @pl.loop(0, count // step, unroll=8 if count // step >= 8 else 4)
    def _(i):
        body(pl.ds(pl.multiple_of(i * step, step), step))


def thirds(x):
    high = x.astype(BF)
    rest = x - high.astype(F32)
    mid = rest.astype(BF)
    low = (rest - mid.astype(F32)).astype(BF)
    return high, mid, low


def by_mask(values, me):
    bit = 1
    while bit < len(values):
        here = (me & bit) != 0
        values = [jnp.where(here, values[m ^ bit], values[m]) for m in range(len(values))]
        bit *= 2
    return values


def by_shift(values, me):
    bit = 1
    n = len(values)
    while bit < n:
        here = (me & bit) != 0
        values = [jnp.where(here, values[(k + bit) % n], values[k]) for k in range(n)]
        bit *= 2
    return values


def of_core(values):
    core = lax.axis_index("dp") & 1
    return [
        jnp.where(core == 1, odd, even) for even, odd in zip(values[0::2], values[1::2])
    ]


def beside(value, count):
    r = value.shape[0] // count
    return jnp.concatenate([value[g * r : (g + 1) * r] for g in range(count)], axis=1)


def below(value):
    count = value.shape[1] // LANES
    return jnp.concatenate([value[:, g * LANES : (g + 1) * LANES] for g in range(count)], axis=0)


def stats_rows(total, inner):
    terms = [term.astype(F32) for term in thirds(total)]
    rest = inner - 3 * LANES
    return jnp.concatenate(terms + ([jnp.zeros((8, rest), F32)] if rest else []), axis=1)


def padded(value, rows):
    gap = rows - value.shape[0]
    if gap == 0:
        return value
    return jnp.concatenate([value, jnp.zeros((gap, value.shape[1]), F32)], axis=0)


def vmem(n):
    return [pl.BlockSpec(memory_space=pltpu.VMEM)] * n


def call(kernel, ins, outs, scratch=(), us=1, limit=12, name=None, after=(), free=0):
    count = len(ins)
    skipped = len(after)

    def body(*refs):
        kernel(*refs[:count], *refs[count + skipped :])

    return pl.pallas_call(
        body,
        out_shape=list(outs),
        in_specs=[pl.BlockSpec(memory_space=pltpu.HBM)] * free
        + vmem(count - free)
        + [pl.BlockSpec(memory_space=pl.ANY)] * skipped,
        out_specs=vmem(len(outs)),
        scratch_shapes=list(scratch),
        compiler_params=pltpu.CompilerParams(vmem_limit_bytes=limit * MIB),
        cost_estimate=pl.CostEstimate(flops=int(us * 1e9), bytes_accessed=1000, transcendentals=0),
        name=name,
    )(*ins, *after)


def sds(shape, dtype):
    return jax.ShapeDtypeStruct(shape, dtype)


def fetch(sources, targets, sems):
    copies = [
        pltpu.make_async_copy(source, target, sems.at[j])
        for j, (source, target) in enumerate(zip(sources, targets))
    ]
    for copy in copies:
        copy.start()
    for copy in copies:
        copy.wait()


def pack_a_kernel(vocab, *refs):
    count = 2 + WIDE_VECTORS + NARROW_VECTORS
    group, tile, sems = refs[count : count + 3]
    held = refs[count + 3 :]
    fetch(refs[:count], held, sems)
    w_in, head_t, vecs = held[0], held[1], held[2:]
    wide, inner = w_in.shape
    tile[...] = jnp.zeros_like(tile)
    tile[0:vocab, 0:wide] = head_t[...].astype(F32)
    for j, v in enumerate(vecs):
        n = v.shape[-1]
        tile[vocab + j : vocab + j + 1, 0:n] = v[...].astype(F32).reshape(1, n)
    group[:, 0:inner] = w_in[...]
    group[:, inner : inner + LANES] = jnp.transpose(tile[...])[0:wide].astype(BF)


def pack_b_kernel(conv, w_out, group, sems, conv_held, out_held):
    fetch((conv, w_out), (conv_held, out_held), sems)
    inner = group.shape[1]
    rows = [conv_held[k].astype(F32) for k in range(KERNEL_TAPS)]
    for h in range(w_out.shape[1] // inner):
        rows.append(out_held[:, h * inner : (h + 1) * inner].astype(F32))
    group[...] = jnp.concatenate(rows, axis=0).astype(BF)


def line_a_kernel(n, *refs):
    parts, out = refs[:n], refs[n]
    ordered = by_shift([parts[-k % n][...].astype(F32) for k in range(n)], -lax.axis_index("seq") % n)
    out[...] = jnp.concatenate(ordered, axis=0).astype(BF)


def line_b_kernel(n, *refs):
    parts, out = refs[:n], refs[n]
    slabs = out.shape[0]
    values = [parts[-k % n][...].astype(F32) for k in range(n)]
    ordered = by_shift(values, -lax.axis_index("seq") % n)
    part = values[0].shape[0] // slabs
    for slab in range(slabs):
        out[slab] = jnp.concatenate(
            [value[slab * part : (slab + 1) * part] for value in ordered], axis=0
        ).astype(BF)


def first_kernel(wide, narrow, tokens, n1, r1, spread):
    spread[...] = spread_matrix(tokens.shape[1], spread.shape[1], wide, narrow)

    def body(c):
        n, r = standardize(tokens[c, :].astype(F32))
        n1[c, :] = n
        r1[c, :] = jnp.broadcast_to(r, (r.shape[0], LANES))

    each_chunk(tokens.shape[0], 16, body)


def spread_matrix(width, inner, wide, narrow):
    row = lax.broadcasted_iota(jnp.int32, (width, 1), 0)
    device = row // wide
    r = row - device * wide
    at = jnp.where(r < narrow, device * narrow + r, -1)
    return (lax.broadcasted_iota(jnp.int32, (width, inner), 1) == at).astype(F32).astype(BF)


def second_kernel(chips, vocab, n1, spread, *refs):
    pieces = refs[: 2 * chips]
    (w_in, extras, wide_v, narrow_v, act, gp1, n2, gp2, r2, conv_in, proj) = refs[2 * chips :]
    width, inner = w_in.shape
    rows = n1.shape[0]
    me = lax.axis_index("dp")
    block = pieces[0].shape[0]
    for c in range(2):
        for m in range(chips):
            at = pl.multiple_of((me ^ (2 * m + c)) * block, block)
            w_in[pl.ds(at, block), :] = pieces[c * chips + m][:, 0:inner]
            extras[pl.ds(at, block), :] = pieces[c * chips + m][:, inner : inner + LANES]
    turned = jnp.transpose(extras[...].astype(F32))
    wide_v[...] = jnp.zeros_like(wide_v)
    wide_v[0:WIDE_VECTORS, :] = turned[vocab : vocab + WIDE_VECTORS]
    first = vocab + WIDE_VECTORS
    narrow_v[0:NARROW_VECTORS, :] = dot(
        turned.astype(BF), spread[...]
    )[first : first + NARROW_VECTORS]
    g1, b1 = wide_v[0:1, :], wide_v[1:2, :]
    bias, g2, b2 = narrow_v[0:1, :], narrow_v[1:2, :], narrow_v[2:3, :]

    def body(c):
        u = n1[c, :] * g1 + b1
        cdf, pdf = gauss(u)
        act[c, :] = (u * cdf).astype(BF)
        gp1[c, :] = cdf + u * pdf

    half = rows // 2
    for at in range(0, rows, half):
        for j in range(at, at + half, 16):
            body(pl.ds(j, 16))
        proj[at : at + half, :] = dot(act[at : at + half, :], w_in[...])

    def later(c):
        n, r = standardize(proj[c, :] + bias)
        u = n * g2 + b2
        cdf, pdf = gauss(u)
        conv_in[c, :] = (u * cdf).astype(BF)
        gp2[c, :] = cdf + u * pdf
        n2[c, :] = n
        r2[c, :] = jnp.broadcast_to(r, (r.shape[0], LANES))

    for j in range(0, rows, 32):
        later(pl.ds(j, 32))


def middle_kernel(
    layout,
    hops,
    seqs,
    vocab,
    wide_v,
    narrow_v,
    extras,
    head_bias,
    types,
    positions,
    targets,
    tokens,
    *refs,
):
    blocks = refs[: 2 * hops + 1]
    pieces = refs[2 * hops + 1 : 2 * hops + 1 + len(layout)]
    (
        taps,
        block_out,
        bundle,
        head_grad,
        conv_low,
        narrow_sums,
        stats,
        ext,
        n3,
        gp3,
        r3,
        work,
        product,
    ) = refs[2 * hops + 1 + len(layout) :]
    inner = taps.shape[1]
    width = tokens.shape[1]
    rows = tokens.shape[0]
    length = rows // seqs
    me = lax.axis_index("dp")
    block = pieces[0].shape[1]
    for (mask, first), piece in zip(layout, pieces):
        at = pl.multiple_of((me ^ mask) * block, block)
        for slab in range(piece.shape[0]):
            taps[first + slab, pl.ds(at, block), :] = piece[slab]
    for b, ref in enumerate(blocks):
        ext[:, b * length : (b + 1) * length, :] = ref[...]
    bias, g3, b3 = narrow_v[3:4, :], narrow_v[4:5, :], narrow_v[5:6, :]
    bias_out = wide_v[2:3, :]
    narrow_sums[...] = jnp.zeros_like(narrow_sums)
    value = dot(taps[KERNEL_TAPS], extras[0:inner, :])
    for h in range(1, width // inner):
        value += dot(taps[KERNEL_TAPS + h], extras[h * inner : (h + 1) * inner, :])
    product[:, 0:LANES] = value.astype(BF)
    product[:, LANES : 2 * LANES] = (value - value.astype(BF).astype(F32)).astype(BF)
    stats[...] = jnp.zeros_like(stats)
    head_grad[...] = jnp.zeros_like(head_grad)
    seat = lax.axis_index("seq")

    @pl.loop(0, seqs, unroll=True)
    def _(s):
        whole = pl.ds(pl.multiple_of(s * length, length), length)
        total = dot(ext[s, pl.ds(hops * length - REACH, length), :], taps[0])
        for k in range(1, KERNEL_TAPS):
            at = hops * length + (k - CENTRE) * DILATION_RATE
            total += dot(ext[s, pl.ds(at, length), :], taps[k])
        work[:, 0:inner] = total

        def ahead(c):
            low = (work[c, 0:inner] + bias).astype(BF).astype(F32)
            n, r = standardize(low)
            u = n * g3 + b3
            cdf, pdf = gauss(u)
            here = pl.ds(pl.multiple_of(s * length + c.start, c.size), c.size)
            bundle[here, inner : 2 * inner] = (u * cdf).astype(BF)
            gp3[c, :] = cdf + u * pdf
            n3[c, :] = n
            r3[c, :] = jnp.broadcast_to(r, (r.shape[0], LANES))

        each_chunk(length, 32, ahead)
        for h in range(width // inner):
            work[:, h * inner : (h + 1) * inner] = dot(
                bundle[whole, inner : 2 * inner], taps[KERNEL_TAPS + h]
            )

        def add(c):
            here = pl.ds(pl.multiple_of(s * length + c.start, c.size), c.size)
            block_out[here, :] = (tokens[here, :].astype(F32) + work[c, :] + bias_out).astype(BF)

        each_chunk(length, 32, add)
        lane = lax.broadcasted_iota(jnp.int32, (length, LANES), 1)
        logits = dot(block_out[whole, :], extras[...]) + head_bias[...]
        logits = jnp.where(lane < vocab, logits, -1e30)
        highest = jnp.max(logits, axis=1, keepdims=True)
        raised = jnp.exp(logits - highest)
        log_total = highest + jnp.log(jnp.sum(raised, axis=1, keepdims=True))
        place = lax.broadcasted_iota(jnp.int32, (length, positions.shape[1]), 0) + seat * length
        matches = positions[pl.ds(s, 1), :] == place
        mask = jnp.sum(jnp.where(matches, 1.0, 0.0), axis=1, keepdims=True)
        goal = jnp.sum(
            jnp.where(matches, targets[pl.ds(s, 1), :].astype(F32), 0.0), axis=1, keepdims=True
        )
        hot = jnp.where(lane == goal.astype(jnp.int32), 1.0, 0.0)
        picked = jnp.sum(logits * hot, axis=1, keepdims=True)
        entropy = log_total - picked
        chance = jnp.exp(picked - log_total)
        grad = (LOSS_SCALE * mask * (jnp.exp(logits - log_total) - hot)).astype(BF)
        bundle[whole, 2 * inner :] = grad
        columns = jnp.where(lane == 0, mask, jnp.where(lane == 1, mask * chance, 0.0))
        kinds = lax.broadcasted_iota(jnp.int32, (LANES, length), 0) == types[pl.ds(s, 1), :]
        tallies = jnp.dot(
            jnp.where(kinds, 1.0, 0.0),
            columns,
            preferred_element_type=F32,
            precision=lax.Precision.HIGHEST,
        )
        stats[0:2, :] += jnp.transpose(tallies)[0:2]
        stats[2:3, :] += jnp.sum(grad.astype(F32), axis=0, keepdims=True)
        stats[3:4, :] += jnp.broadcast_to(
            jnp.sum(mask * entropy, axis=0, keepdims=True), (1, LANES)
        )
        head_grad[...] += dot_tn(block_out[whole, :], grad)
        work[:, 0:inner] = dot_nt(jnp.concatenate([grad, grad], axis=1), product[...])

        def behind(c):
            e = work[c, 0:inner] * gp3[c, :]
            n = n3[c, :]
            narrow_sums[0:8, :] += rows8(e * n)
            narrow_sums[8:16, :] += rows8(e)
            eg = e * g3
            mean_e = jnp.mean(eg, axis=1, keepdims=True)
            mean_en = jnp.mean(eg * n, axis=1, keepdims=True)
            low = (r3[c, 0:1] * (eg - mean_e - n * mean_en)).astype(BF)
            here = pl.ds(pl.multiple_of(s * length + c.start, c.size), c.size)
            conv_low[here, :] = low
            bundle[here, 0:inner] = low
            narrow_sums[16:24, :] += rows8(low.astype(F32))

        each_chunk(length, 32, behind)

    bundle[rows:, :] = jnp.zeros((16, bundle.shape[1]), BF)
    for j, term in enumerate(thirds(stats[...])):
        bundle[rows : rows + 8, j * LANES : (j + 1) * LANES] = term


def conv_grad_kernel(
    chips,
    hops,
    seqs,
    bundle_own,
    bundle_other,
    stats,
    *refs,
):
    count = 2 * hops + 1
    blocks = (refs[:count], refs[count : 2 * count])
    own, own_stats, own_out = refs[2 * count : 2 * count + 3]
    sends = refs[2 * count + 3 : 2 * count + 2 + chips]
    turned, turn, third_t = refs[2 * count + 2 + chips :]
    slabs, block, inner = own.shape
    rows = bundle_own.shape[0] - 16
    length = rows // seqs
    me = lax.axis_index("dp") // 2
    core = lax.axis_index("dp") & 1
    total_stats = stats[...] + sum_terms(bundle_other[rows:, :])
    own_stats[...] = total_stats
    tail = jnp.concatenate([stats_rows(total_stats, inner), jnp.zeros((8, inner), F32)], axis=0)
    for send in sends:
        send[send.shape[0] - 16 :, :] = tail.astype(BF)

    def chosen(ref, q):
        even = ref[2 * q * block : (2 * q + 1) * block, :]
        odd = ref[(2 * q + 1) * block : (2 * q + 2) * block, :]
        return jnp.where(core == 1, odd, even)

    for side in range(2):
        for s in range(seqs):
            for b, ref in enumerate(blocks[side]):
                turn[...] = jnp.transpose(ref[s])
                for q in range(chips):
                    turned[
                        side * seqs + s,
                        q * block : (q + 1) * block,
                        b * length : (b + 1) * length,
                    ] = chosen(turn, q)
        for s in range(seqs):
            columns = slice(s * length, (s + 1) * length)
            source = (bundle_own, bundle_other)[side]
            turn[...] = jnp.transpose(source[columns, inner : 2 * inner])
            for q in range(chips):
                third_t[side, q * block : (q + 1) * block, columns] = chosen(turn, q)

    def share(slab, value):
        parts = by_mask([value[q * block : (q + 1) * block] for q in range(chips)], me)
        own[slab] = parts[0]
        for m in range(1, chips):
            sends[m - 1][slab * block : (slab + 1) * block, :] = parts[m].astype(BF)

    for k in range(KERNEL_TAPS):
        at = hops * length + (k - CENTRE) * DILATION_RATE
        value = 0.0
        for side, low in enumerate((bundle_own, bundle_other)):
            for s in range(seqs):
                value = value + dot(
                    turned[side * seqs + s, :, at : at + length],
                    low[s * length : (s + 1) * length, 0:inner],
                )
        share(k, value)
    value = dot(third_t[0], bundle_own[0:rows, 2 * inner :])
    value += dot(third_t[1], bundle_other[0:rows, 2 * inner :])
    parts = by_mask([value[q * block : (q + 1) * block] for q in range(chips)], me)
    own_out[...] = parts[0]
    for m in range(1, chips):
        lines = beside(parts[m], inner // LANES)
        sends[m - 1][slabs * block : slabs * block + lines.shape[0], :] = lines.astype(BF)


def sum_terms(ref_value):
    return (
        ref_value[0:8, 0:LANES].astype(F32)
        + ref_value[0:8, LANES : 2 * LANES].astype(F32)
        + ref_value[0:8, 2 * LANES : 3 * LANES].astype(F32)
    )


def line_grad_b_kernel(count, size, part, own, stats, own_out, *refs):
    parts = refs[:count]
    keep, keep_stats, keep_out = refs[count : count + 3]
    sends = refs[count + 3 :]
    slabs, block, inner = own.shape
    me = lax.axis_index("seq")
    rows = parts[0].shape[0]
    sums = stats[...]
    out = own_out[...]
    for p in parts:
        sums += sum_terms(p[rows - 16 :, :])
        out += below(p[slabs * block : rows - 16, :].astype(F32))
    keep_stats[...] = sums
    pieces = [[] for _ in range(size)]
    for slab in range(slabs):
        value = own[slab]
        for p in parts:
            value += p[slab * block : (slab + 1) * block, :].astype(F32)
        cut = by_shift([value[z * part : (z + 1) * part] for z in range(size)], me)
        keep[slab] = cut[0]
        for k in range(1, size):
            pieces[k].append(cut[k])
    cut = by_shift([out[z * part : (z + 1) * part] for z in range(size)], me)
    tail_rows = keep_out.shape[0]
    keep_out[...] = padded(cut[0], tail_rows)
    terms = padded(stats_rows(sums, 3 * LANES), tail_rows)
    gap = sends[0].shape[0] - slabs * part - tail_rows
    for k in range(1, size):
        rest = inner - 4 * LANES
        tail = [terms, padded(cut[k], tail_rows), jnp.zeros((tail_rows, rest), F32)]
        lines = pieces[k] + ([jnp.zeros((gap, inner), F32)] if gap else [])
        lines.append(jnp.concatenate(tail, axis=1))
        sends[k - 1][...] = jnp.concatenate(lines, axis=0).astype(BF)


def end_b_kernel(count, keep, stats, keep_out, extras, *refs):
    parts = refs[:count]
    conv, out, sums = refs[count:]
    slabs, part, inner = keep.shape
    tail_rows = keep_out.shape[0]
    values = [p[...].astype(F32) for p in parts]
    total = stats[...]
    product = keep_out[...]
    for value in values:
        tail = value[value.shape[0] - tail_rows :]
        total += sum_terms(tail)
        product += tail[:, 3 * LANES : 4 * LANES]
    sums[...] = total
    value = 0.0
    for term in thirds(product):
        value = value + dot_nt(term, extras[...])
    out[...] = value[0:part]
    for slab in range(slabs):
        value = keep[slab]
        for v in values:
            value += v[slab * part : (slab + 1) * part]
        conv[slab] = value


def split_a_kernel(chips, keep, got_low, got_high, own, token, *sends):
    token[...] = jnp.zeros_like(token)
    half = chips // 2
    sums = [
        keep[q] + (got_low, got_high)[q // half][q % half].astype(F32) for q in range(chips)
    ]
    sums = by_mask(sums, lax.axis_index("dp") // 2)
    own[...] = sums[0]
    for m in range(1, chips):
        sends[m - 1][...] = sums[m].astype(BF)


def line_grad_a_kernel(count, size, part, own, *refs):
    parts = refs[:count]
    keep = refs[count]
    sends = refs[count + 1 :]
    me = lax.axis_index("seq")
    value = own[...]
    for p in parts:
        value += p[...].astype(F32)
    cut = [value[z * part : (z + 1) * part] for z in range(size)]
    for k in range(size):
        piece = cut[0]
        for z in range(1, size):
            piece = jnp.where(lax.rem(me + k, size) == z, cut[z], piece)
        if k == 0:
            keep[...] = piece
        else:
            sends[k - 1][...] = piece.astype(BF)


def end_a_kernel(count, vocab, keep, *refs):
    parts = refs[:count]
    w_in, head_t = refs[count : count + 2]
    vecs = refs[count + 2 : count + 2 + WIDE_VECTORS + NARROW_VECTORS]
    (tile,) = refs[count + 2 + WIDE_VECTORS + NARROW_VECTORS :]
    wide, inner = w_in.shape
    value = keep[...]
    for p in parts:
        value += p[...].astype(F32)
    w_in[...] = value[:, 0:inner]
    tile[...] = jnp.zeros_like(tile)
    tile[0:wide, :] = value[:, inner : inner + LANES]
    turned = jnp.transpose(tile[...])
    head_t[...] = turned[0:vocab, 0:wide]
    for j, v in enumerate(vecs):
        n = v.shape[-1]
        v[...] = turned[vocab + j : vocab + j + 1, 0:n].reshape(v.shape)


def back_kernel(
    chips,
    hops,
    seqs,
    vocab,
    wide,
    narrow,
    taps,
    n2,
    gp2,
    r2,
    n1,
    gp1,
    act,
    w_in,
    wide_v,
    narrow_v,
    narrow_sums,
    stats,
    extras,
    head_grad,
    *refs,
):
    blocks = refs[: 2 * hops + 1]
    keep, send_low, send_high, e1, low, ext, work, act_t, sums1, sums2 = refs[2 * hops + 1 :]
    half = chips // 2
    width, inner = w_in.shape
    rows = low.shape[0]
    length = rows // seqs
    g2 = narrow_v[1:2, :]
    for b, ref in enumerate(blocks):
        ext[:, b * length : (b + 1) * length, :] = ref[...]
    sums1[...] = jnp.zeros_like(sums1)
    sums2[...] = jnp.zeros_like(sums2)

    @pl.loop(0, seqs)
    def _(s):
        whole = pl.ds(pl.multiple_of(s * length, length), length)
        total = dot_nt(ext[s, pl.ds(hops * length + REACH, length), :], taps[0])
        for k in range(1, KERNEL_TAPS):
            at = hops * length - (k - CENTRE) * DILATION_RATE
            total += dot_nt(ext[s, pl.ds(at, length), :], taps[k])
        work[:, 0:inner] = total

        def second(c):
            here = pl.ds(pl.multiple_of(s * length + c.start, c.size), c.size)
            e = work[c, 0:inner].astype(BF).astype(F32) * gp2[here, :]
            n = n2[here, :]
            sums2[0:8, :] += rows8(e * n)
            sums2[8:16, :] += rows8(e)
            eg = e * g2
            mean_e = jnp.mean(eg, axis=1, keepdims=True)
            mean_en = jnp.mean(eg * n, axis=1, keepdims=True)
            value = (r2[here, 0:1] * (eg - mean_e - n * mean_en)).astype(BF)
            low[here, :] = value
            sums2[16:24, :] += rows8(value.astype(F32))

        each_chunk(length, 32, second)
        work[...] = dot_nt(low[whole, :], w_in[...])

        def first(c):
            here = pl.ds(pl.multiple_of(s * length + c.start, c.size), c.size)
            e = work[c, :] * gp1[here, :]
            e1[here, :] = e
            sums1[0:8, :] += rows8(e * n1[here, :])
            sums1[8:16, :] += rows8(e)

        each_chunk(length, 16, first)

    def folded(ref, j):
        return jnp.sum(ref[8 * j : 8 * j + 8, :], axis=0, keepdims=True)

    bias = 0.0
    for term in thirds(stats[...]):
        bias = bias + dot_nt(term, extras[...])
    wides = [folded(sums1, 0), folded(sums1, 1), bias[2:3, :]]
    narrows = [folded(sums2, 2), folded(sums2, 0), folded(sums2, 1)]
    narrows += [folded(narrow_sums, 2), folded(narrow_sums, 0), folded(narrow_sums, 1)]
    row = lax.broadcasted_iota(jnp.int32, (16, inner), 0)
    stacked = jnp.zeros((16, inner), F32)
    for j, v in enumerate(narrows):
        stacked = jnp.where(row == j, v, stacked)
    spread = spread_matrix(width, inner, wide, narrow)
    placed = 0.0
    for term in thirds(stacked):
        placed = placed + dot_nt(term, spread)
    row = lax.broadcasted_iota(jnp.int32, (LANES, width), 0)
    grid = jnp.zeros((LANES, width), F32)
    for j, v in enumerate(wides):
        grid = jnp.where(row == vocab + j, v, grid)
    for j in range(NARROW_VECTORS):
        grid = jnp.where(row == vocab + WIDE_VECTORS + j, placed[j : j + 1, :], grid)
    extra = jnp.transpose(grid) + head_grad[...]
    act_t[...] = jnp.transpose(act[...])
    core = lax.axis_index("dp") & 1
    block = keep.shape[1]
    for q in range(chips):
        for c in range(2):
            d = 2 * q + c
            lines = slice(d * block, (d + 1) * block)
            value = dot(act_t[lines, :], low[...])

            @pl.when(core == c)
            def _():
                keep[q, :, 0:inner] = value
                keep[q, :, inner : inner + LANES] = extra[lines]

            @pl.when(core != c)
            def _():
                send = (send_low, send_high)[q // half]
                send[q % half, :, 0:inner] = value.astype(BF)
                send[q % half, :, inner : inner + LANES] = extra[lines].astype(BF)


def input_kernel(e1, n1, r1, wide_v, bundle, extras, input_grad, token, work):
    token[...] = jnp.zeros_like(token)
    logit_grad = bundle[0 : e1.shape[0], bundle.shape[1] - LANES :]
    work[...] = dot_nt(logit_grad, extras[...])
    g1 = wide_v[0:1, :]

    def body(c):
        n = n1[c, :]
        eg = e1[c, :] * g1
        mean_e = jnp.mean(eg, axis=1, keepdims=True)
        mean_en = jnp.mean(eg * n, axis=1, keepdims=True)
        input_grad[c, :] = (work[c, :] + r1[c, 0:1] * (eg - mean_e - n * mean_en)).astype(BF)

    each_chunk(e1.shape[0], 16, body)


def swap(value, mask):
    count = lax.axis_size("dp")
    return lax.ppermute(value, "dp", [(i, i ^ mask) for i in range(count)])


def shifted(value, k):
    size = lax.axis_size("seq")
    return lax.ppermute(value, "seq", [(i, (i + k) % size) for i in range(size)])


def line_parts(block):
    return [block] + [shifted(block, k) for k in range(1, lax.axis_size("seq"))]


def chip_pieces(block):
    chips = lax.axis_size("dp") // 2
    own = [block] + [swap(block, 2 * m) for m in range(1, chips)]
    return own + [swap(piece, 1) for piece in own]


def halo(series):
    size = lax.axis_size("seq")
    hops = -(-REACH // series.shape[1])
    before = [
        lax.ppermute(series, "seq", [(i, i + h) for i in range(size - h)])
        for h in range(hops, 0, -1)
    ]
    after = [
        lax.ppermute(series, "seq", [(i + h, i) for i in range(size - h)])
        for h in range(1, hops + 1)
    ]
    return before + [series] + after


def shards(
    tokens,
    first_gain,
    first_bias,
    in_weight,
    in_bias,
    second_gain,
    second_bias,
    conv_weight,
    conv_bias,
    third_gain,
    third_bias,
    out_weight,
    out_bias,
    head_weight,
    head_bias,
    residue_types,
    mask_positions,
    targets,
):
    dp = lax.axis_size("dp")
    size = lax.axis_size("seq")
    chips = dp // 2
    seqs, length, width = tokens.shape
    wide, inner = in_weight.shape
    narrow = out_weight.shape[0]
    vocab = head_weight.shape[1]
    rows = seqs * length
    hops = -(-REACH // length)
    slabs = KERNEL_TAPS + width // inner
    flat = tokens.reshape(rows, width)

    ins = [
        in_weight,
        head_weight.T,
        first_gain,
        first_bias,
        out_bias,
        in_bias,
        second_gain,
        second_bias,
        conv_bias,
        third_gain,
        third_bias,
    ]
    (block_a,) = call(
        functools.partial(pack_a_kernel, vocab),
        ins,
        [sds((wide, inner + LANES), BF)],
        [pltpu.VMEM((LANES, LANES), F32), pltpu.SemaphoreType.DMA((len(ins),))]
        + [pltpu.VMEM(x.shape, BF) for x in ins],
        limit=56,
        name="pack_a",
        free=len(ins),
    )
    parts_a = line_parts(block_a)
    (line_a,) = call(
        functools.partial(line_a_kernel, size),
        parts_a,
        [sds((size * wide, inner + LANES), BF)],
        name="line_a",
    )
    ins = [jnp.transpose(conv_weight, (1, 0, 2)), out_weight]
    (block_b,) = call(
        pack_b_kernel,
        ins,
        [sds((slabs * narrow, inner), BF)],
        [pltpu.SemaphoreType.DMA((2,))] + [pltpu.VMEM(x.shape, BF) for x in ins],
        limit=8,
        name="pack_b",
        free=2,
        after=[block_a],
    )
    own_a = [line_a] + [swap(line_a, 2 * m) for m in range(1, chips)]
    parts_b = line_parts(block_b)
    n1, r1, spread = call(
        functools.partial(first_kernel, wide, narrow),
        [flat],
        [sds((rows, width), F32), sds((rows, LANES), F32), sds((width, inner), BF)],
        us=6,
        limit=8,
        name="first",
        after=[block_b],
    )
    *own_a, _ = lax.optimization_barrier((*own_a, r1))
    pieces_a = list(own_a) + [swap(piece, 1) for piece in own_a]
    (line_b,) = call(
        functools.partial(line_b_kernel, size),
        parts_b,
        [sds((slabs, size * narrow, inner), BF)],
        name="line_b",
        after=[r1],
    )
    if chips == 4:
        half = slabs // 2
        by_x, by_y = swap(line_b, 2), swap(line_b, 4)
        own_b = [line_b, by_x, by_y, swap(by_x[:half], 4), swap(by_y[half:], 2)]
        layout = [(0, 0), (2, 0), (4, 0), (6, 0), (6, half)]
    else:
        own_b = [line_b] + [swap(line_b, 2 * m) for m in range(1, chips)]
        layout = [(2 * m, 0) for m in range(chips)]
    layout = layout + [(mask + 1, first) for mask, first in layout]
    w_in, extras, wide_v, narrow_v, act, gp1, n2, gp2, r2, conv_in = call(
        functools.partial(second_kernel, chips, vocab),
        [n1, spread] + pieces_a,
        [
            sds((width, inner), BF),
            sds((width, LANES), BF),
            sds((8, width), F32),
            sds((8, inner), F32),
            sds((rows, width), BF),
            sds((rows, width), F32),
            sds((rows, inner), F32),
            sds((rows, inner), F32),
            sds((rows, LANES), F32),
            sds((rows, inner), BF),
        ],
        [pltpu.VMEM((rows, inner), F32)],
        us=9,
        limit=16,
        name="second",
        after=[line_b],
    )
    blocks = halo(conv_in.reshape(seqs, length, inner))
    other_line = swap(line_b, 1)
    early = 3 if chips == 4 else 1
    near = [swap(piece, 1) for piece in own_b[1:early]]
    *late, _, _ = lax.optimization_barrier((*own_b[early:], blocks[0], blocks[-1]))
    pieces_b = own_b[:early] + list(late) + [other_line] + near + [swap(piece, 1) for piece in late]
    other_blocks = [swap(piece, 1) for piece in blocks]
    (
        taps,
        block_out,
        bundle,
        head_grad,
        conv_low,
        narrow_sums,
        stats,
    ) = call(
        functools.partial(middle_kernel, layout, hops, seqs, vocab),
        [
            wide_v,
            narrow_v,
            extras,
            jnp.pad(head_bias.astype(F32), (0, LANES - vocab)).reshape(1, LANES),
            residue_types,
            mask_positions,
            targets,
            flat,
        ]
        + blocks
        + pieces_b,
        [
            sds((slabs, inner, inner), BF),
            sds((rows, width), BF),
            sds((rows + 16, 2 * inner + LANES), BF),
            sds((width, LANES), F32),
            sds((rows, inner), BF),
            sds((24, inner), F32),
            sds((8, LANES), F32),
        ],
        [
            pltpu.VMEM((seqs, (2 * hops + 1) * length, inner), BF),
            pltpu.VMEM((length, inner), F32),
            pltpu.VMEM((length, inner), F32),
            pltpu.VMEM((length, LANES), F32),
            pltpu.VMEM((length, width), F32),
            pltpu.VMEM((inner, 2 * LANES), BF),
        ],
        us=17,
        limit=16,
        name="middle",
    )
    grad_blocks = halo(conv_low.reshape(seqs, length, inner))
    other_bundle = swap(bundle, 1)
    message = KERNEL_TAPS * size * narrow + size * narrow // (inner // LANES) + 16
    split_b = call(
        functools.partial(conv_grad_kernel, chips, hops, seqs),
        [bundle, other_bundle, stats]
        + blocks
        + other_blocks,
        [
            sds((KERNEL_TAPS, size * narrow, inner), F32),
            sds((8, LANES), F32),
            sds((size * narrow, LANES), F32),
        ]
        + [sds((message, inner), BF)] * (chips - 1),
        [
            pltpu.VMEM((2 * seqs, inner // 2, (2 * hops + 1) * length), BF),
            pltpu.VMEM((inner, length), BF),
            pltpu.VMEM((2, inner // 2, rows), BF),
        ],
        us=7,
        limit=16,
        name="conv_grad",
    )
    from_chips_b = [swap(piece, 2 * m) for m, piece in zip(range(1, chips), split_b[3:])]
    keep_a, send_low, send_high, e1 = call(
        functools.partial(back_kernel, chips, hops, seqs, vocab, wide, narrow),
        [taps, n2, gp2, r2, n1, gp1, act, w_in, wide_v, narrow_v]
        + [narrow_sums, stats, extras, head_grad]
        + grad_blocks,
        [
            sds((chips, size * wide, inner + LANES), F32),
            sds((chips // 2, size * wide, inner + LANES), BF),
            sds((chips // 2, size * wide, inner + LANES), BF),
            sds((rows, width), F32),
        ],
        [
            pltpu.VMEM((rows, inner), BF),
            pltpu.VMEM((seqs, (2 * hops + 1) * length, inner), BF),
            pltpu.VMEM((length, width), F32),
            pltpu.VMEM((width, rows), BF),
            pltpu.VMEM((16, width), F32),
            pltpu.VMEM((24, inner), F32),
        ],
        us=US_S,
        limit=20,
        name="back",
        after=[split_b[1]],
    )
    got_low, got_high = swap(send_low, 1), swap(send_high, 1)
    split = call(
        functools.partial(split_a_kernel, chips),
        [keep_a, got_low, got_high],
        [sds((size * wide, inner + LANES), F32), sds((8, LANES), F32)]
        + [sds((size * wide, inner + LANES), BF)] * (chips - 1),
        us=US_S,
        name="split_a",
    )
    tail = -(-max(narrow, 8) // 8) * 8
    line_b2 = call(
        functools.partial(line_grad_b_kernel, chips - 1, size, narrow),
        list(split_b[:3]) + from_chips_b,
        [sds((KERNEL_TAPS, narrow, inner), F32), sds((8, LANES), F32), sds((tail, LANES), F32)]
        + [sds((-(-KERNEL_TAPS * narrow // 8) * 8 + tail, inner), BF)] * (size - 1),
        name="line_grad_b",
        after=[split[1]],
    )
    *a_sends, _ = lax.optimization_barrier((*split[2:], line_b2[1]))
    from_chips = [swap(piece, 2 * m) for m, piece in zip(range(1, chips), a_sends)]

    input_grad, input_token = call(
        input_kernel,
        [e1, n1, r1, wide_v, bundle, extras],
        [sds((rows, width), BF), sds((8, LANES), F32)],
        [pltpu.VMEM((rows, width), F32)],
        us=3,
        name="input",
        after=[line_b2[1]],
    )
    from_line_b = [shifted(piece, k) for k, piece in zip(range(1, size), line_b2[3:])]
    line = call(
        functools.partial(line_grad_a_kernel, chips - 1, size, wide),
        [split[0]] + from_chips,
        [sds((wide, inner + LANES), F32)] + [sds((wide, inner + LANES), BF)] * (size - 1),
        name="line_grad_a",
        after=[input_token],
    )
    conv_share, out_share, sums = call(
        functools.partial(end_b_kernel, size - 1),
        [line_b2[0], line_b2[1], line_b2[2], extras] + from_line_b,
        [sds((KERNEL_TAPS, narrow, inner), F32), sds((narrow, width), F32), sds((8, LANES), F32)],
        name="end_b",
        after=[line[0]],
    )
    from_line = [shifted(piece, k) for k, piece in zip(range(1, size), line[1:])]
    ended = call(
        functools.partial(end_a_kernel, size - 1, vocab),
        [line[0]] + from_line,
        [sds((wide, inner), F32), sds((vocab, wide), F32)]
        + [sds((wide,), F32)] * WIDE_VECTORS
        + [sds((narrow,), F32)] * NARROW_VECTORS,
        [pltpu.VMEM((LANES, LANES), F32)],
        name="end_a",
    )
    in_share, head_share, g1, b1, bo, bi, g2, b2, bc, g3, b3 = ended
    masked_total = seqs * dp * mask_positions.shape[1]
    return (
        block_out.reshape(seqs, length, width),
        input_grad.reshape(seqs, length, width),
        g1,
        b1,
        in_share,
        bi,
        g2,
        b2,
        jnp.transpose(conv_share, (1, 0, 2)),
        bc,
        g3,
        b3,
        out_share,
        bo,
        head_share.T,
        sums[2, :vocab],
        sums[0, :vocab].astype(jnp.int32),
        sums[1, :vocab],
        sums[3, 0] / masked_total,
    )


def solution(mesh):
    both = P(("dp", "seq"))
    matrix = P(("dp", "seq"), None)
    cube = P(("dp", "seq"), None, None)
    rows = P("dp", "seq", None)
    return jax.shard_map(
        shards,
        mesh=mesh,
        in_specs=(rows, both, both, matrix, both, both, both, cube, both, both, both, matrix)
        + (both, matrix, P(), P("dp", "seq"), P("dp", None), P("dp", None)),
        out_specs=(rows, rows, both, both, matrix, both, both, both, cube, both, both, both)
        + (matrix, both, matrix, P(), P(), P(), P()),
        check_vma=False,
    )
```

```python
import functools

import jax
import jax.numpy as jnp
from jax import lax
from jax.experimental import pallas as pl
from jax.experimental.pallas import tpu as pltpu
from jax.sharding import PartitionSpec as P

KERNEL_TAPS = 5
CENTRE = KERNEL_TAPS // 2
DILATION_RATE = 128
NORM_EPSILON = 1e-05
LOSS_SCALE = 16.0
REACH = CENTRE * DILATION_RATE
BF = jnp.bfloat16
F32 = jnp.float32
LANES = 128
US_S = 0.1
WIDE_VECTORS = 3
NARROW_VECTORS = 6
MIB = 1024 * 1024
HALF_ROOT = 0.7071067811865476
INV_ROOT_TWO_PI = 0.3989422804014327


def gauss(u):
    t = pl.reciprocal(1.0 + (0.3275911 * HALF_ROOT) * jnp.abs(u), approx=False)
    e = jnp.exp2(u * u * -0.7213475204444817)
    poly = t * (
        0.127414796
        + t * (-0.142248368 + t * (0.7107068705 + t * (-0.7265760135 + t * 0.5307027145)))
    )
    tail = poly * e
    return jnp.where(u < 0, tail, 1.0 - tail), e * INV_ROOT_TWO_PI


def standardize(v):
    average = jnp.mean(v, axis=-1, keepdims=True)
    centred = v - average
    spread = jnp.mean(centred * centred, axis=-1, keepdims=True)
    r = lax.rsqrt(spread + NORM_EPSILON)
    return centred * r, r


def dot(a, b):
    return jnp.dot(a, b, preferred_element_type=F32)


def dot_nt(a, b):
    return lax.dot_general(a, b, (((1,), (1,)), ((), ())), preferred_element_type=F32)


def dot_tn(a, b):
    return lax.dot_general(a, b, (((0,), (0,)), ((), ())), preferred_element_type=F32)


def rows8(x):
    return jnp.sum(x.reshape(x.shape[0] // 8, 8, x.shape[1]), axis=0)


def each_chunk(count, step, body):
    @pl.loop(0, count // step, unroll=8 if count // step >= 8 else 4)
    def _(i):
        body(pl.ds(pl.multiple_of(i * step, step), step))


def thirds(x):
    high = x.astype(BF)
    rest = x - high.astype(F32)
    mid = rest.astype(BF)
    low = (rest - mid.astype(F32)).astype(BF)
    return high, mid, low


def by_mask(values, me):
    bit = 1
    while bit < len(values):
        here = (me & bit) != 0
        values = [jnp.where(here, values[m ^ bit], values[m]) for m in range(len(values))]
        bit *= 2
    return values


def by_shift(values, me):
    bit = 1
    n = len(values)
    while bit < n:
        here = (me & bit) != 0
        values = [jnp.where(here, values[(k + bit) % n], values[k]) for k in range(n)]
        bit *= 2
    return values


def of_core(values):
    core = lax.axis_index("dp") & 1
    return [
        jnp.where(core == 1, odd, even) for even, odd in zip(values[0::2], values[1::2])
    ]


def beside(value, count):
    r = value.shape[0] // count
    return jnp.concatenate([value[g * r : (g + 1) * r] for g in range(count)], axis=1)


def below(value):
    count = value.shape[1] // LANES
    return jnp.concatenate([value[:, g * LANES : (g + 1) * LANES] for g in range(count)], axis=0)


def stats_rows(total, inner):
    terms = [term.astype(F32) for term in thirds(total)]
    rest = inner - 3 * LANES
    return jnp.concatenate(terms + ([jnp.zeros((8, rest), F32)] if rest else []), axis=1)


def padded(value, rows):
    gap = rows - value.shape[0]
    if gap == 0:
        return value
    return jnp.concatenate([value, jnp.zeros((gap, value.shape[1]), F32)], axis=0)


def vmem(n):
    return [pl.BlockSpec(memory_space=pltpu.VMEM)] * n


def call(kernel, ins, outs, scratch=(), us=1, limit=12, name=None, after=(), free=0):
    count = len(ins)
    skipped = len(after)

    def body(*refs):
        kernel(*refs[:count], *refs[count + skipped :])

    return pl.pallas_call(
        body,
        out_shape=list(outs),
        in_specs=[pl.BlockSpec(memory_space=pltpu.HBM)] * free
        + vmem(count - free)
        + [pl.BlockSpec(memory_space=pl.ANY)] * skipped,
        out_specs=vmem(len(outs)),
        scratch_shapes=list(scratch),
        compiler_params=pltpu.CompilerParams(vmem_limit_bytes=limit * MIB),
        cost_estimate=pl.CostEstimate(flops=int(us * 1e9), bytes_accessed=1000, transcendentals=0),
        name=name,
    )(*ins, *after)


def sds(shape, dtype):
    return jax.ShapeDtypeStruct(shape, dtype)


def fetch(sources, targets, sems):
    copies = [
        pltpu.make_async_copy(source, target, sems.at[j])
        for j, (source, target) in enumerate(zip(sources, targets))
    ]
    for copy in copies:
        copy.start()
    for copy in copies:
        copy.wait()


def pack_a_kernel(vocab, *refs):
    count = 2 + WIDE_VECTORS + NARROW_VECTORS
    group, tile, sems = refs[count : count + 3]
    held = refs[count + 3 :]
    fetch(refs[:count], held, sems)
    w_in, head_t, vecs = held[0], held[1], held[2:]
    wide, inner = w_in.shape
    tile[...] = jnp.zeros_like(tile)
    tile[0:vocab, 0:wide] = head_t[...].astype(F32)
    for j, v in enumerate(vecs):
        n = v.shape[-1]
        tile[vocab + j : vocab + j + 1, 0:n] = v[...].astype(F32).reshape(1, n)
    group[:, 0:inner] = w_in[...]
    group[:, inner : inner + LANES] = jnp.transpose(tile[...])[0:wide].astype(BF)


def pack_b_kernel(conv, w_out, group, sems, conv_held, out_held):
    fetch((conv, w_out), (conv_held, out_held), sems)
    inner = group.shape[1]
    rows = [conv_held[k].astype(F32) for k in range(KERNEL_TAPS)]
    for h in range(w_out.shape[1] // inner):
        rows.append(out_held[:, h * inner : (h + 1) * inner].astype(F32))
    group[...] = jnp.concatenate(rows, axis=0).astype(BF)


def line_a_kernel(n, *refs):
    parts, out = refs[:n], refs[n]
    ordered = by_shift([parts[-k % n][...].astype(F32) for k in range(n)], -lax.axis_index("seq") % n)
    out[...] = jnp.concatenate(ordered, axis=0).astype(BF)


def line_b_kernel(n, *refs):
    parts, out = refs[:n], refs[n]
    slabs = out.shape[0]
    values = [parts[-k % n][...].astype(F32) for k in range(n)]
    ordered = by_shift(values, -lax.axis_index("seq") % n)
    part = values[0].shape[0] // slabs
    for slab in range(slabs):
        out[slab] = jnp.concatenate(
            [value[slab * part : (slab + 1) * part] for value in ordered], axis=0
        ).astype(BF)


def first_kernel(wide, narrow, tokens, n1, r1, spread):
    spread[...] = spread_matrix(tokens.shape[1], spread.shape[1], wide, narrow)

    def body(c):
        n, r = standardize(tokens[c, :].astype(F32))
        n1[c, :] = n
        r1[c, :] = jnp.broadcast_to(r, (r.shape[0], LANES))

    each_chunk(tokens.shape[0], 16, body)


def spread_matrix(width, inner, wide, narrow):
    row = lax.broadcasted_iota(jnp.int32, (width, 1), 0)
    device = row // wide
    r = row - device * wide
    at = jnp.where(r < narrow, device * narrow + r, -1)
    return (lax.broadcasted_iota(jnp.int32, (width, inner), 1) == at).astype(F32).astype(BF)


def second_kernel(chips, vocab, n1, spread, *refs):
    pieces = refs[: 2 * chips]
    (w_in, extras, wide_v, narrow_v, act, gp1, n2, gp2, r2, conv_in, proj) = refs[2 * chips :]
    width, inner = w_in.shape
    rows = n1.shape[0]
    me = lax.axis_index("dp")
    block = pieces[0].shape[0]
    for c in range(2):
        for m in range(chips):
            at = pl.multiple_of((me ^ (2 * m + c)) * block, block)
            w_in[pl.ds(at, block), :] = pieces[c * chips + m][:, 0:inner]
            extras[pl.ds(at, block), :] = pieces[c * chips + m][:, inner : inner + LANES]
    turned = jnp.transpose(extras[...].astype(F32))
    wide_v[...] = jnp.zeros_like(wide_v)
    wide_v[0:WIDE_VECTORS, :] = turned[vocab : vocab + WIDE_VECTORS]
    first = vocab + WIDE_VECTORS
    narrow_v[0:NARROW_VECTORS, :] = dot(
        turned.astype(BF), spread[...]
    )[first : first + NARROW_VECTORS]
    g1, b1 = wide_v[0:1, :], wide_v[1:2, :]
    bias, g2, b2 = narrow_v[0:1, :], narrow_v[1:2, :], narrow_v[2:3, :]

    def body(c):
        u = n1[c, :] * g1 + b1
        cdf, pdf = gauss(u)
        act[c, :] = (u * cdf).astype(BF)
        gp1[c, :] = cdf + u * pdf

    half = rows // 2
    for at in range(0, rows, half):
        for j in range(at, at + half, 16):
            body(pl.ds(j, 16))
        proj[at : at + half, :] = dot(act[at : at + half, :], w_in[...])

    def later(c):
        n, r = standardize(proj[c, :] + bias)
        u = n * g2 + b2
        cdf, pdf = gauss(u)
        conv_in[c, :] = (u * cdf).astype(BF)
        gp2[c, :] = cdf + u * pdf
        n2[c, :] = n
        r2[c, :] = jnp.broadcast_to(r, (r.shape[0], LANES))

    for j in range(0, rows, 32):
        later(pl.ds(j, 32))


def middle_kernel(
    layout,
    hops,
    seqs,
    vocab,
    wide_v,
    narrow_v,
    extras,
    head_bias,
    types,
    positions,
    targets,
    tokens,
    *refs,
):
    blocks = refs[: 2 * hops + 1]
    pieces = refs[2 * hops + 1 : 2 * hops + 1 + len(layout)]
    (
        taps,
        block_out,
        bundle,
        head_grad,
        conv_low,
        narrow_sums,
        stats,
        ext,
        n3,
        gp3,
        r3,
        work,
        product,
    ) = refs[2 * hops + 1 + len(layout) :]
    inner = taps.shape[1]
    width = tokens.shape[1]
    rows = tokens.shape[0]
    length = rows // seqs
    me = lax.axis_index("dp")
    block = pieces[0].shape[1]
    for (mask, first), piece in zip(layout, pieces):
        at = pl.multiple_of((me ^ mask) * block, block)
        for slab in range(piece.shape[0]):
            taps[first + slab, pl.ds(at, block), :] = piece[slab]
    for b, ref in enumerate(blocks):
        ext[:, b * length : (b + 1) * length, :] = ref[...]
    bias, g3, b3 = narrow_v[3:4, :], narrow_v[4:5, :], narrow_v[5:6, :]
    bias_out = wide_v[2:3, :]
    narrow_sums[...] = jnp.zeros_like(narrow_sums)
    value = dot(taps[KERNEL_TAPS], extras[0:inner, :])
    for h in range(1, width // inner):
        value += dot(taps[KERNEL_TAPS + h], extras[h * inner : (h + 1) * inner, :])
    product[:, 0:LANES] = value.astype(BF)
    product[:, LANES : 2 * LANES] = (value - value.astype(BF).astype(F32)).astype(BF)
    stats[...] = jnp.zeros_like(stats)
    head_grad[...] = jnp.zeros_like(head_grad)
    seat = lax.axis_index("seq")

    @pl.loop(0, seqs, unroll=True)
    def _(s):
        whole = pl.ds(pl.multiple_of(s * length, length), length)
        total = dot(ext[s, pl.ds(hops * length - REACH, length), :], taps[0])
        for k in range(1, KERNEL_TAPS):
            at = hops * length + (k - CENTRE) * DILATION_RATE
            total += dot(ext[s, pl.ds(at, length), :], taps[k])
        work[:, 0:inner] = total

        def ahead(c):
            low = (work[c, 0:inner] + bias).astype(BF).astype(F32)
            n, r = standardize(low)
            u = n * g3 + b3
            cdf, pdf = gauss(u)
            here = pl.ds(pl.multiple_of(s * length + c.start, c.size), c.size)
            bundle[here, inner : 2 * inner] = (u * cdf).astype(BF)
            gp3[c, :] = cdf + u * pdf
            n3[c, :] = n
            r3[c, :] = jnp.broadcast_to(r, (r.shape[0], LANES))

        each_chunk(length, 32, ahead)
        for h in range(width // inner):
            work[:, h * inner : (h + 1) * inner] = dot(
                bundle[whole, inner : 2 * inner], taps[KERNEL_TAPS + h]
            )

        def add(c):
            here = pl.ds(pl.multiple_of(s * length + c.start, c.size), c.size)
            block_out[here, :] = (tokens[here, :].astype(F32) + work[c, :] + bias_out).astype(BF)

        each_chunk(length, 32, add)
        lane = lax.broadcasted_iota(jnp.int32, (length, LANES), 1)
        logits = dot(block_out[whole, :], extras[...]) + head_bias[...]
        logits = jnp.where(lane < vocab, logits, -1e30)
        highest = jnp.max(logits, axis=1, keepdims=True)
        raised = jnp.exp(logits - highest)
        log_total = highest + jnp.log(jnp.sum(raised, axis=1, keepdims=True))
        place = lax.broadcasted_iota(jnp.int32, (length, positions.shape[1]), 0) + seat * length
        matches = positions[pl.ds(s, 1), :] == place
        mask = jnp.sum(jnp.where(matches, 1.0, 0.0), axis=1, keepdims=True)
        goal = jnp.sum(
            jnp.where(matches, targets[pl.ds(s, 1), :].astype(F32), 0.0), axis=1, keepdims=True
        )
        hot = jnp.where(lane == goal.astype(jnp.int32), 1.0, 0.0)
        picked = jnp.sum(logits * hot, axis=1, keepdims=True)
        entropy = log_total - picked
        chance = jnp.exp(picked - log_total)
        grad = (LOSS_SCALE * mask * (jnp.exp(logits - log_total) - hot)).astype(BF)
        bundle[whole, 2 * inner :] = grad
        columns = jnp.where(lane == 0, mask, jnp.where(lane == 1, mask * chance, 0.0))
        kinds = lax.broadcasted_iota(jnp.int32, (LANES, length), 0) == types[pl.ds(s, 1), :]
        tallies = jnp.dot(
            jnp.where(kinds, 1.0, 0.0),
            columns,
            preferred_element_type=F32,
            precision=lax.Precision.HIGHEST,
        )
        stats[0:2, :] += jnp.transpose(tallies)[0:2]
        stats[2:3, :] += jnp.sum(grad.astype(F32), axis=0, keepdims=True)
        stats[3:4, :] += jnp.broadcast_to(
            jnp.sum(mask * entropy, axis=0, keepdims=True), (1, LANES)
        )
        head_grad[...] += dot_tn(block_out[whole, :], grad)
        work[:, 0:inner] = dot_nt(jnp.concatenate([grad, grad], axis=1), product[...])

        def behind(c):
            e = work[c, 0:inner] * gp3[c, :]
            n = n3[c, :]
            narrow_sums[0:8, :] += rows8(e * n)
            narrow_sums[8:16, :] += rows8(e)
            eg = e * g3
            mean_e = jnp.mean(eg, axis=1, keepdims=True)
            mean_en = jnp.mean(eg * n, axis=1, keepdims=True)
            low = (r3[c, 0:1] * (eg - mean_e - n * mean_en)).astype(BF)
            here = pl.ds(pl.multiple_of(s * length + c.start, c.size), c.size)
            conv_low[here, :] = low
            bundle[here, 0:inner] = low
            narrow_sums[16:24, :] += rows8(low.astype(F32))

        each_chunk(length, 32, behind)

    bundle[rows:, :] = jnp.zeros((16, bundle.shape[1]), BF)
    for j, term in enumerate(thirds(stats[...])):
        bundle[rows : rows + 8, j * LANES : (j + 1) * LANES] = term


def conv_grad_kernel(
    chips,
    hops,
    seqs,
    bundle_own,
    bundle_other,
    stats,
    *refs,
):
    count = 2 * hops + 1
    blocks = (refs[:count], refs[count : 2 * count])
    own, own_stats, own_out = refs[2 * count : 2 * count + 3]
    sends = refs[2 * count + 3 : 2 * count + 2 + chips]
    turned, turn, third_t = refs[2 * count + 2 + chips :]
    slabs, block, inner = own.shape
    rows = bundle_own.shape[0] - 16
    length = rows // seqs
    me = lax.axis_index("dp") // 2
    core = lax.axis_index("dp") & 1
    total_stats = stats[...] + sum_terms(bundle_other[rows:, :])
    own_stats[...] = total_stats
    tail = jnp.concatenate([stats_rows(total_stats, inner), jnp.zeros((8, inner), F32)], axis=0)
    for send in sends:
        send[send.shape[0] - 16 :, :] = tail.astype(BF)

    def chosen(ref, q):
        even = ref[2 * q * block : (2 * q + 1) * block, :]
        odd = ref[(2 * q + 1) * block : (2 * q + 2) * block, :]
        return jnp.where(core == 1, odd, even)

    for side in range(2):
        for s in range(seqs):
            for b, ref in enumerate(blocks[side]):
                turn[...] = jnp.transpose(ref[s])
                for q in range(chips):
                    turned[
                        side * seqs + s,
                        q * block : (q + 1) * block,
                        b * length : (b + 1) * length,
                    ] = chosen(turn, q)
        for s in range(seqs):
            columns = slice(s * length, (s + 1) * length)
            source = (bundle_own, bundle_other)[side]
            turn[...] = jnp.transpose(source[columns, inner : 2 * inner])
            for q in range(chips):
                third_t[side, q * block : (q + 1) * block, columns] = chosen(turn, q)

    def share(slab, value):
        parts = by_mask([value[q * block : (q + 1) * block] for q in range(chips)], me)
        own[slab] = parts[0]
        for m in range(1, chips):
            sends[m - 1][slab * block : (slab + 1) * block, :] = parts[m].astype(BF)

    for k in range(KERNEL_TAPS):
        at = hops * length + (k - CENTRE) * DILATION_RATE
        value = 0.0
        for side, low in enumerate((bundle_own, bundle_other)):
            for s in range(seqs):
                value = value + dot(
                    turned[side * seqs + s, :, at : at + length],
                    low[s * length : (s + 1) * length, 0:inner],
                )
        share(k, value)
    value = dot(third_t[0], bundle_own[0:rows, 2 * inner :])
    value += dot(third_t[1], bundle_other[0:rows, 2 * inner :])
    parts = by_mask([value[q * block : (q + 1) * block] for q in range(chips)], me)
    own_out[...] = parts[0]
    for m in range(1, chips):
        lines = beside(parts[m], inner // LANES)
        sends[m - 1][slabs * block : slabs * block + lines.shape[0], :] = lines.astype(BF)


def sum_terms(ref_value):
    return (
        ref_value[0:8, 0:LANES].astype(F32)
        + ref_value[0:8, LANES : 2 * LANES].astype(F32)
        + ref_value[0:8, 2 * LANES : 3 * LANES].astype(F32)
    )


def line_grad_b_kernel(count, size, part, own, stats, own_out, *refs):
    parts = refs[:count]
    keep, keep_stats, keep_out = refs[count : count + 3]
    sends = refs[count + 3 :]
    slabs, block, inner = own.shape
    me = lax.axis_index("seq")
    rows = parts[0].shape[0]
    sums = stats[...]
    out = own_out[...]
    for p in parts:
        sums += sum_terms(p[rows - 16 :, :])
        out += below(p[slabs * block : rows - 16, :].astype(F32))
    keep_stats[...] = sums
    pieces = [[] for _ in range(size)]
    for slab in range(slabs):
        value = own[slab]
        for p in parts:
            value += p[slab * block : (slab + 1) * block, :].astype(F32)
        cut = by_shift([value[z * part : (z + 1) * part] for z in range(size)], me)
        keep[slab] = cut[0]
        for k in range(1, size):
            pieces[k].append(cut[k])
    cut = by_shift([out[z * part : (z + 1) * part] for z in range(size)], me)
    tail_rows = keep_out.shape[0]
    keep_out[...] = padded(cut[0], tail_rows)
    terms = padded(stats_rows(sums, 3 * LANES), tail_rows)
    gap = sends[0].shape[0] - slabs * part - tail_rows
    for k in range(1, size):
        rest = inner - 4 * LANES
        tail = [terms, padded(cut[k], tail_rows), jnp.zeros((tail_rows, rest), F32)]
        lines = pieces[k] + ([jnp.zeros((gap, inner), F32)] if gap else [])
        lines.append(jnp.concatenate(tail, axis=1))
        sends[k - 1][...] = jnp.concatenate(lines, axis=0).astype(BF)


def end_b_kernel(count, keep, stats, keep_out, extras, *refs):
    parts = refs[:count]
    conv, out, sums = refs[count:]
    slabs, part, inner = keep.shape
    tail_rows = keep_out.shape[0]
    values = [p[...].astype(F32) for p in parts]
    total = stats[...]
    product = keep_out[...]
    for value in values:
        tail = value[value.shape[0] - tail_rows :]
        total += sum_terms(tail)
        product += tail[:, 3 * LANES : 4 * LANES]
    sums[...] = total
    value = 0.0
    for term in thirds(product):
        value = value + dot_nt(term, extras[...])
    out[...] = value[0:part]
    for slab in range(slabs):
        value = keep[slab]
        for v in values:
            value += v[slab * part : (slab + 1) * part]
        conv[slab] = value


def split_a_kernel(chips, keep, got_low, got_high, own, token, *sends):
    token[...] = jnp.zeros_like(token)
    half = chips // 2
    sums = [
        keep[q] + (got_low, got_high)[q // half][q % half].astype(F32) for q in range(chips)
    ]
    sums = by_mask(sums, lax.axis_index("dp") // 2)
    own[...] = sums[0]
    for m in range(1, chips):
        sends[m - 1][...] = sums[m].astype(BF)


def line_grad_a_kernel(count, size, part, own, *refs):
    parts = refs[:count]
    keep = refs[count]
    sends = refs[count + 1 :]
    me = lax.axis_index("seq")
    value = own[...]
    for p in parts:
        value += p[...].astype(F32)
    cut = [value[z * part : (z + 1) * part] for z in range(size)]
    for k in range(size):
        piece = cut[0]
        for z in range(1, size):
            piece = jnp.where(lax.rem(me + k, size) == z, cut[z], piece)
        if k == 0:
            keep[...] = piece
        else:
            sends[k - 1][...] = piece.astype(BF)


def end_a_kernel(count, vocab, keep, *refs):
    parts = refs[:count]
    w_in, head_t = refs[count : count + 2]
    vecs = refs[count + 2 : count + 2 + WIDE_VECTORS + NARROW_VECTORS]
    (tile,) = refs[count + 2 + WIDE_VECTORS + NARROW_VECTORS :]
    wide, inner = w_in.shape
    value = keep[...]
    for p in parts:
        value += p[...].astype(F32)
    w_in[...] = value[:, 0:inner]
    tile[...] = jnp.zeros_like(tile)
    tile[0:wide, :] = value[:, inner : inner + LANES]
    turned = jnp.transpose(tile[...])
    head_t[...] = turned[0:vocab, 0:wide]
    for j, v in enumerate(vecs):
        n = v.shape[-1]
        v[...] = turned[vocab + j : vocab + j + 1, 0:n].reshape(v.shape)


def back_kernel(
    chips,
    hops,
    seqs,
    vocab,
    wide,
    narrow,
    taps,
    n2,
    gp2,
    r2,
    n1,
    gp1,
    act,
    w_in,
    wide_v,
    narrow_v,
    narrow_sums,
    stats,
    extras,
    head_grad,
    *refs,
):
    blocks = refs[: 2 * hops + 1]
    keep, send_low, send_high, e1, low, ext, work, act_t, sums1, sums2 = refs[2 * hops + 1 :]
    half = chips // 2
    width, inner = w_in.shape
    rows = low.shape[0]
    length = rows // seqs
    g2 = narrow_v[1:2, :]
    for b, ref in enumerate(blocks):
        ext[:, b * length : (b + 1) * length, :] = ref[...]
    sums1[...] = jnp.zeros_like(sums1)
    sums2[...] = jnp.zeros_like(sums2)

    @pl.loop(0, seqs)
    def _(s):
        whole = pl.ds(pl.multiple_of(s * length, length), length)
        total = dot_nt(ext[s, pl.ds(hops * length + REACH, length), :], taps[0])
        for k in range(1, KERNEL_TAPS):
            at = hops * length - (k - CENTRE) * DILATION_RATE
            total += dot_nt(ext[s, pl.ds(at, length), :], taps[k])
        work[:, 0:inner] = total

        def second(c):
            here = pl.ds(pl.multiple_of(s * length + c.start, c.size), c.size)
            e = work[c, 0:inner].astype(BF).astype(F32) * gp2[here, :]
            n = n2[here, :]
            sums2[0:8, :] += rows8(e * n)
            sums2[8:16, :] += rows8(e)
            eg = e * g2
            mean_e = jnp.mean(eg, axis=1, keepdims=True)
            mean_en = jnp.mean(eg * n, axis=1, keepdims=True)
            value = (r2[here, 0:1] * (eg - mean_e - n * mean_en)).astype(BF)
            low[here, :] = value
            sums2[16:24, :] += rows8(value.astype(F32))

        each_chunk(length, 32, second)
        work[...] = dot_nt(low[whole, :], w_in[...])

        def first(c):
            here = pl.ds(pl.multiple_of(s * length + c.start, c.size), c.size)
            e = work[c, :] * gp1[here, :]
            e1[here, :] = e
            sums1[0:8, :] += rows8(e * n1[here, :])
            sums1[8:16, :] += rows8(e)

        each_chunk(length, 16, first)

    def folded(ref, j):
        return jnp.sum(ref[8 * j : 8 * j + 8, :], axis=0, keepdims=True)

    bias = 0.0
    for term in thirds(stats[...]):
        bias = bias + dot_nt(term, extras[...])
    wides = [folded(sums1, 0), folded(sums1, 1), bias[2:3, :]]
    narrows = [folded(sums2, 2), folded(sums2, 0), folded(sums2, 1)]
    narrows += [folded(narrow_sums, 2), folded(narrow_sums, 0), folded(narrow_sums, 1)]
    row = lax.broadcasted_iota(jnp.int32, (16, inner), 0)
    stacked = jnp.zeros((16, inner), F32)
    for j, v in enumerate(narrows):
        stacked = jnp.where(row == j, v, stacked)
    spread = spread_matrix(width, inner, wide, narrow)
    placed = 0.0
    for term in thirds(stacked):
        placed = placed + dot_nt(term, spread)
    row = lax.broadcasted_iota(jnp.int32, (LANES, width), 0)
    grid = jnp.zeros((LANES, width), F32)
    for j, v in enumerate(wides):
        grid = jnp.where(row == vocab + j, v, grid)
    for j in range(NARROW_VECTORS):
        grid = jnp.where(row == vocab + WIDE_VECTORS + j, placed[j : j + 1, :], grid)
    extra = jnp.transpose(grid) + head_grad[...]
    act_t[...] = jnp.transpose(act[...])
    core = lax.axis_index("dp") & 1
    block = keep.shape[1]
    for q in range(chips):
        even = slice(2 * q * block, (2 * q + 1) * block)
        odd = slice((2 * q + 1) * block, (2 * q + 2) * block)
        send = (send_low, send_high)[q // half]
        first, second = dot(act_t[even, :], low[...]), dot(act_t[odd, :], low[...])
        keep[q, :, 0:inner] = jnp.where(core == 1, second, first)
        send[q % half, :, 0:inner] = jnp.where(core == 1, first, second).astype(BF)
        keep[q, :, inner : inner + LANES] = jnp.where(core == 1, extra[odd], extra[even])
        send[q % half, :, inner : inner + LANES] = jnp.where(core == 1, extra[even], extra[odd]).astype(BF)


def input_kernel(e1, n1, r1, wide_v, bundle, extras, input_grad, token, work):
    token[...] = jnp.zeros_like(token)
    logit_grad = bundle[0 : e1.shape[0], bundle.shape[1] - LANES :]
    work[...] = dot_nt(logit_grad, extras[...])
    g1 = wide_v[0:1, :]

    def body(c):
        n = n1[c, :]
        eg = e1[c, :] * g1
        mean_e = jnp.mean(eg, axis=1, keepdims=True)
        mean_en = jnp.mean(eg * n, axis=1, keepdims=True)
        input_grad[c, :] = (work[c, :] + r1[c, 0:1] * (eg - mean_e - n * mean_en)).astype(BF)

    each_chunk(e1.shape[0], 16, body)


def swap(value, mask):
    count = lax.axis_size("dp")
    return lax.ppermute(value, "dp", [(i, i ^ mask) for i in range(count)])


def shifted(value, k):
    size = lax.axis_size("seq")
    return lax.ppermute(value, "seq", [(i, (i + k) % size) for i in range(size)])


def line_parts(block):
    return [block] + [shifted(block, k) for k in range(1, lax.axis_size("seq"))]


def chip_pieces(block):
    chips = lax.axis_size("dp") // 2
    own = [block] + [swap(block, 2 * m) for m in range(1, chips)]
    return own + [swap(piece, 1) for piece in own]


def halo(series):
    size = lax.axis_size("seq")
    hops = -(-REACH // series.shape[1])
    before = [
        lax.ppermute(series, "seq", [(i, i + h) for i in range(size - h)])
        for h in range(hops, 0, -1)
    ]
    after = [
        lax.ppermute(series, "seq", [(i + h, i) for i in range(size - h)])
        for h in range(1, hops + 1)
    ]
    return before + [series] + after


def shards(
    tokens,
    first_gain,
    first_bias,
    in_weight,
    in_bias,
    second_gain,
    second_bias,
    conv_weight,
    conv_bias,
    third_gain,
    third_bias,
    out_weight,
    out_bias,
    head_weight,
    head_bias,
    residue_types,
    mask_positions,
    targets,
):
    dp = lax.axis_size("dp")
    size = lax.axis_size("seq")
    chips = dp // 2
    seqs, length, width = tokens.shape
    wide, inner = in_weight.shape
    narrow = out_weight.shape[0]
    vocab = head_weight.shape[1]
    rows = seqs * length
    hops = -(-REACH // length)
    slabs = KERNEL_TAPS + width // inner
    flat = tokens.reshape(rows, width)

    ins = [
        in_weight,
        head_weight.T,
        first_gain,
        first_bias,
        out_bias,
        in_bias,
        second_gain,
        second_bias,
        conv_bias,
        third_gain,
        third_bias,
    ]
    (block_a,) = call(
        functools.partial(pack_a_kernel, vocab),
        ins,
        [sds((wide, inner + LANES), BF)],
        [pltpu.VMEM((LANES, LANES), F32), pltpu.SemaphoreType.DMA((len(ins),))]
        + [pltpu.VMEM(x.shape, BF) for x in ins],
        limit=56,
        name="pack_a",
        free=len(ins),
    )
    parts_a = line_parts(block_a)
    (line_a,) = call(
        functools.partial(line_a_kernel, size),
        parts_a,
        [sds((size * wide, inner + LANES), BF)],
        name="line_a",
    )
    ins = [jnp.transpose(conv_weight, (1, 0, 2)), out_weight]
    (block_b,) = call(
        pack_b_kernel,
        ins,
        [sds((slabs * narrow, inner), BF)],
        [pltpu.SemaphoreType.DMA((2,))] + [pltpu.VMEM(x.shape, BF) for x in ins],
        limit=8,
        name="pack_b",
        free=2,
        after=[block_a],
    )
    own_a = [line_a] + [swap(line_a, 2 * m) for m in range(1, chips)]
    parts_b = line_parts(block_b)
    n1, r1, spread = call(
        functools.partial(first_kernel, wide, narrow),
        [flat],
        [sds((rows, width), F32), sds((rows, LANES), F32), sds((width, inner), BF)],
        us=6,
        limit=8,
        name="first",
        after=[block_b],
    )
    *own_a, _ = lax.optimization_barrier((*own_a, r1))
    pieces_a = list(own_a) + [swap(piece, 1) for piece in own_a]
    (line_b,) = call(
        functools.partial(line_b_kernel, size),
        parts_b,
        [sds((slabs, size * narrow, inner), BF)],
        name="line_b",
        after=[r1],
    )
    if chips == 4:
        half = slabs // 2
        by_x, by_y = swap(line_b, 2), swap(line_b, 4)
        own_b = [line_b, by_x, by_y, swap(by_x[:half], 4), swap(by_y[half:], 2)]
        layout = [(0, 0), (2, 0), (4, 0), (6, 0), (6, half)]
    else:
        own_b = [line_b] + [swap(line_b, 2 * m) for m in range(1, chips)]
        layout = [(2 * m, 0) for m in range(chips)]
    layout = layout + [(mask + 1, first) for mask, first in layout]
    w_in, extras, wide_v, narrow_v, act, gp1, n2, gp2, r2, conv_in = call(
        functools.partial(second_kernel, chips, vocab),
        [n1, spread] + pieces_a,
        [
            sds((width, inner), BF),
            sds((width, LANES), BF),
            sds((8, width), F32),
            sds((8, inner), F32),
            sds((rows, width), BF),
            sds((rows, width), F32),
            sds((rows, inner), F32),
            sds((rows, inner), F32),
            sds((rows, LANES), F32),
            sds((rows, inner), BF),
        ],
        [pltpu.VMEM((rows, inner), F32)],
        us=9,
        limit=16,
        name="second",
        after=[line_b],
    )
    blocks = halo(conv_in.reshape(seqs, length, inner))
    other_line = swap(line_b, 1)
    early = 3 if chips == 4 else 1
    near = [swap(piece, 1) for piece in own_b[1:early]]
    *late, _, _ = lax.optimization_barrier((*own_b[early:], blocks[0], blocks[-1]))
    pieces_b = own_b[:early] + list(late) + [other_line] + near + [swap(piece, 1) for piece in late]
    other_blocks = [swap(piece, 1) for piece in blocks]
    (
        taps,
        block_out,
        bundle,
        head_grad,
        conv_low,
        narrow_sums,
        stats,
    ) = call(
        functools.partial(middle_kernel, layout, hops, seqs, vocab),
        [
            wide_v,
            narrow_v,
            extras,
            jnp.pad(head_bias.astype(F32), (0, LANES - vocab)).reshape(1, LANES),
            residue_types,
            mask_positions,
            targets,
            flat,
        ]
        + blocks
        + pieces_b,
        [
            sds((slabs, inner, inner), BF),
            sds((rows, width), BF),
            sds((rows + 16, 2 * inner + LANES), BF),
            sds((width, LANES), F32),
            sds((rows, inner), BF),
            sds((24, inner), F32),
            sds((8, LANES), F32),
        ],
        [
            pltpu.VMEM((seqs, (2 * hops + 1) * length, inner), BF),
            pltpu.VMEM((length, inner), F32),
            pltpu.VMEM((length, inner), F32),
            pltpu.VMEM((length, LANES), F32),
            pltpu.VMEM((length, width), F32),
            pltpu.VMEM((inner, 2 * LANES), BF),
        ],
        us=17,
        limit=16,
        name="middle",
    )
    grad_blocks = halo(conv_low.reshape(seqs, length, inner))
    other_bundle = swap(bundle, 1)
    message = KERNEL_TAPS * size * narrow + size * narrow // (inner // LANES) + 16
    split_b = call(
        functools.partial(conv_grad_kernel, chips, hops, seqs),
        [bundle, other_bundle, stats]
        + blocks
        + other_blocks,
        [
            sds((KERNEL_TAPS, size * narrow, inner), F32),
            sds((8, LANES), F32),
            sds((size * narrow, LANES), F32),
        ]
        + [sds((message, inner), BF)] * (chips - 1),
        [
            pltpu.VMEM((2 * seqs, inner // 2, (2 * hops + 1) * length), BF),
            pltpu.VMEM((inner, length), BF),
            pltpu.VMEM((2, inner // 2, rows), BF),
        ],
        us=7,
        limit=16,
        name="conv_grad",
    )
    from_chips_b = [swap(piece, 2 * m) for m, piece in zip(range(1, chips), split_b[3:])]
    keep_a, send_low, send_high, e1 = call(
        functools.partial(back_kernel, chips, hops, seqs, vocab, wide, narrow),
        [taps, n2, gp2, r2, n1, gp1, act, w_in, wide_v, narrow_v]
        + [narrow_sums, stats, extras, head_grad]
        + grad_blocks,
        [
            sds((chips, size * wide, inner + LANES), F32),
            sds((chips // 2, size * wide, inner + LANES), BF),
            sds((chips // 2, size * wide, inner + LANES), BF),
            sds((rows, width), F32),
        ],
        [
            pltpu.VMEM((rows, inner), BF),
            pltpu.VMEM((seqs, (2 * hops + 1) * length, inner), BF),
            pltpu.VMEM((length, width), F32),
            pltpu.VMEM((width, rows), BF),
            pltpu.VMEM((16, width), F32),
            pltpu.VMEM((24, inner), F32),
        ],
        us=US_S,
        limit=20,
        name="back",
        after=[split_b[1]],
    )
    got_low, got_high = swap(send_low, 1), swap(send_high, 1)
    split = call(
        functools.partial(split_a_kernel, chips),
        [keep_a, got_low, got_high],
        [sds((size * wide, inner + LANES), F32), sds((8, LANES), F32)]
        + [sds((size * wide, inner + LANES), BF)] * (chips - 1),
        us=US_S,
        name="split_a",
    )
    tail = -(-max(narrow, 8) // 8) * 8
    line_b2 = call(
        functools.partial(line_grad_b_kernel, chips - 1, size, narrow),
        list(split_b[:3]) + from_chips_b,
        [sds((KERNEL_TAPS, narrow, inner), F32), sds((8, LANES), F32), sds((tail, LANES), F32)]
        + [sds((-(-KERNEL_TAPS * narrow // 8) * 8 + tail, inner), BF)] * (size - 1),
        name="line_grad_b",
        after=[split[1]],
    )
    *a_sends, _ = lax.optimization_barrier((*split[2:], line_b2[1]))
    from_chips = [swap(piece, 2 * m) for m, piece in zip(range(1, chips), a_sends)]

    input_grad, input_token = call(
        input_kernel,
        [e1, n1, r1, wide_v, bundle, extras],
        [sds((rows, width), BF), sds((8, LANES), F32)],
        [pltpu.VMEM((rows, width), F32)],
        us=3,
        name="input",
        after=[line_b2[1]],
    )
    from_line_b = [shifted(piece, k) for k, piece in zip(range(1, size), line_b2[3:])]
    line = call(
        functools.partial(line_grad_a_kernel, chips - 1, size, wide),
        [split[0]] + from_chips,
        [sds((wide, inner + LANES), F32)] + [sds((wide, inner + LANES), BF)] * (size - 1),
        name="line_grad_a",
        after=[input_token],
    )
    conv_share, out_share, sums = call(
        functools.partial(end_b_kernel, size - 1),
        [line_b2[0], line_b2[1], line_b2[2], extras] + from_line_b,
        [sds((KERNEL_TAPS, narrow, inner), F32), sds((narrow, width), F32), sds((8, LANES), F32)],
        name="end_b",
        after=[line[0]],
    )
    from_line = [shifted(piece, k) for k, piece in zip(range(1, size), line[1:])]
    ended = call(
        functools.partial(end_a_kernel, size - 1, vocab),
        [line[0]] + from_line,
        [sds((wide, inner), F32), sds((vocab, wide), F32)]
        + [sds((wide,), F32)] * WIDE_VECTORS
        + [sds((narrow,), F32)] * NARROW_VECTORS,
        [pltpu.VMEM((LANES, LANES), F32)],
        name="end_a",
    )
    in_share, head_share, g1, b1, bo, bi, g2, b2, bc, g3, b3 = ended
    masked_total = seqs * dp * mask_positions.shape[1]
    return (
        block_out.reshape(seqs, length, width),
        input_grad.reshape(seqs, length, width),
        g1,
        b1,
        in_share,
        bi,
        g2,
        b2,
        jnp.transpose(conv_share, (1, 0, 2)),
        bc,
        g3,
        b3,
        out_share,
        bo,
        head_share.T,
        sums[2, :vocab],
        sums[0, :vocab].astype(jnp.int32),
        sums[1, :vocab],
        sums[3, 0] / masked_total,
    )


def solution(mesh):
    both = P(("dp", "seq"))
    matrix = P(("dp", "seq"), None)
    cube = P(("dp", "seq"), None, None)
    rows = P("dp", "seq", None)
    return jax.shard_map(
        shards,
        mesh=mesh,
        in_specs=(rows, both, both, matrix, both, both, both, cube, both, both, both, matrix)
        + (both, matrix, P(), P("dp", "seq"), P("dp", None), P("dp", None)),
        out_specs=(rows, rows, both, both, matrix, both, both, both, cube, both, both, both)
        + (matrix, both, matrix, P(), P(), P(), P()),
        check_vma=False,
    )
```
